32 devices in a mesh: dp: 4 (over y, x), expert: 8 (over z, core).
Axes of the slice: x: 2, y: 2, z: 4, core: 2. Of those that a mesh axis runs over, the one named last changes fastest.
Arguments:
- block_input: bfloat16 [4096, 512], P(('dp', 'expert')), may hold values from -6 to 6
- cotangent: bfloat16 [4096, 512], P(('dp', 'expert')), may hold values from -6 to 6
- lengths: int32 [4, 6], P('dp'), may hold values from 1 to 512, 896 in all within a row
- run_loops: int32 [4096], P('dp'), may hold values from 1 to 3
- attn_routes: int32 [3, 4096, 4], P(None, 'dp'), may hold values from 0 to 7, all different within a row; in each aligned block of 1024 rows (0 to 1023, 1024 to 2047, ..., all dimensions but the last counted through in order) at most 640 rows name the same one
- ffn_routes: int32 [3, 4096, 2], P(None, 'dp'), may hold values from 0 to 7, all different within a row; in each aligned block of 1024 rows (0 to 1023, 1024 to 2047, ..., all dimensions but the last counted through in order) at most 320 rows name the same one
- shared_vectors: float32 [5, 512], replicated, as said below
- shared_moment: float32 [5, 512], replicated
- shared_second: float32 [5, 512], replicated, as said below
- key_value: float32 [512, 128], replicated, may hold values from -0.25 to 0.25
- kv_moment: float32 [512, 128], replicated, may hold values from -112 to 112
- kv_second: float32 [512, 128], replicated, may hold values from 358.4 to 1433.6
- router_weights: float32 [512, 16], replicated, may hold values from -0.15625 to 0.15625
- router_moment: float32 [512, 16], replicated, may hold values from -16 to 16
- router_second: float32 [512, 16], replicated, may hold values from 96.0512 to 387.072
- attn_weights: float32 [8, 512, 128], P('expert', 'dp')
- attn_moment: float32 [8, 512, 128], P('expert', 'dp')
- attn_second: float32 [8, 512, 128], P('expert', 'dp'), as said below
- up_weights: float32 [8, 512, 2048], P('expert', 'dp'), may hold values from -0.25 to 0.25
- up_moment: float32 [8, 512, 2048], P('expert', 'dp'), may hold values from -4 to 4
- up_second: float32 [8, 512, 2048], P('expert', 'dp'), may hold values from 0.25088 to 1.00352
- down_weights: float32 [8, 512, 2048], P('expert', 'dp'), may hold values from -0.125 to 0.125
- down_moment: float32 [8, 512, 2048], P('expert', 'dp'), may hold values from -8 to 8
- down_second: float32 [8, 512, 2048], P('expert', 'dp'), may hold values from 1.792 to 7.168
Outputs:
- output: float32 [4096, 512], P(('dp', 'expert'))
- input_grad: float32 [4096, 512], P(('dp', 'expert'))
- shared_new: float32 [5, 512], replicated
- shared_moment_new: float32 [5, 512], replicated
- shared_second_new: float32 [5, 512], replicated
- kv_new: float32 [512, 128], replicated
- kv_moment_new: float32 [512, 128], replicated
- kv_second_new: float32 [512, 128], replicated
- router_new: float32 [512, 16], replicated
- router_moment_new: float32 [512, 16], replicated
- router_second_new: float32 [512, 16], replicated
- attn_new: float32 [8, 512, 128], P('expert', 'dp')
- attn_moment_new: float32 [8, 512, 128], P('expert', 'dp')
- attn_second_new: float32 [8, 512, 128], P('expert', 'dp')
- attn_copy: bfloat16 [8, 512, 128], P('expert', 'dp')
- up_new: float32 [8, 512, 2048], P('expert', 'dp')
- up_moment_new: float32 [8, 512, 2048], P('expert', 'dp')
- up_second_new: float32 [8, 512, 2048], P('expert', 'dp')
- up_copy: bfloat16 [8, 512, 2048], P('expert', 'dp')
- down_new: float32 [8, 512, 2048], P('expert', 'dp')
- down_moment_new: float32 [8, 512, 2048], P('expert', 'dp')
- down_second_new: float32 [8, 512, 2048], P('expert', 'dp')
- down_copy: bfloat16 [8, 512, 2048], P('expert', 'dp')
The draws below stay inside these ranges and needn't reach their ends.
Inputs may be any that keep to these rules, and one draw needn't show every extreme that they name: The lengths of one data device sum to 896; the remaining slots are padding. `attn_routes`: each row names 4 different experts; in each loop at most 640 rows of one data device name one expert, and that many do in some blocks. `ffn_routes`: each row names 2 different experts; in each loop at most 320 rows of one data device name one expert, and that many do in some blocks. `shared_vectors`: gains positive, biases and the halting weight of both signs. `shared_second`: Positive. `attn_second`: Positive.
All inputs are finite; a program needn't handle non-finite values.
Results may differ from the reference program's by a relative error of at most 0.025.
The reference program's roundings to bfloat16 on the way count: a program that leaves them out, or rounds other values in their place, can miss the bound.
Values may be sent and summed in bfloat16 or wider, within the bound.
A program may use at most 192 MiB of HBM per device.

```python
import math
import jax
import jax.numpy as jnp
import numpy as np
from jax import lax

D = 512
HD = 64
FF = 2048
KATT = 4
KFF = 2
LOOPS = 3
STEP = 10
SEQS = 6
TOK_DEV = 1024
NATT = 8
NFF = 8
TOKENS = 4096
MAXLEN = 512
FILLED = 896
CAP_ATT = 640
CAP_FF = 320
N_DP = 4


def shared_scales():
    rows_all = 7 * TOKENS // 4
    gain_scale = math.sqrt(rows_all)
    halt_scale = 3.0 * math.sqrt(2 * TOKENS)
    return jnp.array([gain_scale, gain_scale, gain_scale, gain_scale, halt_scale], dtype=jnp.float32)[:, None]


def attn_scales():
    rows_all = 7 * TOKENS * KATT // (4 * NATT)
    query_scale = 0.8 * math.sqrt(rows_all)
    output_scale = 0.075 * math.sqrt(rows_all)
    return jnp.concatenate([jnp.full((HD,), query_scale, jnp.float32), jnp.full((HD,), output_scale, jnp.float32)])


def draw_shared_vectors(key, part):
    keys = jax.random.split(jax.random.fold_in(key, 11), 3)
    gains = 1.0 + 0.2 * jax.random.truncated_normal(keys[0], -4.0, 4.0, (2, D), jnp.float32)
    biases = 0.6 * jax.random.truncated_normal(keys[1], -4.0, 4.0, (2, D), jnp.float32)
    halting = 3.0 * jax.random.truncated_normal(keys[2], -4.0, 4.0, (1, D), jnp.float32) / math.sqrt(D)
    return jnp.concatenate([gains[0:1], biases[0:1], gains[1:2], biases[1:2], halting], axis=0)


def draw_shared_moment(key, part):
    noise = jax.random.truncated_normal(jax.random.fold_in(key, 12), -4.0, 4.0, (5, D), jnp.float32)
    return 0.11 * noise * shared_scales()


def draw_shared_second(key, part):
    factor = jnp.exp(jax.random.uniform(jax.random.fold_in(key, 13), (5, D), jnp.float32, 0.0, math.log(4.0)))
    scales = shared_scales()
    return 0.0125 * factor * scales * scales


def draw_attn_weights(key, part):
    noise = jax.random.truncated_normal(jax.random.fold_in(key, 21), -4.0, 4.0, (NATT, D, 2 * HD), jnp.float32)
    column_scale = jnp.concatenate([jnp.full((HD,), 2.0 / math.sqrt(D), jnp.float32), jnp.full((HD,), 4.0 / math.sqrt(HD), jnp.float32)])
    return noise * column_scale


def draw_attn_moment(key, part):
    noise = jax.random.truncated_normal(jax.random.fold_in(key, 22), -4.0, 4.0, (NATT, D, 2 * HD), jnp.float32)
    return 0.11 * noise * attn_scales()


def draw_attn_second(key, part):
    factor = jnp.exp(jax.random.uniform(jax.random.fold_in(key, 23), (NATT, D, 2 * HD), jnp.float32, 0.0, math.log(4.0)))
    scales = attn_scales()
    return 0.0047 * factor * scales * scales


def plant(values, own_key, smallest, largest):
    index_at = [jax.random.randint(jax.random.fold_in(own_key, axis), (), 0, length) for axis, length in enumerate(values.shape)]
    widest = values.shape.index(max(values.shape))
    next_to = index_at[:widest] + [(index_at[widest] + 1) % values.shape[widest]] + index_at[widest + 1:]
    return values.at[tuple(index_at)].set(smallest).at[tuple(next_to)].set(largest)


def levels(rng, extent, pieces, least, largest):
    def one(dim, parts):
        steps = jax.random.uniform(jax.random.fold_in(jax.random.fold_in(rng, 6), dim), (parts,), jnp.float32, least / len(pieces), largest / len(pieces))
        return jnp.repeat(jnp.exp(steps), extent[dim] // parts).reshape((-1,) + (1,) * (len(extent) - dim - 1))

    loudness = one(*pieces[0])
    for cut in pieces[1:]:
        loudness = loudness * one(*cut)
    return loudness


def length_profile(count, total, bound, lean):
    weights = [(1 << 20) // math.isqrt(grade ** lean) + 1 for grade in range(2, count + 1)]
    spare, counts = total - bound - (count - 1), [1] * (count - 1)
    while spare > 0:
        candidates = [i for i in range(count - 1) if counts[i] < bound]
        pool, left = sum([weights[i] for i in candidates]), spare
        for i in candidates:
            extra = min(bound - counts[i], max(1, left * weights[i] // pool), spare)
            counts[i] = counts[i] + extra
            spare = spare - extra
    return np.array([bound] + counts)


def uneven(own_key, count, total, reach, lean):
    if count == 2:
        one = jax.random.randint(own_key, (), max(1, total - reach), min(reach, total - 1) + 1)
        return jnp.stack([one, total - one])
    sizes = jnp.asarray(length_profile(count, total, reach, lean), jnp.int32)
    pairs = (count - 1) // 2
    giver, sink = sizes[1:1 + 2 * pairs:2], sizes[2:2 + 2 * pairs:2]
    margin = jnp.minimum(giver - 1, reach - sink)
    shifted = jax.random.randint(jax.random.fold_in(own_key, 1), (pairs,), 0, 1 << 20) % (margin + 1)
    sizes = sizes.at[1:1 + 2 * pairs:2].set(giver - shifted).at[2:2 + 2 * pairs:2].set(sink + shifted)
    return sizes[jax.random.permutation(jax.random.fold_in(own_key, 2), count)]


def shared_out(key, own, number, rows, amount, top, bound, lean):
    sequence = jax.random.permutation(key, amount)
    crowded, common = shares(amount, rows * top, bound, lean, True), shares(amount, rows * top, bound, lean, False)
    places = jnp.arange(amount)

    def named(sizes, rotation):
        used = int((sizes > 0).sum())
        fixed = max(1, used // 4)
        passed = fixed + (places - fixed + rotation * (used - fixed)) % max(1, amount - fixed)
        return jnp.zeros((amount,), jnp.int32).at[sequence[jnp.where(places < fixed, places, passed)]].set(jnp.asarray(sizes, jnp.int32))

    sizes = jnp.where(number % 4 == 0, named(crowded, number // 4), named(common, number - number // 4 - 1))
    mixed = jax.random.permutation(jax.random.fold_in(own, 3), amount)
    giver, taker = mixed[0:amount // 2 * 2:2], mixed[1:amount // 2 * 2:2]
    room = jnp.minimum(sizes[giver] - 1, bound - sizes[taker]) // 2
    room = jnp.where((giver == sequence[0]) | (taker == sequence[0]) | (sizes[taker] == 0), 0, jnp.maximum(room, 0))
    passed = jax.random.randint(jax.random.fold_in(own, 4), (amount // 2,), 0, 1 << 20) % (room + 1)
    sizes = sizes.at[giver].add(-passed).at[taker].add(passed)
    items = jnp.searchsorted(jnp.cumsum(sizes), jnp.arange(rows * top), side="right").astype(jnp.int32)
    grid = items.reshape(top, rows).T
    grid = grid[jax.random.permutation(jax.random.fold_in(own, 1), rows)]
    rotation = jax.random.randint(jax.random.fold_in(own, 2), (rows, 1), 0, top)
    return jnp.take_along_axis(grid, (jnp.arange(top)[None, :] + rotation) % top, axis=1)


def shares(amount, total, bound, skew, full):
    loads = [(1 << 20) // math.isqrt(rank ** skew) + 1 for rank in range(1, amount + 1)]
    largest = bound if full else min(bound, max(-(-total // amount), total * loads[0] // sum(loads)))
    least = 1 if total - largest >= amount - 1 else 0
    holding, rest = [largest] + [least] * (amount - 1), total - largest - least * (amount - 1)
    while rest > 0:
        free = [i for i in range(1, amount) if holding[i] < largest] or [i for i in range(1, amount) if holding[i] < bound]
        whole, remaining = sum([loads[i] for i in free]), rest
        for i in free:
            more = min(bound - holding[i], max(1, remaining * loads[i] // whole), rest)
            holding[i] = holding[i] + more
            rest = rest - more
    return np.array(holding)


def normal_values(stream_key, extent, scale, reach, cuts=(), kind=jnp.bfloat16):
    entries = jax.random.normal(stream_key, extent, jnp.float32) * scale
    if len(cuts) > 0:
        entries = levels(stream_key, extent, cuts, -0.22, 0.18) * entries
    return jnp.clip(entries, min=-reach, max=reach).astype(kind)


def setup_inputs(seed: int = 0) -> dict:
    streams_of = jax.random.split(jax.random.key(seed), 25)
    block_input = normal_values(streams_of[0], (TOKENS, D), 1.0, 6.0, ((0, 32),))
    cotangent = normal_values(streams_of[1], (TOKENS, D), 1.0, 6.0, ((0, 32),))
    lengths = jax.vmap(lambda own: uneven(own, SEQS, FILLED, MAXLEN, 2))(jax.random.split(streams_of[2], N_DP)).reshape((N_DP, SEQS)).astype(jnp.int32)
    run_loops = plant(jax.random.randint(streams_of[3], (TOKENS,), 1, LOOPS + 1), jax.random.fold_in(streams_of[3], 1), 1, LOOPS).astype(jnp.int32)
    attn_routes_keys = jax.random.split(jax.random.fold_in(streams_of[4], 1), LOOPS * TOKENS // TOK_DEV)
    attn_routes_turns = jax.random.permutation(jax.random.fold_in(streams_of[4], 3), LOOPS * TOKENS // TOK_DEV)
    attn_routes = jax.vmap(lambda own, number: shared_out(jax.random.fold_in(streams_of[4], 2), own, number, TOK_DEV, NATT, KATT, CAP_ATT, 2))(attn_routes_keys, attn_routes_turns).reshape((LOOPS, TOKENS, KATT))
    ffn_routes_keys = jax.random.split(jax.random.fold_in(streams_of[5], 1), LOOPS * TOKENS // TOK_DEV)
    ffn_routes_turns = jax.random.permutation(jax.random.fold_in(streams_of[5], 3), LOOPS * TOKENS // TOK_DEV)
    ffn_routes = jax.vmap(lambda own, number: shared_out(jax.random.fold_in(streams_of[5], 2), own, number, TOK_DEV, NFF, KFF, CAP_FF, 2))(ffn_routes_keys, ffn_routes_turns).reshape((LOOPS, TOKENS, KFF))
    shared_vectors = draw_shared_vectors(jax.random.fold_in(streams_of[24], 71), 0)
    shared_moment = draw_shared_moment(jax.random.fold_in(streams_of[24], 71), 0)
    shared_second = draw_shared_second(jax.random.fold_in(streams_of[24], 71), 0)
    key_value = normal_values(streams_of[9], (D, 2 * HD), D ** -0.5, 0.25, (), jnp.float32)
    kv_moment = normal_values(streams_of[10], (D, 2 * HD), (0.22 * (7 * TOKENS // 4) ** 0.5), 112.0, (), jnp.float32)
    kv_second = jnp.clip(jnp.exp(jax.random.uniform(streams_of[11], (D, 2 * HD), jnp.float32, math.log(358.4), math.log(1433.6))), 358.4, 1433.6)
    router_weights = normal_values(streams_of[12], (D, NATT + NFF), (3 * D) ** -0.5, 0.15625, (), jnp.float32)
    router_moment = normal_values(streams_of[13], (D, NATT + NFF), (0.033 * (7 * TOKENS // 4) ** 0.5), 16.0, (), jnp.float32)
    router_second = jnp.clip(jnp.exp(jax.random.uniform(streams_of[14], (D, NATT + NFF), jnp.float32, math.log(96.0512), math.log(387.072))), 96.0512, 387.072)
    attn_weights = draw_attn_weights(jax.random.fold_in(streams_of[24], 71), 0)
    attn_moment = draw_attn_moment(jax.random.fold_in(streams_of[24], 71), 0)
    attn_second = draw_attn_second(jax.random.fold_in(streams_of[24], 71), 0)
    up_weights = normal_values(streams_of[18], (NFF, D, FF), D ** -0.5, 0.25, ((0, 8), (1, 4)), jnp.float32)
    up_moment = normal_values(streams_of[19], (NFF, D, FF), (0.0165 * (7 * TOKENS * KFF // (4 * NFF)) ** 0.5), 4.0, ((0, 8), (1, 4)), jnp.float32)
    up_second = jnp.clip(jnp.exp(math.log(1.00352) - 1.3862944 * jax.random.uniform(streams_of[20], (NFF, D, FF), jnp.float32) ** levels(streams_of[20], (NFF, D, FF), ((0, 8), (1, 4)), -0.2, 0.2)), 0.25088, 1.00352)
    down_weights = normal_values(streams_of[21], (NFF, D, FF), FF ** -0.5, 0.125, ((0, 8), (1, 4)), jnp.float32)
    down_moment = normal_values(streams_of[22], (NFF, D, FF), (0.036 * (7 * TOKENS * KFF // (4 * NFF)) ** 0.5), 8.0, ((0, 8), (1, 4)), jnp.float32)
    down_second = jnp.clip(jnp.exp(math.log(7.168) - 1.3862944 * jax.random.uniform(streams_of[23], (NFF, D, FF), jnp.float32) ** levels(streams_of[23], (NFF, D, FF), ((0, 8), (1, 4)), -0.2, 0.2)), 1.792, 7.168)
    return dict(block_input=block_input, cotangent=cotangent, lengths=lengths, run_loops=run_loops, attn_routes=attn_routes, ffn_routes=ffn_routes, shared_vectors=shared_vectors, shared_moment=shared_moment, shared_second=shared_second, key_value=key_value, kv_moment=kv_moment, kv_second=kv_second, router_weights=router_weights, router_moment=router_moment, router_second=router_second, attn_weights=attn_weights, attn_moment=attn_moment, attn_second=attn_second, up_weights=up_weights, up_moment=up_moment, up_second=up_second, down_weights=down_weights, down_moment=down_moment, down_second=down_second)


ln_eps = 1e-05
beta_one = 0.9
beta_two = 0.999
adam_eps = 1e-08
decay_rate = 0.01
masked_score = -1e+30

@jax.custom_vjp
def low(v):
    return lax.optimization_barrier(v.astype(jnp.bfloat16)).astype(jnp.float32)

@jax.custom_vjp
def low_back(v):
    return v

def low_keep(v):
    return (low(v), None)

def low_pass(kept, grad):
    return (grad,)

def back_keep(v):
    return (v, None)

def back_low(kept, grad):
    return (low(grad),)
low.defvjp(low_keep, low_pass)
low_back.defvjp(back_keep, back_low)

def mult(left, right):
    return jnp.dot(left, right, precision=lax.Precision.HIGHEST, preferred_element_type=jnp.float32)

def layer_norm(values, gain_row, offset):
    centre = values - lax.optimization_barrier(jnp.mean(values, axis=-1, keepdims=True))
    spread = lax.optimization_barrier(jnp.mean(centre * centre, axis=-1, keepdims=True))
    return centre * lax.rsqrt(spread + ln_eps) * gain_row + offset

def compact(selected, capacity):
    total_rows = selected.shape[0]
    as_ints = selected.astype(jnp.int32)
    target = jnp.where(selected, jnp.cumsum(as_ints) - 1, capacity).astype(jnp.int32)
    places = jnp.zeros((capacity + 1,), jnp.int32).at[target].set(jnp.arange(total_rows, dtype=jnp.int32))
    filled = (jnp.arange(capacity, dtype=jnp.int32) < jnp.sum(as_ints)).astype(jnp.float32)
    return (places[:capacity], filled)

def dense_gates(logits, chosen, width):
    picked = jnp.take_along_axis(logits, chosen, axis=1)
    weights = jax.nn.softmax(picked, axis=-1)
    onehot = (chosen[:, :, None] == jnp.arange(width, dtype=jnp.int32)[None, None, :]).astype(jnp.float32)
    return lax.optimization_barrier(jnp.sum(weights[:, :, None] * onehot, axis=1))

def halt_mix(states, halt_weight):
    remain = jnp.ones((states[0].shape[0], 1), jnp.float32)
    result = jnp.zeros_like(states[0])
    last = len(states) - 1
    for number, current in enumerate(states):
        if number < last:
            chance = jax.nn.sigmoid(lax.optimization_barrier(jnp.sum(current * halt_weight, axis=-1, keepdims=True)))
            result = result + remain * chance * current
            remain = remain * (1.0 - chance)
        else:
            result = result + remain * current
    return result

def block_forward(params, inputs, lengths_row, runs, attn_chosen, ffn_chosen):
    shared, key_value, router_weights, attn_weights, up_weights, down_weights = params
    total_rows = inputs.shape[0]
    positions = jnp.arange(total_rows, dtype=jnp.int32)
    bounds = jnp.cumsum(lengths_row)
    segment = lax.optimization_barrier(jnp.sum((positions[:, None] >= bounds[None, :]).astype(jnp.int32), axis=1))
    valid = segment < SEQS
    kv_low = low(key_value)
    router_low = low(router_weights)
    attn_low = low(attn_weights)
    up_low = low(up_weights)
    down_low = low(down_weights)
    scale = HD ** (-0.5)
    state = inputs
    states = []
    for loop_id in range(LOOPS):
        running = valid & (loop_id < runs)
        normed = low(layer_norm(state, shared[0], shared[1]))
        kv_vals = low(low_back(mult(normed, kv_low)))
        key_rows = kv_vals[:, :HD]
        value_rows = kv_vals[:, HD:]
        chosen_att = attn_chosen[loop_id]
        att_gates = dense_gates(low_back(mult(normed, router_low[:, :NATT])), chosen_att, NATT)

        def attend(carry, item):
            weight_one, expert = item
            selected = jnp.any(chosen_att == expert, axis=1) & running
            places, filled = compact(selected, CAP_ATT)
            gate_rows = jnp.take(att_gates, expert, axis=1)[places] * filled
            query = low(low_back(mult(normed[places], weight_one[:, :HD])))
            scores = low_back(mult(query, key_rows.T) * scale)
            allowed = (segment[places][:, None] == segment[None, :]) & (positions[None, :] <= places[:, None])
            prob = jax.nn.softmax(jnp.where(allowed, scores, masked_score), axis=-1)
            out_rows = low(low_back(mult(low(prob), value_rows)))
            part = low_back(mult(out_rows, weight_one[:, HD:].T))
            return (carry.at[places].add(part * gate_rows[:, None]), None)
        mixed = lax.scan(jax.checkpoint(attend), jnp.zeros_like(state), (attn_low, jnp.arange(NATT, dtype=jnp.int32)))[0]
        middle = state + mixed
        second = low(layer_norm(middle, shared[2], shared[3]))
        chosen_ffn = ffn_chosen[loop_id]
        ffn_gates = dense_gates(low_back(mult(second, router_low[:, NATT:])), chosen_ffn, NFF)

        def expert_ffn(carry, item):
            up_one, down_one, expert = item
            selected = jnp.any(chosen_ffn == expert, axis=1) & running
            places, filled = compact(selected, CAP_FF)
            gate_rows = jnp.take(ffn_gates, expert, axis=1)[places] * filled
            inner = low_back(mult(second[places], up_one))
            hidden = low(jax.nn.gelu(inner))
            part = low_back(mult(hidden, down_one.T))
            return (carry.at[places].add(part * gate_rows[:, None]), None)
        ffn_out = lax.scan(jax.checkpoint(expert_ffn), jnp.zeros_like(state), (up_low, down_low, jnp.arange(NFF, dtype=jnp.int32)))[0]
        state = jnp.where(running[:, None], middle + ffn_out, state)
        states.append(state)
    return halt_mix(tuple(states), shared[4])

def adam_update(weight, moment, second, grad, rate, decay):
    moment_new = beta_one * moment + (1.0 - beta_one) * grad
    second_new = beta_two * second + (1.0 - beta_two) * grad * grad
    moment_hat = moment_new / (1.0 - beta_one ** STEP)
    second_hat = second_new / (1.0 - beta_two ** STEP)
    weight_new = weight - rate * (moment_hat / (jnp.sqrt(second_hat) + adam_eps) + decay * weight)
    return (weight_new, moment_new, second_new)

def reference(block_input, cotangent, lengths, run_loops, attn_routes, ffn_routes, shared_vectors, shared_moment, shared_second, key_value, kv_moment, kv_second, router_weights, router_moment, router_second, attn_weights, attn_moment, attn_second, up_weights, up_moment, up_second, down_weights, down_moment, down_second):
    params = (shared_vectors, key_value, router_weights, attn_weights, up_weights, down_weights)
    inputs = block_input.astype(jnp.float32).reshape(N_DP, TOK_DEV, D)
    grads_in = cotangent.astype(jnp.float32).reshape(N_DP, TOK_DEV, D)
    runs = run_loops.reshape(N_DP, TOK_DEV)
    attn_split = attn_routes.reshape(LOOPS, N_DP, TOK_DEV, KATT).transpose(1, 0, 2, 3)
    ffn_split = ffn_routes.reshape(LOOPS, N_DP, TOK_DEV, KFF).transpose(1, 0, 2, 3)

    def per_block(acc, item):
        block_in, block_grad, lengths_row, runs_row, attn_row, ffn_row = item

        def forward(weights_all, rows_in):
            return block_forward(weights_all, rows_in, lengths_row, runs_row, attn_row, ffn_row)
        result, back = jax.vjp(forward, params, block_in)
        param_grads, row_grad = back(block_grad)
        acc = jax.tree.map(lambda left, right: left + right, acc, param_grads)
        return (acc, (result, row_grad))
    zeros = jax.tree.map(jnp.zeros_like, params)
    grads, (outputs, row_grads) = lax.scan(per_block, zeros, (inputs, grads_in, lengths, runs, attn_split, ffn_split))
    shared_g, kv_g, router_g, attn_g, up_g, down_g = grads
    shared_rates = jnp.array([6.0, 6.0, 6.0, 6.0, 20.0 / math.sqrt(D)], dtype=jnp.float32)[:, None]
    attn_rates = jnp.concatenate([jnp.full((HD,), 25.0 / math.sqrt(D), jnp.float32), jnp.full((HD,), 50.0 / math.sqrt(HD), jnp.float32)])
    shared_new = adam_update(shared_vectors, shared_moment, shared_second, shared_g, shared_rates, 0.0)
    kv_new = adam_update(key_value, kv_moment, kv_second, kv_g, 20.0 / math.sqrt(D), decay_rate)
    router_new = adam_update(router_weights, router_moment, router_second, router_g, 50.0 / math.sqrt(3 * D), decay_rate)
    attn_new = adam_update(attn_weights, attn_moment, attn_second, attn_g, attn_rates, decay_rate)
    up_new = adam_update(up_weights, up_moment, up_second, up_g, 14.0 / math.sqrt(D), decay_rate)
    down_new = adam_update(down_weights, down_moment, down_second, down_g, 17.0 / math.sqrt(FF), decay_rate)
    return (outputs.reshape(TOKENS, D), row_grads.reshape(TOKENS, D), shared_new[0], shared_new[1], shared_new[2], kv_new[0], kv_new[1], kv_new[2], router_new[0], router_new[1], router_new[2], attn_new[0], attn_new[1], attn_new[2], attn_new[0].astype(jnp.bfloat16), up_new[0], up_new[1], up_new[2], up_new[0].astype(jnp.bfloat16), down_new[0], down_new[1], down_new[2], down_new[0].astype(jnp.bfloat16))
```

```python
import functools
import math

import jax
import jax.numpy as jnp
from jax import lax
from jax.experimental import pallas as pl
from jax.experimental.pallas import tpu as pltpu
from jax.sharding import PartitionSpec as P

D = 512
HD = 64
FF = 2048
KATT = 4
KFF = 2
LOOPS = 3
STEP = 10
MAXLEN = 512
FILLED = 896

ln_eps = 1e-05
beta_one = 0.9
beta_two = 0.999
adam_eps = 1e-08
decay_rate = 0.01
masked_score = -1e30

F32 = jnp.float32
BF16 = jnp.bfloat16
MESH = pl.DeviceIdType.MESH
LANES = 128
RANK_LANE = 16
RUN_LANE = 17
SEG_LANE = 18
TILE = 512
EXTRA = 16


def nn(left, right):
    return lax.dot_general(left, right, (((1,), (0,)), ((), ())), preferred_element_type=F32)


def nt(left, right):
    return lax.dot_general(left, right, (((1,), (1,)), ((), ())), preferred_element_type=F32)


def tn(left, right):
    return lax.dot_general(left, right, (((0,), (0,)), ((), ())), preferred_element_type=F32)


def normalise(values):
    centre = values - jnp.mean(values, axis=-1, keepdims=True)
    inverse = lax.rsqrt(jnp.mean(centre * centre, axis=-1, keepdims=True) + ln_eps)
    return centre * inverse, inverse


def norm_back(grad, unit, inverse, gain):
    scaled = grad * gain
    first = jnp.mean(scaled, axis=-1, keepdims=True)
    second = jnp.mean(scaled * unit, axis=-1, keepdims=True)
    return inverse * (scaled - first - unit * second)


def masked_softmax(logits, valid):
    top = jnp.max(jnp.where(valid, logits, masked_score), axis=-1, keepdims=True)
    powers = jnp.where(valid, jnp.exp(jnp.where(valid, logits - top, 0.0)), 0.0)
    return powers / jnp.maximum(jnp.sum(powers, axis=-1, keepdims=True), 0.5)


def adam_update(weight, moment, second, grad, rate, decay):
    moment_new = beta_one * moment + (1.0 - beta_one) * grad
    second_new = beta_two * second + (1.0 - beta_two) * grad * grad
    moment_hat = moment_new / (1.0 - beta_one**STEP)
    second_hat = second_new / (1.0 - beta_two**STEP)
    weight_new = weight - rate * (moment_hat / (jnp.sqrt(second_hat) + adam_eps) + decay * weight)
    return (weight_new, moment_new, second_new)


def block_kernel(
    n_exp,
    n_dp,
    n_act,
    cap,
    x_ref,
    cot_ref,
    meta_ref,
    rowm_ref,
    vec_ref,
    kvw_ref,
    rw_ref,
    aw_ref,
    uw_ref,
    dw_ref,
    out_ref,
    xgrad_ref,
    ugrad_ref,
    dgrad_ref,
    agrad_ref,
    small_ref,
    kvb,
    rb,
    w_all,
    up_w,
    down_w,
    up_acc,
    down_acc,
    attn_acc,
    small_acc,
    state,
    middle,
    normed_k,
    second_k,
    kv_k,
    q_k,
    o_k,
    p_k,
    bias,
    mix,
    dga,
    dkv_t,
    dkv,
    gate_k,
    rows_all,
    rows_k,
    hid,
    gprime,
    part_k,
    fgate_k,
    sgrad,
    carry,
    total,
    pair_send,
    pair_recv,
    far_send,
    far_recv,
    dkv_send,
    dkv_recv,
    ug_recv,
    dg_recv,
    a_pair_send,
    a_pair_recv,
    a_far_send,
    a_far_recv,
    a_total,
    a_stage,
    a_recv,
    s_pair_send,
    s_pair_recv,
    s_far_send,
    s_far_recv,
    s_total,
    s_dp,
    s_all,
    w_send,
    w_recv,
    ag_send,
    ag_recv,
    kg_send,
    kg_recv,
    wg_send,
    wg_recv,
    sg_send,
    sg_recv,
    rs_sems,
    s_sems,
    a_sems,
    dk_send,
    dk_recv,
    g_send,
    g_recv,
    t_send,
    t_recv,
):
    me = lax.axis_index("expert")
    dp = lax.axis_index("dp")
    pairs = n_exp // 2
    core = lax.rem(me, 2)
    chip = lax.div(me, 2)
    sibling = 2 * chip + 1 - core
    own = x_ref.shape[0]
    width = x_ref.shape[1]
    shard = aw_ref.shape[0]
    valid_rows = n_act * own
    window = min(n_act, MAXLEN // own + 1)
    keys = window * own
    win_at = jnp.clip(me - (window - 1), 0, n_act - window)
    scale = HD ** (-0.5)
    active = me < n_act

    def to_expert(src, dst, send, recv, where):
        return pltpu.make_async_remote_copy(
            src_ref=src,
            dst_ref=dst,
            send_sem=send,
            recv_sem=recv,
            device_id={"expert": where},
            device_id_type=MESH,
        )

    def to_dp(src, dst, send, recv, where):
        return pltpu.make_async_remote_copy(
            src_ref=src,
            dst_ref=dst,
            send_sem=send,
            recv_sem=recv,
            device_id={"dp": where},
            device_id_type=MESH,
        )

    def each_peer(body):
        def step(k, none):
            body(lax.rem(dp + k, n_dp))
            return none

        lax.fori_loop(1, n_dp, step, 0)

    def gather_start(buf, send, recv, count):
        @pl.when(me < count)
        def _():
            for k in range(1, pairs):
                zz = lax.rem(chip + k, pairs)
                to_expert(buf.at[me], buf.at[me], send.at[zz], recv.at[me], 2 * zz + core).start()
            to_expert(buf.at[me], buf.at[me], send.at[chip], recv.at[me], sibling).start()

    def gather_finish(buf, send, recv, count):
        for k in range(1, pairs):
            zz = lax.rem(chip + k, pairs)
            src = 2 * zz + core

            @pl.when(src < count)
            def _():
                to_expert(buf.at[src], buf.at[src], send.at[zz], recv.at[src], src).wait_recv()
                to_expert(
                    buf.at[src], buf.at[src], send.at[pairs + zz], recv.at[src], sibling
                ).start()

        for k in range(pairs):
            zz = lax.rem(chip + k, pairs)
            src = 2 * zz + 1 - core

            @pl.when(src < count)
            def _():
                to_expert(buf.at[src], buf.at[src], send.at[zz], recv.at[src], sibling).wait_recv()

        @pl.when(me < count)
        def _():
            for k in range(1, pairs):
                zz = lax.rem(chip + k, pairs)
                to_expert(
                    buf.at[me], buf.at[me], send.at[zz], recv.at[me], 2 * zz + core
                ).wait_send()
            to_expert(buf.at[me], buf.at[me], send.at[chip], recv.at[me], sibling).wait_send()

        for k in range(1, pairs):
            zz = lax.rem(chip + k, pairs)
            src = 2 * zz + core

            @pl.when(src < count)
            def _():
                to_expert(
                    buf.at[src], buf.at[src], send.at[pairs + zz], recv.at[src], sibling
                ).wait_send()

    def reduce_blocks(make, count, rows, psend, precv, fsend, frecv, sems, result):
        part = pl.ds(0, rows)
        rs_psend, rs_precv, rs_fsend, rs_frecv = (sems.at[index] for index in range(4))

        def pair_copy(zz):
            return to_expert(
                psend.at[zz, part],
                precv.at[zz, part],
                rs_psend.at[zz],
                rs_precv.at[zz],
                sibling,
            )

        def far_copy(zz, slot):
            return to_expert(
                fsend.at[zz, part],
                frecv.at[slot, part],
                rs_fsend.at[zz],
                rs_frecv.at[slot],
                2 * zz + core,
            )

        for k in range(pairs):
            zz = lax.rem(chip + 1 + k, pairs)
            block = 2 * zz + 1 - core

            @pl.when(block < count)
            def _():
                psend[zz, part] = make(block).astype(BF16)
                pair_copy(zz).start()

        for k in range(1, pairs):
            zz = lax.rem(chip + k, pairs)
            block = 2 * zz + core

            @pl.when(block < count)
            def _():
                mine = make(block)
                pair_copy(zz).wait_recv()
                fsend[zz, part] = (mine + precv[zz, part].astype(F32)).astype(BF16)
                far_copy(zz, chip).start()

        @pl.when(me < count)
        def _():
            mine = make(me)
            pair_copy(chip).wait_recv()
            result[part] = mine + precv[chip, part].astype(F32)
            for k in range(1, pairs):
                zz = lax.rem(chip + k, pairs)
                far_copy(zz, zz).wait_recv()
                result[part] += frecv[zz, part].astype(F32)

        @pl.when(me >= count)
        def _():
            result[part] = jnp.zeros((rows, result.shape[1]), F32)

        for k in range(pairs):
            zz = lax.rem(chip + 1 + k, pairs)

            @pl.when(2 * zz + 1 - core < count)
            def _():
                pair_copy(zz).wait_send()

        for k in range(1, pairs):
            zz = lax.rem(chip + k, pairs)

            @pl.when(2 * zz + core < count)
            def _():
                far_copy(zz, chip).wait_send()

    barrier = pltpu.get_barrier_semaphore()
    for k in range(1, n_exp):
        pl.semaphore_signal(
            barrier, inc=1, device_id={"expert": lax.rem(me + k, n_exp)}, device_id_type=MESH
        )
    for k in range(1, n_dp):
        pl.semaphore_signal(
            barrier, inc=1, device_id={"dp": lax.rem(dp + k, n_dp)}, device_id_type=MESH
        )
    dp_rows = pl.ds(pl.multiple_of(dp * shard, shard), shard)
    w_all[me, dp_rows] = aw_ref[...].astype(BF16)
    up_w[dp_rows] = uw_ref[...].astype(BF16)
    down_w[dp_rows] = dw_ref[...].astype(BF16)
    pl.semaphore_wait(barrier, n_exp + n_dp - 2)

    def weight_copy(index, peer, slot):
        rows = pl.ds(pl.multiple_of(slot * shard, shard), shard)
        ref = (w_all.at[me], up_w, down_w)[index].at[rows]
        return to_dp(ref, ref, w_send.at[index, peer], w_recv.at[index, slot], peer)

    for index in range(3):
        each_peer(lambda peer, index=index: weight_copy(index, peer, dp).start())

    kvb[...] = kvw_ref[...].astype(BF16)
    rb[...] = rw_ref[...].astype(BF16)
    gain_one = vec_ref[0:1, :]
    bias_one = vec_ref[1:2, :]
    gain_two = vec_ref[2:3, :]
    bias_two = vec_ref[3:4, :]
    halt = vec_ref[4:5, :]
    state[0] = x_ref[...].astype(F32)
    own_rows = pl.ds(pl.multiple_of(me * own, own), own)
    seg_own = meta_ref[0, own_rows, SEG_LANE : SEG_LANE + 1]
    key_cols = pl.ds(pl.multiple_of(win_at * own, own), keys)
    seg_keys = rowm_ref[LOOPS, :, key_cols]
    row_at = me * own + lax.broadcasted_iota(jnp.int32, (own, keys), 0)
    key_at = win_at * own + lax.broadcasted_iota(jnp.int32, (own, keys), 1)
    allowed = (seg_own == seg_keys) & (key_at <= row_at)
    bias[...] = jnp.where(allowed, 0.0, masked_score)
    up_acc[...] = jnp.zeros_like(up_acc)
    down_acc[...] = jnp.zeros_like(down_acc)
    attn_acc[...] = jnp.zeros_like(attn_acc)
    small_acc[...] = jnp.zeros_like(small_acc)

    each_peer(lambda peer: weight_copy(0, peer, peer).wait_recv())
    gather_start(w_all, wg_send, wg_recv, n_exp)
    gather_finish(w_all, wg_send, wg_recv, n_exp)

    lane = lax.broadcasted_iota(jnp.int32, (own, LANES), 1)
    lane_two = lax.broadcasted_iota(jnp.int32, (2 * own, LANES), 1)
    lane_cap = lax.broadcasted_iota(jnp.int32, (cap, LANES), 1)
    slot_rows = lax.broadcasted_iota(jnp.int32, (cap, valid_rows), 0).astype(F32)
    slot_cols = lax.broadcasted_iota(jnp.int32, (own, cap), 1).astype(F32)

    def gather_matrix(loop):
        ranks = rowm_ref[loop, :, 0:valid_rows]
        return jnp.where(slot_rows == ranks, 1.0, 0.0).astype(BF16)

    def scatter_matrix(loop, block):
        rows = pl.ds(pl.multiple_of(block * own, own), own)
        ranks = meta_ref[loop, rows, RANK_LANE : RANK_LANE + 1]
        return jnp.where(slot_cols == ranks, 1.0, 0.0).astype(BF16)

    def column(values, index, lanes):
        return jnp.sum(jnp.where(lanes == index, values, 0.0), axis=1, keepdims=True)

    def cap_rows(loop):
        return pl.ds(pl.multiple_of(loop * cap, cap), cap)

    def window_keys(loop):
        return kv_k[loop, pl.ds(win_at, window)].reshape(keys, 2 * HD)

    def forward(loop, none):
        current = state[loop]
        unit, _ = normalise(current)
        normed = (unit * gain_one + bias_one).astype(BF16)
        normed_k[loop] = normed
        kv_k[loop, me] = nn(normed, kvb[...]).astype(BF16)
        gather_start(kv_k.at[loop], kg_send, kg_recv, n_act)
        info = meta_ref[loop, own_rows]
        running = info[:, RUN_LANE : RUN_LANE + 1]
        gates = masked_softmax(nn(normed, rb[...]), (info > 0.5) & (lane < n_exp))
        gate_k[loop] = gates

        def queries(expert, none):
            query = jnp.where(lane < HD, nn(normed, w_all[expert]), 0.0).astype(BF16)
            q_k[loop, pl.ds(pl.multiple_of(expert * own, own), own)] = query
            return none

        lax.fori_loop(0, n_exp, queries, 0)
        gather_finish(kv_k.at[loop], kg_send, kg_recv, n_act)
        kv_rows = window_keys(loop)
        mix[...] = jnp.zeros_like(mix)

        def attend(pair, none):
            rows = pl.ds(pl.multiple_of(pair * 2 * own, 2 * own), 2 * own)
            scores = nt(q_k[loop, rows], kv_rows) * scale
            scores = (scores.reshape(2, own, keys) + bias[...][None]).reshape(2 * own, keys)
            powers = jnp.exp(scores - jnp.max(scores, axis=1, keepdims=True))
            prob = (powers * (1.0 / jnp.sum(powers, axis=1, keepdims=True))).astype(BF16)
            p_k[loop, rows] = prob
            outs = jnp.where(lane_two < HD, 0.0, nn(prob, kv_rows)).astype(BF16)
            o_k[loop, rows] = outs
            for half in range(2):
                expert = 2 * pair + half
                gate = column(gates, expert, lane) * running
                mix[...] += gate * nt(outs[half * own : (half + 1) * own], w_all[expert])
            return none

        lax.fori_loop(0, n_exp // 2, attend, 0)
        centre = current + mix[...]
        middle[loop] = centre
        unit, _ = normalise(centre)
        second = (unit * gain_two + bias_two).astype(BF16)
        second_k[loop] = second
        rows_all[me] = second
        gather_start(rows_all, ag_send, ag_recv, n_act)

        @pl.when(loop == 0)
        def _():
            for index in (1, 2):
                each_peer(lambda peer, index=index: weight_copy(index, peer, peer).wait_recv())

        gather_finish(rows_all, ag_send, ag_recv, n_act)
        places = gather_matrix(loop)
        rows_in = nn(places, rows_all[0:n_act].reshape(valid_rows, width)).astype(BF16)
        rows_k[cap_rows(loop)] = rows_in
        chosen = nn(places, meta_ref[loop, 0:valid_rows].astype(BF16))
        allowed_lanes = (chosen > 0.5) & (lane_cap >= n_exp) & (lane_cap < 2 * n_exp)
        gate = column(masked_softmax(nn(rows_in, rb[...]), allowed_lanes), n_exp + me, lane_cap)
        fgate_k[cap_rows(loop)] = gate
        part_k[cap_rows(loop)] = jnp.zeros((cap, width), F32)

        def hidden_tile(tile, none):
            cols = pl.ds(pl.multiple_of(tile * TILE, TILE), TILE)
            inner = nn(rows_in, up_w[:, cols])
            root = math.sqrt(2.0 / math.pi)
            square = inner * inner
            curve = jnp.tanh(root * inner * (1.0 + 0.044715 * square))
            upper = 0.5 * (1.0 + curve)
            hidden = (inner * upper).astype(BF16)
            slope = upper + 0.5 * inner * (1.0 - curve * curve) * (
                root + (3.0 * 0.044715 * root) * square
            )
            hid[cap_rows(loop), cols] = hidden
            gprime[cap_rows(loop), cols] = slope.astype(BF16)
            part_k[cap_rows(loop)] += nt(hidden, down_w[:, cols])
            return none

        lax.fori_loop(0, up_w.shape[1] // TILE, hidden_tile, 0)
        terms = (part_k[cap_rows(loop)] * gate).astype(BF16)
        reduce_blocks(
            lambda block: nn(scatter_matrix(loop, block), terms),
            n_act,
            own,
            pair_send,
            pair_recv,
            far_send,
            far_recv,
            rs_sems,
            total,
        )
        state[loop + 1] = jnp.where(running > 0.5, centre + total[0:own], current)
        return none

    lax.fori_loop(0, LOOPS, forward, 0)

    cot = cot_ref[...].astype(F32)
    first, next_one, last = state[1], state[2], state[3]
    chance_one = jax.nn.sigmoid(jnp.sum(first * halt, axis=1, keepdims=True))
    chance_two = jax.nn.sigmoid(jnp.sum(next_one * halt, axis=1, keepdims=True))
    stay = 1.0 - chance_one
    weight_two = stay * chance_two
    weight_three = stay * (1.0 - chance_two)
    out_ref[...] = chance_one * first + weight_two * next_one + weight_three * last
    dot_one = jnp.sum(cot * first, axis=1, keepdims=True)
    dot_two = jnp.sum(cot * next_one, axis=1, keepdims=True)
    dot_three = jnp.sum(cot * last, axis=1, keepdims=True)
    slope_one = (chance_one * stay) * (
        dot_one - chance_two * dot_two - (1.0 - chance_two) * dot_three
    )
    slope_two = (chance_two * (1.0 - chance_two)) * stay * (dot_two - dot_three)
    sgrad[0] = chance_one * cot + slope_one * halt
    sgrad[1] = weight_two * cot + slope_two * halt
    sgrad[2] = weight_three * cot
    vec_at = 2 * HD + EXTRA
    small_acc[vec_at + 4 : vec_at + 5] = jnp.sum(
        slope_one * first + slope_two * next_one, axis=0, keepdims=True
    )
    carry[...] = jnp.zeros_like(carry)

    def weight_grad_copy(index, peer, slot):
        src = (hid, gprime)[index].at[pl.ds(pl.multiple_of(peer * shard, shard), shard)]
        dst = (ug_recv, dg_recv)[index].at[pl.ds(pl.multiple_of(slot * shard, shard), shard)]
        return to_dp(src, dst, g_send.at[index, peer], g_recv.at[index, slot], peer)

    def backward(step, none):
        loop = LOOPS - 1 - step
        info = meta_ref[loop, own_rows]
        running = info[:, RUN_LANE : RUN_LANE + 1]
        after = sgrad[loop] + carry[...]
        branch = after * running
        rows_all[me] = branch.astype(BF16)
        gather_start(rows_all, ag_send, ag_recv, n_act)
        gather_finish(rows_all, ag_send, ag_recv, n_act)
        places = gather_matrix(loop)
        grad_rows = nn(places, rows_all[0:n_act].reshape(valid_rows, width))
        gate = fgate_k[cap_rows(loop)]
        gate_grad = jnp.sum(grad_rows * part_k[cap_rows(loop)], axis=1, keepdims=True)
        scaled = (grad_rows * gate).astype(BF16)
        rows_in = rows_k[cap_rows(loop)]
        part_k[cap_rows(loop)] = jnp.zeros((cap, width), F32)

        def hidden_tile(tile, none):
            cols = pl.ds(pl.multiple_of(tile * TILE, TILE), TILE)
            hidden = hid[cap_rows(loop), cols]
            down_acc[:, cols] += tn(scaled, hidden)
            inner_grad = (
                nn(scaled, down_w[:, cols]) * gprime[cap_rows(loop), cols].astype(F32)
            ).astype(BF16)
            up_acc[:, cols] += tn(rows_in, inner_grad)
            part_k[cap_rows(loop)] += nt(inner_grad, up_w[:, cols])
            return none

        lax.fori_loop(0, up_w.shape[1] // TILE, hidden_tile, 0)
        terms = part_k[cap_rows(loop)].astype(BF16)
        high = gate_grad.astype(BF16).astype(F32)
        spread = jnp.where(lane_cap == n_exp + me, high, 0.0) + jnp.where(
            lane_cap == me, gate_grad - high, 0.0
        )
        spread_t = jnp.transpose(spread)[0:EXTRA].astype(BF16)

        def row_terms(block):
            matrix = scatter_matrix(loop, block)
            grads = nt(spread_t, matrix)
            return jnp.concatenate(
                [
                    nn(matrix, terms),
                    jnp.concatenate([grads, jnp.zeros((EXTRA, width - own), F32)], axis=1),
                ],
                axis=0,
            )

        reduce_blocks(
            row_terms,
            n_act,
            own + EXTRA,
            pair_send,
            pair_recv,
            far_send,
            far_recv,
            rs_sems,
            total,
        )

        @pl.when(loop == 0)
        def _():
            hid[0:width] = up_acc[...].astype(BF16)
            each_peer(lambda peer: weight_grad_copy(0, peer, dp).start())
            gprime[0:width] = down_acc[...].astype(BF16)
            each_peer(lambda peer: weight_grad_copy(1, peer, dp).start())

        second_grad = total[0:own]
        gate_rows = total[own : own + n_exp, 0:own] + total[own + n_exp : own + 2 * n_exp, 0:own]
        gate_rows = jnp.concatenate(
            [jnp.zeros((n_exp, own), F32), gate_rows, jnp.zeros((LANES - 2 * n_exp, own), F32)],
            axis=0,
        )
        gate_grads = jnp.transpose(gate_rows)
        second = second_k[loop]
        gates = masked_softmax(
            nn(second, rb[...]), (info > 0.5) & (lane >= n_exp) & (lane < 2 * n_exp)
        )
        logit_grad = (
            gates * (gate_grads - jnp.sum(gates * gate_grads, axis=1, keepdims=True))
        ).astype(BF16)
        small_acc[2 * HD : vec_at] += tn(logit_grad, second)[0:EXTRA]
        second_grad = second_grad + nt(logit_grad, rb[...])
        unit, inverse = normalise(middle[loop])
        small_acc[vec_at + 2 : vec_at + 3] += jnp.sum(second_grad * unit, axis=0, keepdims=True)
        small_acc[vec_at + 3 : vec_at + 4] += jnp.sum(second_grad, axis=0, keepdims=True)
        middle_grad = norm_back(second_grad, unit, inverse, gain_two) + branch

        normed = normed_k[loop]
        gates = gate_k[loop]
        kv_rows = window_keys(loop)
        mix[...] = jnp.zeros_like(mix)
        dga[...] = jnp.zeros_like(dga)
        dkv_t[...] = jnp.zeros_like(dkv_t)

        def attend_back(pair, none):
            rows = pl.ds(pl.multiple_of(pair * 2 * own, 2 * own), 2 * own)
            outs = o_k[loop, rows]
            out_grads, parts = [], []
            for half in range(2):
                expert = 2 * pair + half
                out_half = outs[half * own : (half + 1) * own]
                gate = column(gates, expert, lane)
                dot = jnp.sum(middle_grad * nt(out_half, w_all[expert]), axis=1, keepdims=True)
                dga[...] += jnp.where(lane == expert, dot, 0.0)
                part_grad = (gate * middle_grad).astype(BF16)
                parts.append(part_grad)
                out_grads.append(
                    jnp.where(lane < HD, 0.0, nn(part_grad, w_all[expert])).astype(BF16)
                )
            out_grad = jnp.concatenate(out_grads, axis=0)
            prob_low = p_k[loop, rows]
            prob = prob_low.astype(F32)
            prob_grad = nt(out_grad, kv_rows)
            centre = jnp.sum(prob * prob_grad, axis=1, keepdims=True)
            score_grad = (prob * (prob_grad - centre)).astype(BF16)
            query_grad = jnp.where(lane_two < HD, nn(score_grad, kv_rows) * scale, 0.0).astype(BF16)
            query = q_k[loop, rows]
            dkv_t[...] += tn(query, score_grad) * scale + tn(out_grad, prob_low)
            for half in range(2):
                expert = 2 * pair + half
                cut = slice(half * own, (half + 1) * own)
                attn_acc[expert] += tn(query_grad[cut], normed) + tn(outs[cut], parts[half])
                mix[...] += nt(query_grad[cut], w_all[expert])
            return none

        lax.fori_loop(0, n_exp // 2, attend_back, 0)
        for block in range(window):
            grads = jnp.transpose(dkv_t[:, block * own : (block + 1) * own])
            dkv[block] = grads
            dkv_send[block] = grads.astype(BF16)

        def kv_copy(distance, owner):
            return to_expert(
                dkv_send.at[jnp.clip(owner - win_at, 0, window - 1)],
                dkv_recv.at[distance - 1],
                dk_send.at[distance - 1],
                dk_recv.at[distance - 1],
                owner,
            )

        for distance in range(1, window):

            @pl.when(active & (me >= distance))
            def _():
                kv_copy(distance, me - distance).start()

        gate_grads = dga[...]
        logit_grad = (
            gates * (gate_grads - jnp.sum(gates * gate_grads, axis=1, keepdims=True))
        ).astype(BF16)
        small_acc[2 * HD : vec_at] += tn(logit_grad, normed)[0:EXTRA]
        normed_grad = mix[...] + nt(logit_grad, rb[...])
        unit, inverse = normalise(state[loop])

        own_block = jnp.clip(me - win_at, 0, window - 1)
        dkv[window] = jnp.where(active, dkv[own_block], 0.0)
        for distance in range(1, window):

            @pl.when(me + distance < n_act)
            def _():
                to_expert(
                    dkv_send.at[0],
                    dkv_recv.at[distance - 1],
                    dk_send.at[distance - 1],
                    dk_recv.at[distance - 1],
                    me + distance,
                ).wait_recv()
                dkv[window] += dkv_recv[distance - 1].astype(F32)

        for distance in range(1, window):

            @pl.when(active & (me >= distance))
            def _():
                kv_copy(distance, me - distance).wait_send()

        kv_grad = dkv[window].astype(BF16)
        small_acc[0 : 2 * HD] += tn(kv_grad, normed)
        normed_grad = normed_grad + nt(kv_grad, kvb[...])
        small_acc[vec_at : vec_at + 1] += jnp.sum(normed_grad * unit, axis=0, keepdims=True)
        small_acc[vec_at + 1 : vec_at + 2] += jnp.sum(normed_grad, axis=0, keepdims=True)
        carry[...] = (
            after * (1.0 - running)
            + middle_grad
            + norm_back(normed_grad, unit, inverse, gain_one)
        )
        return none

    lax.fori_loop(0, LOOPS, backward, 0)
    xgrad_ref[...] = carry[...]

    chunk = small_acc.shape[0] // n_exp
    reduce_blocks(
        lambda block: small_acc[pl.ds(pl.multiple_of(block * chunk, chunk), chunk)],
        n_exp,
        chunk,
        s_pair_send,
        s_pair_recv,
        s_far_send,
        s_far_recv,
        s_sems,
        s_total,
    )
    s_dp[dp] = s_total[...].astype(BF16)

    def small_copy(peer, slot):
        return to_dp(s_dp.at[slot], s_dp.at[slot], t_send.at[0, peer], t_recv.at[0, slot], peer)

    each_peer(lambda peer: small_copy(peer, dp).start())

    reduce_blocks(
        lambda block: jnp.transpose(attn_acc[block]),
        n_exp,
        width,
        a_pair_send,
        a_pair_recv,
        a_far_send,
        a_far_recv,
        a_sems,
        a_total,
    )
    a_stage[...] = a_total[...].astype(BF16)

    def attn_copy(peer, slot):
        src = a_stage.at[pl.ds(pl.multiple_of(peer * shard, shard), shard)]
        dst = a_recv.at[pl.ds(pl.multiple_of(slot * shard, shard), shard)]
        return to_dp(src, dst, t_send.at[1, peer], t_recv.at[1, slot], peer)

    each_peer(lambda peer: attn_copy(peer, dp).start())

    each_peer(lambda peer: small_copy(peer, peer).wait_recv())
    s_total[...] = jnp.zeros_like(s_total)

    def add_small(index, none):
        s_total[...] += s_dp[index].astype(F32)
        return none

    lax.fori_loop(0, n_dp, add_small, 0)
    s_all[me] = s_total[...]
    gather_start(s_all, sg_send, sg_recv, n_exp)

    each_peer(lambda peer: attn_copy(peer, peer).wait_recv())
    agrad_ref[...] = a_total[dp_rows]

    def add_attn(peer):
        rows = pl.ds(pl.multiple_of(peer * shard, shard), shard)
        agrad_ref[...] += a_recv[rows].astype(F32)

    each_peer(add_attn)
    ugrad_ref[...] = up_acc[dp_rows]
    dgrad_ref[...] = down_acc[dp_rows]

    def add_up(peer):
        rows = pl.ds(pl.multiple_of(peer * shard, shard), shard)
        weight_grad_copy(0, peer, peer).wait_recv()
        ugrad_ref[...] += ug_recv[rows].astype(F32)

    def add_down(peer):
        rows = pl.ds(pl.multiple_of(peer * shard, shard), shard)
        weight_grad_copy(1, peer, peer).wait_recv()
        dgrad_ref[...] += dg_recv[rows].astype(F32)

    each_peer(add_up)
    each_peer(add_down)
    gather_finish(s_all, sg_send, sg_recv, n_exp)
    small_ref[...] = s_all[...]

    def sent(peer):
        for index in range(3):
            weight_copy(index, peer, dp).wait_send()
        for index in range(2):
            weight_grad_copy(index, peer, dp).wait_send()
        small_copy(peer, dp).wait_send()
        attn_copy(peer, dp).wait_send()

    each_peer(sent)


def per_device(
    block_input,
    cotangent,
    lengths,
    run_loops,
    attn_routes,
    ffn_routes,
    shared_vectors,
    shared_moment,
    shared_second,
    key_value,
    kv_moment,
    kv_second,
    router_weights,
    router_moment,
    router_second,
    attn_weights,
    attn_moment,
    attn_second,
    up_weights,
    up_moment,
    up_second,
    down_weights,
    down_moment,
    down_second,
):
    n_exp = lax.axis_size("expert")
    n_dp = lax.axis_size("dp")
    me = lax.axis_index("expert")
    own, width = block_input.shape
    row_total = run_loops.shape[0]
    shard = attn_weights.shape[1]
    hidden = up_weights.shape[2]
    cap = 5 * row_total * KFF // (4 * n_exp)
    n_act = FILLED // own
    window = min(n_act, MAXLEN // own + 1)
    pairs = n_exp // 2
    valid_rows = n_act * own

    positions = jnp.arange(row_total, dtype=jnp.int32)
    bounds = jnp.cumsum(lengths[0])
    segment = jnp.sum((positions[:, None] >= bounds[None, :]).astype(jnp.int32), axis=1)
    valid = segment < lengths.shape[1]
    loops = jnp.arange(LOOPS, dtype=jnp.int32)
    running = valid[None, :] & (loops[:, None] < run_loops[None, :])
    selected = jnp.any(ffn_routes == me, axis=2) & running
    ranks = jnp.where(selected, jnp.cumsum(selected.astype(jnp.int32), axis=1) - 1, -1).astype(F32)
    lane = jnp.arange(LANES, dtype=jnp.int32)
    chosen = jnp.any(attn_routes[..., None] == lane, axis=2) | jnp.any(
        ffn_routes[..., None] + n_exp == lane, axis=2
    )
    seg_rows = segment.astype(F32)
    meta = jnp.where(
        lane == RANK_LANE,
        ranks[..., None],
        jnp.where(
            lane == RUN_LANE,
            running.astype(F32)[..., None],
            jnp.where(lane == SEG_LANE, seg_rows[None, :, None], chosen.astype(F32)),
        ),
    )
    row_meta = jnp.concatenate([ranks, seg_rows[None]], axis=0)[:, None, :]
    vectors = jnp.pad(shared_vectors, ((0, 3), (0, 0)))
    router = jnp.pad(router_weights, ((0, 0), (0, LANES - router_weights.shape[1])))

    small_rows = 32 * n_exp
    vmem = pltpu.VMEM
    dma = pltpu.SemaphoreType.DMA
    block = (pairs, own + EXTRA, width)
    attn_block = (pairs, width, 2 * HD)
    small_block = (pairs, 32, width)
    scratch = [
        vmem((width, 2 * HD), BF16),
        vmem((width, LANES), BF16),
        vmem((n_exp, width, 2 * HD), BF16),
        vmem((width, hidden), BF16),
        vmem((width, hidden), BF16),
        vmem((width, hidden), F32),
        vmem((width, hidden), F32),
        vmem((n_exp, 2 * HD, width), F32),
        vmem((small_rows, width), F32),
        vmem((LOOPS + 1, own, width), F32),
        vmem((LOOPS, own, width), F32),
        vmem((LOOPS, own, width), BF16),
        vmem((LOOPS, own, width), BF16),
        vmem((LOOPS, n_exp, own, 2 * HD), BF16),
        vmem((LOOPS, n_exp * own, 2 * HD), BF16),
        vmem((LOOPS, n_exp * own, 2 * HD), BF16),
        vmem((LOOPS, n_exp * own, window * own), BF16),
        vmem((own, window * own), F32),
        vmem((own, width), F32),
        vmem((own, LANES), F32),
        vmem((2 * HD, window * own), F32),
        vmem((window + 1, own, 2 * HD), F32),
        vmem((LOOPS, own, LANES), F32),
        vmem((n_exp, own, width), BF16),
        vmem((LOOPS * cap, width), BF16),
        vmem((LOOPS * cap, hidden), BF16),
        vmem((LOOPS * cap, hidden), BF16),
        vmem((LOOPS * cap, width), F32),
        vmem((LOOPS * cap, 1), F32),
        vmem((LOOPS, own, width), F32),
        vmem((own, width), F32),
        vmem((own + EXTRA, width), F32),
        vmem(block, BF16),
        vmem(block, BF16),
        vmem(block, BF16),
        vmem(block, BF16),
        vmem((window, own, 2 * HD), BF16),
        vmem((window, own, 2 * HD), BF16),
        vmem((width, hidden), BF16),
        vmem((width, hidden), BF16),
        vmem(attn_block, BF16),
        vmem(attn_block, BF16),
        vmem(attn_block, BF16),
        vmem(attn_block, BF16),
        vmem((width, 2 * HD), F32),
        vmem((width, 2 * HD), BF16),
        vmem((width, 2 * HD), BF16),
        vmem(small_block, BF16),
        vmem(small_block, BF16),
        vmem(small_block, BF16),
        vmem(small_block, BF16),
        vmem((32, width), F32),
        vmem((n_dp, 32, width), BF16),
        vmem((n_exp, 32, width), F32),
        dma((3, n_dp)),
        dma((3, n_dp)),
        dma((2 * pairs,)),
        dma((n_exp,)),
        dma((2 * pairs,)),
        dma((n_exp,)),
        dma((2 * pairs,)),
        dma((n_exp,)),
        dma((2 * pairs,)),
        dma((n_exp,)),
        dma((4, pairs)),
        dma((4, pairs)),
        dma((4, pairs)),
        dma((window,)),
        dma((window,)),
        dma((2, n_dp)),
        dma((2, n_dp)),
        dma((2, n_dp)),
        dma((2, n_dp)),
    ]
    whole = pl.BlockSpec(memory_space=pltpu.VMEM)
    output, input_grad, up_sum, down_sum, attn_sum, small = pl.pallas_call(
        functools.partial(block_kernel, n_exp, n_dp, n_act, cap),
        out_shape=(
            jax.ShapeDtypeStruct((own, width), F32),
            jax.ShapeDtypeStruct((own, width), F32),
            jax.ShapeDtypeStruct((shard, hidden), F32),
            jax.ShapeDtypeStruct((shard, hidden), F32),
            jax.ShapeDtypeStruct((shard, 2 * HD), F32),
            jax.ShapeDtypeStruct((n_exp, 32, width), F32),
        ),
        in_specs=[whole] * 10,
        out_specs=[whole] * 6,
        scratch_shapes=scratch,
        compiler_params=pltpu.CompilerParams(
            collective_id=0, has_side_effects=True, vmem_limit_bytes=62 * 1024 * 1024
        ),
        name="block",
    )(
        block_input,
        cotangent,
        meta,
        row_meta,
        vectors,
        key_value,
        router,
        attn_weights[0],
        up_weights[0],
        down_weights[0],
    )

    small = small.reshape(small_rows, width)
    kv_sum = small[: 2 * HD].T
    router_sum = small[2 * HD : 2 * HD + 2 * n_exp].T
    shared_sum = small[2 * HD + EXTRA : 2 * HD + EXTRA + 5]
    shared_rates = jnp.array([6.0, 6.0, 6.0, 6.0, 20.0 / math.sqrt(D)], dtype=F32)[:, None]
    attn_rates = jnp.concatenate(
        [
            jnp.full((HD,), 25.0 / math.sqrt(D), F32),
            jnp.full((HD,), 50.0 / math.sqrt(HD), F32),
        ]
    )
    shared_new = adam_update(
        shared_vectors, shared_moment, shared_second, shared_sum, shared_rates, 0.0
    )
    kv_new = adam_update(key_value, kv_moment, kv_second, kv_sum, 20.0 / math.sqrt(D), decay_rate)
    router_new = adam_update(
        router_weights,
        router_moment,
        router_second,
        router_sum,
        50.0 / math.sqrt(3 * D),
        decay_rate,
    )
    attn_new = adam_update(
        attn_weights, attn_moment, attn_second, attn_sum[None], attn_rates, decay_rate
    )
    up_new = adam_update(
        up_weights, up_moment, up_second, up_sum[None], 14.0 / math.sqrt(D), decay_rate
    )
    down_new = adam_update(
        down_weights, down_moment, down_second, down_sum[None], 17.0 / math.sqrt(FF), decay_rate
    )
    return (
        output,
        input_grad,
        *shared_new,
        *kv_new,
        *router_new,
        *attn_new,
        attn_new[0].astype(BF16),
        *up_new,
        up_new[0].astype(BF16),
        *down_new,
        down_new[0].astype(BF16),
    )


def solution(mesh):
    rows = P(("dp", "expert"), None)
    weights = P("expert", "dp", None)
    return jax.shard_map(
        per_device,
        mesh=mesh,
        in_specs=(
            rows,
            rows,
            P("dp", None),
            P("dp"),
            P(None, "dp", None),
            P(None, "dp", None),
            *([P()] * 9),
            *([weights] * 9),
        ),
        out_specs=(rows, rows, *([P()] * 9), *([weights] * 12)),
        check_vma=False,
    )
```

```python
import functools
import math

import jax
import jax.numpy as jnp
from jax import lax
from jax.experimental import pallas as pl
from jax.experimental.pallas import tpu as pltpu
from jax.sharding import PartitionSpec as P

D = 512
HD = 64
FF = 2048
KATT = 4
KFF = 2
LOOPS = 3
STEP = 10
MAXLEN = 512
FILLED = 896

ln_eps = 1e-05
beta_one = 0.9
beta_two = 0.999
adam_eps = 1e-08
decay_rate = 0.01
masked_score = -1e30

F32 = jnp.float32
BF16 = jnp.bfloat16
MESH = pl.DeviceIdType.MESH
LANES = 128
RANK_LANE = 16
RUN_LANE = 17
SEG_LANE = 18
INFO = 32
TILE = 512
EXTRA = 16


def nn(left, right):
    return lax.dot_general(left, right, (((1,), (0,)), ((), ())), preferred_element_type=F32)


def nt(left, right):
    return lax.dot_general(left, right, (((1,), (1,)), ((), ())), preferred_element_type=F32)


def tn(left, right):
    return lax.dot_general(left, right, (((0,), (0,)), ((), ())), preferred_element_type=F32)


def normalise(values):
    centre = values - jnp.mean(values, axis=-1, keepdims=True)
    inverse = lax.rsqrt(jnp.mean(centre * centre, axis=-1, keepdims=True) + ln_eps)
    return centre * inverse, inverse


def norm_back(grad, unit, inverse, gain):
    scaled = grad * gain
    first = jnp.mean(scaled, axis=-1, keepdims=True)
    second = jnp.mean(scaled * unit, axis=-1, keepdims=True)
    return inverse * (scaled - first - unit * second)


def masked_softmax(logits, valid):
    top = jnp.max(jnp.where(valid, logits, masked_score), axis=-1, keepdims=True)
    powers = jnp.where(valid, jnp.exp(jnp.where(valid, logits - top, 0.0)), 0.0)
    return powers / jnp.maximum(jnp.sum(powers, axis=-1, keepdims=True), 0.5)


def adam_update(weight, moment, second, grad, rate, decay):
    moment_new = beta_one * moment + (1.0 - beta_one) * grad
    second_new = beta_two * second + (1.0 - beta_two) * grad * grad
    moment_hat = moment_new * (1.0 / (1.0 - beta_one**STEP))
    second_hat = second_new * (1.0 / (1.0 - beta_two**STEP))
    weight_new = weight - rate * (moment_hat / (jnp.sqrt(second_hat) + adam_eps) + decay * weight)
    return (weight_new, moment_new, second_new)


def block_kernel(
    n_exp,
    n_dp,
    n_act,
    cap,
    x_ref,
    cot_ref,
    len_ref,
    run_ref,
    ar_ref,
    fr_ref,
    vec_ref,
    kvw_ref,
    rw_ref,
    aw_ref,
    uw_hbm,
    dw_hbm,
    out_ref,
    xgrad_ref,
    ugrad_ref,
    dgrad_ref,
    agrad_ref,
    kvgrad_ref,
    rgrad_ref,
    vgrad_ref,
    meta_ref,
    rowm_ref,
    kvb,
    rb,
    w_all,
    up_w,
    down_w,
    up_acc,
    down_acc,
    attn_acc,
    small_acc,
    state,
    middle,
    normed_k,
    second_k,
    kv_k,
    q_k,
    o_k,
    p_k,
    ds_k,
    bias,
    mix,
    dga,
    dkv_t,
    dkv,
    gate_k,
    rows_all,
    rows_two,
    gather_m,
    scatter_m,
    rows_k,
    hid,
    gprime,
    row_grads,
    part_k,
    fgate_k,
    ggrad,
    scaled_k,
    sgrad,
    carry,
    mgrad,
    total,
    total_two,
    pair_send,
    pair_recv,
    far_send,
    far_recv,
    pair_send_two,
    pair_recv_two,
    far_send_two,
    far_recv_two,
    dkv_send,
    dkv_recv,
    u_first,
    u_last,
    d_first,
    d_last,
    a_total,
    a_stage,
    a_recv,
    s_pair_send,
    s_pair_recv,
    s_far_send,
    s_far_recv,
    s_total,
    s_dp,
    s_all,
    in_sems,
    w_send,
    w_recv,
    uw_send,
    uw_recv,
    uw_send_two,
    uw_recv_two,
    dw_send,
    dw_recv,
    dw_send_two,
    dw_recv_two,
    ag_send,
    ag_recv,
    bg_send,
    bg_recv,
    wg_send,
    wg_recv,
    sg_send,
    sg_recv,
    kg_send,
    kg_recv,
    rs_sems,
    rs_sems_two,
    s_sems,
    a_sems,
    dk_send,
    dk_recv,
    ug_send,
    ug_recv,
    ug_send_two,
    ug_recv_two,
    dg_send,
    dg_recv,
    dg_send_two,
    dg_recv_two,
    t_send,
    t_recv,
):
    me = lax.axis_index("expert")
    dp = lax.axis_index("dp")
    pairs = n_exp // 2
    core = lax.rem(me, 2)
    chip = lax.div(me, 2)
    sibling = 2 * chip + 1 - core
    n_low, n_high = dp_grid(n_dp)
    high = lax.div(dp, n_low)
    low = lax.rem(dp, n_low)
    own = x_ref.shape[0]
    width = x_ref.shape[1]
    slots = run_ref.shape[1]
    shard = aw_ref.shape[0]
    hidden_units = up_w.shape[1]
    tiles = hidden_units // TILE
    valid_rows = n_act * own
    window = min(n_act, MAXLEN // own + 1)
    keys = window * own
    win_at = jnp.clip(me - (window - 1), 0, n_act - window)
    scale = HD ** (-0.5)
    active = me < n_act
    last = LOOPS - 1

    def remote(src, dst, send, recv, **where):
        return pltpu.make_async_remote_copy(
            src_ref=src,
            dst_ref=dst,
            send_sem=send,
            recv_sem=recv,
            device_id=where,
            device_id_type=MESH,
        )

    def shard_rows(index, count=1):
        return pl.ds(pl.multiple_of(index * shard, shard), count * shard)

    def each_peer(body):
        def step(k, none):
            body(lax.rem(dp + k, n_dp))
            return none

        lax.fori_loop(1, n_dp, step, 0)

    def high_peers():
        return [lax.rem(high + k, n_high) for k in range(1, n_high)]

    def low_peers():
        return [lax.rem(low + k, n_low) for k in range(1, n_low)]

    class Gather:
        def __init__(self, buf, send, recv, count):
            self.buf, self.send, self.recv, self.count = buf, send, recv, count

        def copy(self, block, sem, where):
            ref = self.buf.at[block]
            return remote(ref, ref, self.send.at[sem], self.recv.at[block], expert=where)

        def start(self):
            @pl.when(me < self.count)
            def _():
                for k in range(1, pairs):
                    zz = lax.rem(chip + k, pairs)
                    self.copy(me, zz, 2 * zz + core).start()
                self.copy(me, chip, sibling).start()

        def finish(self):
            for k in range(pairs - 1, 0, -1):
                zz = lax.rem(chip + k, pairs)
                src = 2 * zz + core

                @pl.when(src < self.count)
                def _():
                    self.copy(src, zz, src).wait_recv()
                    self.copy(src, pairs + zz, sibling).start()

            for k in range(pairs):
                zz = lax.rem(chip + k, pairs)
                src = 2 * zz + 1 - core

                @pl.when(src < self.count)
                def _():
                    self.copy(src, zz, sibling).wait_recv()

            @pl.when(me < self.count)
            def _():
                for k in range(1, pairs):
                    zz = lax.rem(chip + k, pairs)
                    self.copy(me, zz, 2 * zz + core).wait_send()
                self.copy(me, chip, sibling).wait_send()

            for k in range(1, pairs):
                zz = lax.rem(chip + k, pairs)
                src = 2 * zz + core

                @pl.when(src < self.count)
                def _():
                    self.copy(src, pairs + zz, sibling).wait_send()

    class Reduce:
        def __init__(self, count, rows, psend, precv, fsend, frecv, sems, result):
            self.count, self.rows, self.part = count, rows, pl.ds(0, rows)
            self.psend, self.precv, self.fsend, self.frecv = psend, precv, fsend, frecv
            self.sems, self.result = sems, result

        def pair_copy(self, zz):
            return remote(
                self.psend.at[zz, self.part],
                self.precv.at[zz, self.part],
                self.sems.at[0, zz],
                self.sems.at[1, zz],
                expert=sibling,
            )

        def far_copy(self, zz, slot):
            return remote(
                self.fsend.at[zz, self.part],
                self.frecv.at[slot, self.part],
                self.sems.at[2, zz],
                self.sems.at[3, slot],
                expert=2 * zz + core,
            )

        def start(self, make):
            for k in range(pairs):
                zz = lax.rem(chip + 1 + k, pairs)
                block = 2 * zz + 1 - core

                @pl.when(block < self.count)
                def _():
                    self.psend[zz, self.part] = make(block).astype(BF16)
                    self.pair_copy(zz).start()

            for k in range(1, pairs):
                zz = lax.rem(chip + k, pairs)
                block = 2 * zz + core

                @pl.when(block < self.count)
                def _():
                    mine = make(block)
                    self.pair_copy(zz).wait_recv()
                    self.fsend[zz, self.part] = (
                        mine + self.precv[zz, self.part].astype(F32)
                    ).astype(BF16)
                    self.far_copy(zz, chip).start()

            @pl.when(me < self.count)
            def _():
                mine = make(me)
                self.pair_copy(chip).wait_recv()
                self.result[self.part] = mine + self.precv[chip, self.part].astype(F32)

            @pl.when(me >= self.count)
            def _():
                self.result[self.part] = jnp.zeros((self.rows, self.result.shape[1]), F32)

        def finish(self):
            @pl.when(me < self.count)
            def _():
                for k in range(1, pairs):
                    zz = lax.rem(chip + k, pairs)
                    self.far_copy(zz, zz).wait_recv()
                    self.result[self.part] += self.frecv[zz, self.part].astype(F32)

            for k in range(pairs):
                zz = lax.rem(chip + 1 + k, pairs)

                @pl.when(2 * zz + 1 - core < self.count)
                def _():
                    self.pair_copy(zz).wait_send()

            for k in range(1, pairs):
                zz = lax.rem(chip + k, pairs)

                @pl.when(2 * zz + core < self.count)
                def _():
                    self.far_copy(zz, chip).wait_send()

    def attn_weight_copy(peer, slot):
        ref = w_all.at[me, shard_rows(slot)]
        return remote(ref, ref, w_send.at[peer], w_recv.at[slot], dp=peer)

    def up_first(peer, slot):
        ref = up_w.at[shard_rows(high * n_low + slot)]
        return remote(ref, ref, uw_send.at[peer], uw_recv.at[slot], dp=high * n_low + peer)

    def up_second(peer, slot):
        ref = up_w.at[shard_rows(slot * n_low, n_low)]
        return remote(ref, ref, uw_send_two.at[peer], uw_recv_two.at[slot], dp=peer * n_low + low)

    def down_first(peer, slot):
        ref = down_w.at[shard_rows(slot * n_low + low)]
        return remote(ref, ref, dw_send.at[peer], dw_recv.at[slot], dp=peer * n_low + low)

    def down_second(peer, slot, block):
        ref = down_w.at[shard_rows(block * n_low + slot)]
        return remote(
            ref,
            ref,
            dw_send_two.at[peer, block],
            dw_recv_two.at[slot, block],
            dp=high * n_low + peer,
        )

    up_in = pltpu.make_async_copy(uw_hbm, ugrad_ref, in_sems.at[0])
    down_in = pltpu.make_async_copy(dw_hbm, dgrad_ref, in_sems.at[1])
    up_in.start()
    down_in.start()
    kv_k[...] = jnp.zeros_like(kv_k)
    barrier = pltpu.get_barrier_semaphore()
    for k in range(1, n_exp):
        pl.semaphore_signal(
            barrier, inc=1, device_id={"expert": lax.rem(me + k, n_exp)}, device_id_type=MESH
        )
    for k in range(1, n_dp):
        pl.semaphore_signal(
            barrier, inc=1, device_id={"dp": lax.rem(dp + k, n_dp)}, device_id_type=MESH
        )
    w_all[me, shard_rows(dp)] = aw_ref[...].astype(BF16)
    up_in.wait()
    up_w[shard_rows(dp)] = ugrad_ref[...].astype(BF16)
    down_in.wait()
    down_w[shard_rows(dp)] = dgrad_ref[...].astype(BF16)
    pl.semaphore_wait(barrier, n_exp + n_dp - 2)
    each_peer(lambda peer: attn_weight_copy(peer, dp).start())
    for peer in low_peers():
        up_first(peer, low).start()
    for peer in high_peers():
        down_first(peer, high).start()

    kvb[...] = kvw_ref[...].astype(BF16)
    rb[...] = rw_ref[...].astype(BF16)
    gain_one = vec_ref[0:1, :]
    bias_one = vec_ref[1:2, :]
    gain_two = vec_ref[2:3, :]
    bias_two = vec_ref[3:4, :]
    halt = vec_ref[4:5, :]
    state[0] = x_ref[...].astype(F32)
    own_rows = pl.ds(pl.multiple_of(me * own, own), own)

    lane = lax.broadcasted_iota(jnp.int32, (own, LANES), 1)
    route_lane = lax.broadcasted_iota(jnp.int32, (own, 2 * n_exp), 1)
    lane_two = lax.broadcasted_iota(jnp.int32, (2 * own, LANES), 1)
    lane_cap = lax.broadcasted_iota(jnp.int32, (cap, LANES), 1)
    route_cap = lax.broadcasted_iota(jnp.int32, (cap, 2 * n_exp), 1)

    def column(values, index, lanes):
        return jnp.sum(jnp.where(lanes == index, values, 0.0), axis=1, keepdims=True)

    def cap_rows(loop):
        return pl.ds(pl.multiple_of(loop * cap, cap), cap)

    def window_keys(loop):
        return kv_k[loop, pl.ds(win_at, window)].reshape(keys, 2 * HD)

    def routing():
        position = lax.broadcasted_iota(jnp.int32, (1, slots), 1)
        bound = 0
        segment = jnp.zeros((1, slots), F32)
        for index in range(len_ref.shape[1]):
            bound = bound + len_ref[0, index]
            segment = segment + jnp.where(position >= bound, 1.0, 0.0)
        sub = lax.broadcasted_iota(jnp.int32, (n_exp, slots), 0)
        position_all = lax.broadcasted_iota(jnp.int32, (n_exp, slots), 1)
        valid = segment < len_ref.shape[1] - 0.5
        rowm_ref[LOOPS] = segment
        picks, selected = [], jnp.zeros((n_exp, slots), F32)
        for loop in range(LOOPS):
            running = jnp.where(valid & (run_ref[...] > loop), 1.0, 0.0)
            att = jnp.zeros((n_exp, slots), F32)
            for k in range(ar_ref.shape[1]):
                att = att + jnp.where(ar_ref[loop, k : k + 1, :] == sub, 1.0, 0.0)
            ffn = jnp.zeros((n_exp, slots), F32)
            mine = jnp.zeros((1, slots), F32)
            for k in range(fr_ref.shape[1]):
                ffn = ffn + jnp.where(fr_ref[loop, k : k + 1, :] == sub, 1.0, 0.0)
                mine = mine + jnp.where(fr_ref[loop, k : k + 1, :] == me, running, 0.0)
            picks.append((att, ffn, running))
            selected = selected + jnp.where(sub == loop, mine, 0.0)
        ranks = selected
        shift = 1
        while shift < slots:
            moved = pltpu.roll(ranks, shift, 1)
            ranks = ranks + jnp.where(position_all >= shift, moved, 0.0)
            shift *= 2
        ranks = jnp.where(selected > 0.5, ranks - 1.0, -1.0)
        for loop in range(LOOPS):
            att, ffn, running = picks[loop]
            rank = ranks[loop : loop + 1]
            rowm_ref[loop] = rank
            rest = jnp.where(
                sub == 0,
                rank,
                jnp.where(sub == 1, running, jnp.where(sub == 2, segment, 0.0)),
            )
            spare = jnp.zeros((INFO - 3 * n_exp, slots), F32)
            meta_ref[loop] = jnp.transpose(jnp.concatenate([att, ffn, rest, spare], axis=0))

    def kv_copy(loop, where, sem):
        ref = kv_k.at[loop, me]
        return remote(ref, ref, kg_send.at[sem], kg_recv.at[me], expert=where)

    def prepare(loop):
        unit, _ = normalise(state[loop])
        normed = (unit * gain_one + bias_one).astype(BF16)
        normed_k[loop] = normed
        kv_k[loop, me] = nn(normed, kvb[...]).astype(BF16)
        for k in range(1, window):

            @pl.when(me + k < n_act)
            def _():
                kv_copy(loop, me + k, k - 1).start()

        info = meta_ref[loop, own_rows, 0 : 2 * n_exp]
        gate_k[loop] = masked_softmax(
            nt(normed, rb[...]), (info > 0.5) & (route_lane < n_exp)
        )

    def running_rows(loop):
        return meta_ref[loop, own_rows, RUN_LANE : RUN_LANE + 1]

    each_peer(lambda peer: attn_weight_copy(peer, peer).wait_recv())
    weights_gather = Gather(w_all, wg_send, wg_recv, n_exp)
    weights_gather.start()
    routing()
    prepare(0)
    seg_own = meta_ref[0, own_rows, SEG_LANE : SEG_LANE + 1]
    key_cols = pl.ds(pl.multiple_of(win_at * own, own), keys)
    seg_keys = rowm_ref[LOOPS, :, key_cols]
    row_at = me * own + lax.broadcasted_iota(jnp.int32, (own, keys), 0)
    key_at = win_at * own + lax.broadcasted_iota(jnp.int32, (own, keys), 1)
    allowed = (seg_own == seg_keys) & (key_at <= row_at)
    bias[...] = jnp.where(allowed, 0.0, masked_score)
    for peer in low_peers():
        up_first(peer, peer).wait_recv()
    for peer in high_peers():
        up_second(peer, high).start()
    for peer in high_peers():
        down_first(peer, peer).wait_recv()
    for peer in low_peers():
        for block in range(n_high):
            down_second(peer, low, block).start()
    down_acc[...] = jnp.zeros_like(down_acc)
    attn_acc[...] = jnp.zeros_like(attn_acc)
    small_acc[...] = jnp.zeros_like(small_acc)
    weights_gather.finish()

    def attention(loop):
        normed = normed_k[loop]

        def queries(expert, none):
            query = jnp.where(lane < HD, nn(normed, w_all[expert]), 0.0).astype(BF16)
            q_k[loop, pl.ds(pl.multiple_of(expert * own, own), own)] = query
            return none

        lax.fori_loop(0, n_exp, queries, 0)
        running = running_rows(loop)
        gates = gate_k[loop] * running
        mix[...] = jnp.zeros_like(mix)
        for k in range(1, window):

            @pl.when(active & (me >= k))
            def _():
                ref = kv_k.at[loop, me - k]
                remote(
                    ref, ref, kg_send.at[k - 1], kg_recv.at[me - k], expert=me - k
                ).wait_recv()

        kv_rows = window_keys(loop)

        def attend(pair, none):
            rows = pl.ds(pl.multiple_of(pair * 2 * own, 2 * own), 2 * own)
            scores = nt(q_k[loop, rows], kv_rows) * scale
            scores = (scores.reshape(2, own, keys) + bias[...][None]).reshape(2 * own, keys)
            powers = jnp.exp(scores - jnp.max(scores, axis=1, keepdims=True))
            prob = (powers * (1.0 / jnp.sum(powers, axis=1, keepdims=True))).astype(BF16)
            p_k[loop, rows] = prob
            outs = jnp.where(lane_two < HD, 0.0, nn(prob, kv_rows)).astype(BF16)
            o_k[loop, rows] = outs
            for half in range(2):
                expert = 2 * pair + half
                gate = column(gates, expert, route_lane)
                mix[...] += gate * nt(outs[half * own : (half + 1) * own], w_all[expert])
            return none

        lax.fori_loop(0, n_exp // 2, attend, 0)
        for k in range(1, window):

            @pl.when(me + k < n_act)
            def _():
                kv_copy(loop, me + k, k - 1).wait_send()

        centre = state[loop] + mix[...]
        middle[loop] = centre
        unit, _ = normalise(centre)
        second = (unit * gain_two + bias_two).astype(BF16)
        second_k[loop] = second
        rows_all[me] = second

    rows_gather = Gather(rows_all, ag_send, ag_recv, n_act)

    def place_matrices(loop):
        ranks = rowm_ref[loop, :, 0:valid_rows]
        slot = lax.broadcasted_iota(jnp.int32, (cap, valid_rows), 0).astype(F32)
        gather_m[...] = jnp.where(slot == ranks, 1.0, 0.0).astype(BF16)
        slot = lax.broadcasted_iota(jnp.int32, (own, cap), 1).astype(F32)

        def block_matrix(block, none):
            rows = pl.ds(pl.multiple_of(block * own, own), own)
            ranks = meta_ref[loop, rows, RANK_LANE : RANK_LANE + 1]
            scatter_m[rows] = jnp.where(slot == ranks, 1.0, 0.0).astype(BF16)
            return none

        lax.fori_loop(0, n_act, block_matrix, 0)

    def scatter_rows(block):
        return scatter_m[pl.ds(pl.multiple_of(block * own, own), own)]

    def take(buf):
        return nn(gather_m[...], buf[0:n_act].reshape(valid_rows, width))

    def expert_rows(loop, chosen):
        rows_in = take(rows_all).astype(BF16)
        rows_k[cap_rows(loop)] = rows_in
        allowed_lanes = (chosen > 0.5) & (route_cap >= n_exp)
        gate = column(masked_softmax(nt(rows_in, rb[...]), allowed_lanes), n_exp + me, route_cap)
        fgate_k[cap_rows(loop)] = gate
        part_k[cap_rows(loop)] = jnp.zeros((cap, width), F32)

    def chosen_rows(loop):
        return nn(gather_m[...], meta_ref[loop, 0:valid_rows, 0 : 2 * n_exp].astype(BF16))

    root = math.sqrt(2.0 / math.pi)

    def tile_cols(tile):
        return pl.ds(pl.multiple_of(tile * TILE, TILE), TILE)

    def hidden_layer(loop, with_slope):
        rows_in = rows_k[cap_rows(loop)]

        def step(tile, none):
            cols = tile_cols(tile)
            inner = nn(rows_in, up_w[:, cols])
            square = inner * inner
            curve = jnp.tanh(root * inner * (1.0 + 0.044715 * square))
            upper = 0.5 * (1.0 + curve)
            hidden = (inner * upper).astype(BF16)
            hid[cap_rows(loop), cols] = hidden
            if with_slope:
                gprime[cap_rows(loop), cols] = slope_of(inner, square, curve).astype(BF16)
            else:
                up_acc[0:cap, cols] = inner
            part_k[cap_rows(loop)] += nt(hidden, down_w[:, cols])
            return none

        lax.fori_loop(0, tiles, step, 0)

    def slope_of(inner, square, curve):
        return 0.5 * (1.0 + curve) + 0.5 * inner * (1.0 - curve * curve) * (
            root + (3.0 * 0.044715 * root) * square
        )

    def slopes(loop):
        def step(tile, none):
            cols = tile_cols(tile)
            inner = up_acc[0:cap, cols]
            square = inner * inner
            curve = jnp.tanh(root * inner * (1.0 + 0.044715 * square))
            gprime[cap_rows(loop), cols] = slope_of(inner, square, curve).astype(BF16)
            return none

        lax.fori_loop(0, tiles, step, 0)

    sums = Reduce(
        n_act, own, pair_send, pair_recv, far_send, far_recv, rs_sems, total
    )
    sums_two = Reduce(
        n_act,
        own,
        pair_send_two,
        pair_recv_two,
        far_send_two,
        far_recv_two,
        rs_sems_two,
        total_two,
    )
    back_sums = Reduce(
        n_act, own + EXTRA, pair_send, pair_recv, far_send, far_recv, rs_sems, total
    )

    def start_terms(loop, where):
        terms = (part_k[cap_rows(loop)] * fgate_k[cap_rows(loop)]).astype(BF16)
        where.start(lambda block: nn(scatter_rows(block), terms))

    def wait_weights():
        for peer in high_peers():
            up_second(peer, peer).wait_recv()
        for peer in low_peers():
            for block in range(n_high):
                down_second(peer, peer, block).wait_recv()

    def forward(loop, none):
        attention(loop)
        rows_gather.start()
        place_matrices(loop)
        chosen = chosen_rows(loop)

        @pl.when(loop == 0)
        def _():
            wait_weights()

        rows_gather.finish()
        expert_rows(loop, chosen)
        hidden_layer(loop, False)
        start_terms(loop, sums)
        slopes(loop)
        sums.finish()
        running = running_rows(loop)
        state[loop + 1] = jnp.where(running > 0.5, middle[loop] + total[0:own], state[loop])
        prepare(loop + 1)
        return none

    lax.fori_loop(0, last, forward, 0)

    cot = cot_ref[...].astype(F32)

    def chances():
        chance_one = jax.nn.sigmoid(jnp.sum(state[1] * halt, axis=1, keepdims=True))
        chance_two = jax.nn.sigmoid(jnp.sum(state[2] * halt, axis=1, keepdims=True))
        return chance_one, chance_two

    chance_one, chance_two = chances()
    sgrad[last] = ((1.0 - chance_one) * (1.0 - chance_two)) * cot
    rows_two[me] = (sgrad[last] * running_rows(last)).astype(BF16)
    back_gather = Gather(rows_two, bg_send, bg_recv, n_act)
    back_gather.start()
    carry[...] = jnp.zeros_like(carry)

    def finish_output():
        chance_one, chance_two = chances()
        first, next_one = state[1], state[2]
        final = jnp.where(running_rows(last) > 0.5, middle[last] + total_two[0:own], next_one)
        stay = 1.0 - chance_one
        weight_two = stay * chance_two
        weight_three = stay * (1.0 - chance_two)
        out_ref[...] = chance_one * first + weight_two * next_one + weight_three * final
        dot_one = jnp.sum(cot * first, axis=1, keepdims=True)
        dot_two = jnp.sum(cot * next_one, axis=1, keepdims=True)
        dot_three = jnp.sum(cot * final, axis=1, keepdims=True)
        slope_one = (chance_one * stay) * (
            dot_one - chance_two * dot_two - (1.0 - chance_two) * dot_three
        )
        slope_two = (chance_two * (1.0 - chance_two)) * stay * (dot_two - dot_three)
        sgrad[0] = chance_one * cot + slope_one * halt
        sgrad[1] = weight_two * cot + slope_two * halt
        small_acc[vec_at + 4 : vec_at + 5] = jnp.sum(
            slope_one * first + slope_two * next_one, axis=0, keepdims=True
        )

    vec_at = 2 * HD + EXTRA

    def expert_back(loop, grad_rows):
        gate = fgate_k[cap_rows(loop)]
        ggrad[...] = jnp.sum(grad_rows * part_k[cap_rows(loop)], axis=1, keepdims=True)
        scaled = (grad_rows * gate).astype(BF16)
        scaled_k[...] = scaled
        row_grads[...] = jnp.zeros_like(row_grads)

        def step(tile, none):
            cols = tile_cols(tile)
            inner_grad = (
                nn(scaled, down_w[:, cols]) * gprime[cap_rows(loop), cols].astype(F32)
            ).astype(BF16)
            gprime[cap_rows(loop), cols] = inner_grad
            row_grads[...] += nt(inner_grad, up_w[:, cols])
            return none

        lax.fori_loop(0, tiles, step, 0)
        terms = row_grads[...].astype(BF16)
        gate_grad = ggrad[...]
        upper = gate_grad.astype(BF16).astype(F32)
        spread = jnp.where(lane_cap == n_exp + me, upper, 0.0) + jnp.where(
            lane_cap == me, gate_grad - upper, 0.0
        )
        spread_t = jnp.transpose(spread)[0:EXTRA].astype(BF16)

        def row_terms(block):
            matrix = scatter_rows(block)
            grads = nt(spread_t, matrix)
            return jnp.concatenate(
                [
                    nn(matrix, terms),
                    jnp.concatenate([grads, jnp.zeros((EXTRA, width - own), F32)], axis=1),
                ],
                axis=0,
            )

        back_sums.start(row_terms)

    def expert_weights(loop):
        rows_in = rows_k[cap_rows(loop)]
        scaled = scaled_k[...]

        def step(tile, none):
            cols = tile_cols(tile)
            down_acc[:, cols] += tn(scaled, hid[cap_rows(loop), cols])
            up_acc[:, cols] += tn(rows_in, gprime[cap_rows(loop), cols])
            return none

        lax.fori_loop(0, tiles, step, 0)

    def order_at(source, receiver, count):
        return lax.rem(source - receiver + count, count) - 1

    spare = width // shard

    def up_grad_first(peer, slot, block, receiver):
        return remote(
            hid.at[shard_rows(block * n_low + peer)],
            u_first.at[order_at(slot, receiver, n_low), shard_rows(block)],
            ug_send.at[peer, block],
            ug_recv.at[slot, block],
            dp=high * n_low + peer,
        )

    def up_grad_second(peer, slot, receiver):
        return remote(
            hid.at[shard_rows(spare + peer)],
            u_last.at[order_at(slot, receiver, n_high)],
            ug_send_two.at[peer],
            ug_recv_two.at[slot],
            dp=peer * n_low + low,
        )

    def down_grad_first(peer, slot, receiver):
        return remote(
            gprime.at[shard_rows(peer * n_low, n_low)],
            d_first.at[order_at(slot, receiver, n_high)],
            dg_send.at[peer],
            dg_recv.at[slot],
            dp=peer * n_low + low,
        )

    def down_grad_second(peer, slot, receiver):
        return remote(
            gprime.at[shard_rows(spare + peer)],
            d_last.at[order_at(slot, receiver, n_low)],
            dg_send_two.at[peer],
            dg_recv_two.at[slot],
            dp=high * n_low + peer,
        )

    def send_expert_weights():
        hid[0:width] = up_acc[...].astype(BF16)
        for peer in low_peers():
            for block in range(n_high):
                up_grad_first(peer, low, block, peer).start()
        gprime[0:width] = down_acc[...].astype(BF16)
        for peer in high_peers():
            down_grad_first(peer, high, peer).start()

    def pass_expert_weights():
        for peer in low_peers():
            for block in range(n_high):
                up_grad_first(peer, peer, block, low).wait_recv()
        for block in range(n_high):
            added = up_acc[shard_rows(block * n_low + low)]
            for peer in low_peers():
                added = added + u_first[
                    order_at(peer, low, n_low), shard_rows(block)
                ].astype(F32)
            hid[shard_rows(spare + block)] = added.astype(BF16)
        for peer in high_peers():
            up_grad_second(peer, high, peer).start()
        for peer in high_peers():
            down_grad_first(peer, peer, high).wait_recv()
        for block in range(n_low):
            added = down_acc[shard_rows(high * n_low + block)]
            for peer in high_peers():
                added = added + d_first[
                    order_at(peer, high, n_high), shard_rows(block)
                ].astype(F32)
            gprime[shard_rows(spare + block)] = added.astype(BF16)
        for peer in low_peers():
            down_grad_second(peer, low, peer).start()

    def finish_expert_weights():
        added = hid[shard_rows(spare + high)].astype(F32)
        for peer in high_peers():
            up_grad_second(peer, peer, high).wait_recv()
            added = added + u_last[order_at(peer, high, n_high)].astype(F32)
        ugrad_ref[...] = added
        added = gprime[shard_rows(spare + low)].astype(F32)
        for peer in low_peers():
            down_grad_second(peer, peer, low).wait_recv()
            added = added + d_last[order_at(peer, low, n_low)].astype(F32)
        dgrad_ref[...] = added

    attn_sums = Reduce(
        n_exp,
        2 * HD,
        pair_send_two,
        pair_recv_two,
        far_send_two,
        far_recv_two,
        a_sems,
        total_two,
    )

    def dkv_copy(distance, owner):
        return remote(
            dkv_send.at[jnp.clip(owner - win_at, 0, window - 1)],
            dkv_recv.at[distance - 1],
            dk_send.at[distance - 1],
            dk_recv.at[distance - 1],
            expert=owner,
        )

    def attention_back(loop):
        info = meta_ref[loop, own_rows, 0 : 2 * n_exp]
        running = running_rows(loop)
        branch = (sgrad[loop] + carry[...]) * running
        second_grad = total[0:own]
        gate_rows = total[own : own + n_exp, 0:own] + total[own + n_exp : own + 2 * n_exp, 0:own]
        gate_rows = jnp.concatenate(
            [jnp.zeros((n_exp, own), F32), gate_rows, jnp.zeros((LANES - 2 * n_exp, own), F32)],
            axis=0,
        )
        gate_grads = jnp.transpose(gate_rows)[:, 0 : 2 * n_exp]
        second = second_k[loop]
        gates = masked_softmax(nt(second, rb[...]), (info > 0.5) & (route_lane >= n_exp))
        logit_grad = (
            gates * (gate_grads - jnp.sum(gates * gate_grads, axis=1, keepdims=True))
        ).astype(BF16)
        second_grad = second_grad + nn(logit_grad, rb[...])
        unit, inverse = normalise(middle[loop])
        middle_grad = norm_back(second_grad, unit, inverse, gain_two) + branch
        mgrad[...] = middle_grad

        gates = gate_k[loop]
        kv_rows = window_keys(loop)
        dkv_t[...] = jnp.zeros_like(dkv_t)

        def scores_back(pair, none):
            rows = pl.ds(pl.multiple_of(pair * 2 * own, 2 * own), 2 * own)
            out_grads = []
            for half in range(2):
                expert = 2 * pair + half
                part_grad = (column(gates, expert, route_lane) * mgrad[...]).astype(BF16)
                out_grads.append(
                    jnp.where(lane < HD, 0.0, nn(part_grad, w_all[expert])).astype(BF16)
                )
            out_grad = jnp.concatenate(out_grads, axis=0)
            prob_low = p_k[loop, rows]
            prob = prob_low.astype(F32)
            prob_grad = nt(out_grad, kv_rows)
            centre = jnp.sum(prob * prob_grad, axis=1, keepdims=True)
            score_grad = (prob * (prob_grad - centre)).astype(BF16)
            ds_k[rows] = score_grad
            dkv_t[...] += tn(q_k[loop, rows], score_grad) * scale + tn(out_grad, prob_low)
            return none

        lax.fori_loop(0, n_exp // 2, scores_back, 0)
        for block in range(window):
            grads = jnp.transpose(dkv_t[:, block * own : (block + 1) * own])
            dkv[block] = grads
            dkv_send[block] = grads.astype(BF16)
        for distance in range(1, window):

            @pl.when(active & (me >= distance))
            def _():
                dkv_copy(distance, me - distance).start()

        small_acc[2 * HD : vec_at] += tn(logit_grad, second)
        small_acc[vec_at + 2 : vec_at + 3] += jnp.sum(second_grad * unit, axis=0, keepdims=True)
        small_acc[vec_at + 3 : vec_at + 4] += jnp.sum(second_grad, axis=0, keepdims=True)
        normed = normed_k[loop]
        mix[...] = jnp.zeros_like(mix)
        dga[...] = jnp.zeros_like(dga)

        def queries_back(pair, none):
            rows = pl.ds(pl.multiple_of(pair * 2 * own, 2 * own), 2 * own)
            outs = o_k[loop, rows]
            query_grad = jnp.where(lane_two < HD, nn(ds_k[rows], kv_rows) * scale, 0.0).astype(BF16)
            for half in range(2):
                expert = 2 * pair + half
                cut = slice(half * own, (half + 1) * own)
                middle_grad = mgrad[...]
                dot = jnp.sum(middle_grad * nt(outs[cut], w_all[expert]), axis=1, keepdims=True)
                dga[...] += jnp.where(route_lane == expert, dot, 0.0)
                part_grad = (column(gates, expert, route_lane) * middle_grad).astype(BF16)
                attn_acc[expert] += tn(query_grad[cut], normed) + tn(outs[cut], part_grad)
                mix[...] += nt(query_grad[cut], w_all[expert])
            return none

        lax.fori_loop(0, n_exp // 2, queries_back, 0)

        @pl.when(loop == 0)
        def _():
            attn_sums.start(lambda block: attn_acc[block])

        gate_grads = dga[...]
        logit_grad = (
            gates * (gate_grads - jnp.sum(gates * gate_grads, axis=1, keepdims=True))
        ).astype(BF16)
        small_acc[2 * HD : vec_at] += tn(logit_grad, normed)
        normed_grad = mix[...] + nn(logit_grad, rb[...])
        unit, inverse = normalise(state[loop])

        own_block = jnp.clip(me - win_at, 0, window - 1)
        dkv[window] = jnp.where(active, dkv[own_block], 0.0)
        for distance in range(1, window):

            @pl.when(me + distance < n_act)
            def _():
                remote(
                    dkv_send.at[0],
                    dkv_recv.at[distance - 1],
                    dk_send.at[distance - 1],
                    dk_recv.at[distance - 1],
                    expert=me + distance,
                ).wait_recv()
                dkv[window] += dkv_recv[distance - 1].astype(F32)

        for distance in range(1, window):

            @pl.when(active & (me >= distance))
            def _():
                dkv_copy(distance, me - distance).wait_send()

        kv_grad = dkv[window].astype(BF16)
        small_acc[0 : 2 * HD] += tn(kv_grad, normed)
        normed_grad = normed_grad + nt(kv_grad, kvb[...])
        small_acc[vec_at : vec_at + 1] += jnp.sum(normed_grad * unit, axis=0, keepdims=True)
        small_acc[vec_at + 1 : vec_at + 2] += jnp.sum(normed_grad, axis=0, keepdims=True)
        carry[...] = (
            (sgrad[loop] + carry[...]) * (1.0 - running)
            + mgrad[...]
            + norm_back(normed_grad, unit, inverse, gain_one)
        )

    attention(last)
    rows_gather.start()
    up_acc[...] = jnp.zeros_like(up_acc)
    place_matrices(last)
    chosen = chosen_rows(last)
    back_gather.finish()
    grad_rows = take(rows_two)
    rows_gather.finish()
    expert_rows(last, chosen)
    hidden_layer(last, True)
    expert_back(last, grad_rows)
    start_terms(last, sums_two)
    expert_weights(last)
    back_sums.finish()
    attention_back(last)
    sums_two.finish()
    finish_output()

    def backward(step, none):
        loop = last - 1 - step
        branch = (sgrad[loop] + carry[...]) * running_rows(loop)
        rows_all[me] = branch.astype(BF16)
        rows_gather.start()
        place_matrices(loop)
        rows_gather.finish()
        expert_back(loop, take(rows_all))
        expert_weights(loop)

        @pl.when(loop == 0)
        def _():
            send_expert_weights()

        back_sums.finish()
        attention_back(loop)
        return none

    lax.fori_loop(0, last, backward, 0)
    xgrad_ref[...] = carry[...]

    chunk = small_acc.shape[0] // n_exp
    small_sums = Reduce(
        n_exp, chunk, s_pair_send, s_pair_recv, s_far_send, s_far_recv, s_sems, s_total
    )
    small_sums.start(lambda block: small_acc[pl.ds(pl.multiple_of(block * chunk, chunk), chunk)])
    pass_expert_weights()
    attn_sums.finish()
    a_total[...] = jnp.transpose(total_two[...])
    a_stage[...] = a_total[...].astype(BF16)

    def attn_copy(peer, slot):
        return remote(
            a_stage.at[shard_rows(peer)],
            a_recv.at[shard_rows(slot)],
            t_send.at[1, peer],
            t_recv.at[1, slot],
            dp=peer,
        )

    def small_copy(peer, slot):
        return remote(
            s_dp.at[slot], s_dp.at[slot], t_send.at[0, peer], t_recv.at[0, slot], dp=peer
        )

    small_sums.finish()
    s_dp[dp] = s_total[...].astype(BF16)
    each_peer(lambda peer: small_copy(peer, dp).start())
    each_peer(lambda peer: attn_copy(peer, dp).start())
    each_peer(lambda peer: small_copy(peer, peer).wait_recv())
    s_total[...] = jnp.zeros_like(s_total)

    def add_small(index, none):
        s_total[...] += s_dp[index].astype(F32)
        return none

    lax.fori_loop(0, n_dp, add_small, 0)
    s_all[me] = s_total[...]
    small_gather = Gather(s_all, sg_send, sg_recv, n_exp)
    small_gather.start()
    agrad_ref[...] = a_total[shard_rows(dp)]

    def add_attn(peer):
        attn_copy(peer, peer).wait_recv()
        agrad_ref[...] += a_recv[shard_rows(peer)].astype(F32)

    each_peer(add_attn)
    finish_expert_weights()
    small_gather.finish()
    small = s_all[...].reshape(n_exp * chunk, width)
    kvgrad_ref[...] = jnp.transpose(small[0 : 2 * HD])
    rgrad_ref[...] = small[2 * HD : vec_at]
    vgrad_ref[...] = small[vec_at : vec_at + 8]

    def sent(peer):
        attn_weight_copy(peer, dp).wait_send()
        small_copy(peer, dp).wait_send()
        attn_copy(peer, dp).wait_send()

    each_peer(sent)
    for peer in low_peers():
        up_first(peer, low).wait_send()
        down_grad_second(peer, low, peer).wait_send()
        for block in range(n_high):
            down_second(peer, low, block).wait_send()
            up_grad_first(peer, low, block, peer).wait_send()
    for peer in high_peers():
        down_first(peer, high).wait_send()
        up_second(peer, high).wait_send()
        up_grad_second(peer, high, peer).wait_send()
        down_grad_first(peer, high, peer).wait_send()


def adam_kernel(*refs):
    out_in, xgrad_in, ugrad, dgrad, agrad, kvgrad, rgrad, vgrad = refs[:8]
    shared, kv, router, attn, up, down = (refs[8 + 3 * index : 11 + 3 * index] for index in range(6))
    out, xgrad = refs[26:28]
    shared_out, kv_out, router_out, attn_out, up_out, down_out = (
        refs[28:31],
        refs[31:34],
        refs[34:37],
        refs[37:41],
        refs[41:45],
        refs[45:49],
    )

    def update(sources, grad, results, rate, decay):
        values = adam_update(*(source[...] for source in sources), grad, rate, decay)
        for result, value in zip(results, values):
            result[...] = value
        if len(results) > 3:
            results[3][...] = values[0].astype(BF16)

    out[...] = out_in[...]
    xgrad[...] = xgrad_in[...]
    update(up, ugrad[...], up_out, 14.0 / math.sqrt(D), decay_rate)
    update(down, dgrad[...], down_out, 17.0 / math.sqrt(FF), decay_rate)

    @pl.when(pl.program_id(0) == 0)
    def _():
        row = lax.broadcasted_iota(jnp.int32, shared[0].shape, 0)
        rates = jnp.where(row < 4, 6.0, 20.0 / math.sqrt(D))
        update(shared, vgrad[0 : shared[0].shape[0]], shared_out, rates, 0.0)
        update(kv, kvgrad[...], kv_out, 20.0 / math.sqrt(D), decay_rate)
        update(router, rgrad[...], router_out, 50.0 / math.sqrt(3 * D), decay_rate)
        lane = lax.broadcasted_iota(jnp.int32, attn[0].shape, 1)
        rates = jnp.where(lane < HD, 25.0 / math.sqrt(D), 50.0 / math.sqrt(HD))
        update(attn, agrad[...], attn_out, rates, decay_rate)


def dp_grid(n_dp):
    n_low = 1
    while n_low * n_low * 4 <= n_dp:
        n_low *= 2
    return n_low, n_dp // n_low


def per_device(
    block_input,
    cotangent,
    lengths,
    run_loops,
    attn_routes,
    ffn_routes,
    shared_vectors,
    shared_moment,
    shared_second,
    key_value,
    kv_moment,
    kv_second,
    router_weights,
    router_moment,
    router_second,
    attn_weights,
    attn_moment,
    attn_second,
    up_weights,
    up_moment,
    up_second,
    down_weights,
    down_moment,
    down_second,
):
    n_exp = lax.axis_size("expert")
    n_dp = lax.axis_size("dp")
    own, width = block_input.shape
    slots = run_loops.shape[0]
    shard = attn_weights.shape[1]
    hidden = up_weights.shape[2]
    cap = 5 * slots * KFF // (4 * n_exp)
    n_act = FILLED // own
    window = min(n_act, MAXLEN // own + 1)
    pairs = n_exp // 2
    valid_rows = n_act * own
    n_low, n_high = dp_grid(n_dp)

    small_rows = 32 * n_exp
    vmem = pltpu.VMEM
    dma = pltpu.SemaphoreType.DMA
    block = (pairs, own + EXTRA, width)
    small_block = (pairs, 32, width)
    scratch = [
        vmem((LOOPS, slots, INFO), F32),
        vmem((LOOPS + 1, 1, slots), F32),
        vmem((width, 2 * HD), BF16),
        vmem((2 * n_exp, width), BF16),
        vmem((n_exp, width, 2 * HD), BF16),
        vmem((width, hidden), BF16),
        vmem((width, hidden), BF16),
        vmem((width, hidden), F32),
        vmem((width, hidden), F32),
        vmem((n_exp, 2 * HD, width), F32),
        vmem((small_rows, width), F32),
        vmem((LOOPS, own, width), F32),
        vmem((LOOPS, own, width), F32),
        vmem((LOOPS, own, width), BF16),
        vmem((LOOPS, own, width), BF16),
        vmem((LOOPS, n_exp, own, 2 * HD), BF16),
        vmem((LOOPS, n_exp * own, 2 * HD), BF16),
        vmem((LOOPS, n_exp * own, 2 * HD), BF16),
        vmem((LOOPS, n_exp * own, window * own), BF16),
        vmem((n_exp * own, window * own), BF16),
        vmem((own, window * own), F32),
        vmem((own, width), F32),
        vmem((own, 2 * n_exp), F32),
        vmem((2 * HD, window * own), F32),
        vmem((window + 1, own, 2 * HD), F32),
        vmem((LOOPS, own, 2 * n_exp), F32),
        vmem((n_exp, own, width), BF16),
        vmem((n_exp, own, width), BF16),
        vmem((cap, valid_rows), BF16),
        vmem((valid_rows, cap), BF16),
        vmem((LOOPS * cap, width), BF16),
        vmem((LOOPS * cap, hidden), BF16),
        vmem((LOOPS * cap, hidden), BF16),
        vmem((cap, width), F32),
        vmem((LOOPS * cap, width), F32),
        vmem((LOOPS * cap, 1), F32),
        vmem((cap, 1), F32),
        vmem((cap, width), BF16),
        vmem((LOOPS, own, width), F32),
        vmem((own, width), F32),
        vmem((own, width), F32),
        vmem((own + EXTRA, width), F32),
        vmem((own, width), F32),
        vmem(block, BF16),
        vmem(block, BF16),
        vmem(block, BF16),
        vmem(block, BF16),
        vmem((pairs, own, width), BF16),
        vmem((pairs, own, width), BF16),
        vmem((pairs, own, width), BF16),
        vmem((pairs, own, width), BF16),
        vmem((window, own, 2 * HD), BF16),
        vmem((window, own, 2 * HD), BF16),
        vmem((n_low - 1, n_high * shard, hidden), BF16),
        vmem((n_high - 1, shard, hidden), BF16),
        vmem((n_high - 1, n_low * shard, hidden), BF16),
        vmem((n_low - 1, shard, hidden), BF16),
        vmem((width, 2 * HD), F32),
        vmem((width, 2 * HD), BF16),
        vmem((width, 2 * HD), BF16),
        vmem(small_block, BF16),
        vmem(small_block, BF16),
        vmem(small_block, BF16),
        vmem(small_block, BF16),
        vmem((32, width), F32),
        vmem((n_dp, 32, width), BF16),
        vmem((n_exp, 32, width), F32),
        dma((2,)),
        dma((n_dp,)),
        dma((n_dp,)),
        dma((n_low,)),
        dma((n_low,)),
        dma((n_high,)),
        dma((n_high,)),
        dma((n_high,)),
        dma((n_high,)),
        dma((n_low, n_high)),
        dma((n_low, n_high)),
        dma((2 * pairs,)),
        dma((n_exp,)),
        dma((2 * pairs,)),
        dma((n_exp,)),
        dma((2 * pairs,)),
        dma((n_exp,)),
        dma((2 * pairs,)),
        dma((n_exp,)),
        dma((window,)),
        dma((n_exp,)),
        dma((4, pairs)),
        dma((4, pairs)),
        dma((4, pairs)),
        dma((4, pairs)),
        dma((window,)),
        dma((window,)),
        dma((n_low, n_high)),
        dma((n_low, n_high)),
        dma((n_high,)),
        dma((n_high,)),
        dma((n_high,)),
        dma((n_high,)),
        dma((n_low,)),
        dma((n_low,)),
        dma((2, n_dp)),
        dma((2, n_dp)),
    ]
    whole = pl.BlockSpec(memory_space=pltpu.VMEM)
    scalars = pl.BlockSpec(memory_space=pltpu.SMEM)
    outside = pl.BlockSpec(memory_space=pl.ANY)
    shape = jax.ShapeDtypeStruct
    sums = pl.pallas_call(
        functools.partial(block_kernel, n_exp, n_dp, n_act, cap),
        out_shape=(
            shape((own, width), F32),
            shape((own, width), F32),
            shape((shard, hidden), F32),
            shape((shard, hidden), F32),
            shape((shard, 2 * HD), F32),
            shape((width, 2 * HD), F32),
            shape((2 * n_exp, width), F32),
            shape((8, width), F32),
        ),
        in_specs=[whole, whole, scalars, *([whole] * 7), outside, outside],
        out_specs=[whole] * 8,
        scratch_shapes=scratch,
        compiler_params=pltpu.CompilerParams(
            collective_id=0, has_side_effects=True, vmem_limit_bytes=63 * 1024 * 1024
        ),
        name="block",
    )(
        block_input,
        cotangent,
        lengths,
        run_loops[None],
        attn_routes.transpose(0, 2, 1),
        ffn_routes.transpose(0, 2, 1),
        shared_vectors,
        key_value,
        router_weights.T,
        attn_weights[0],
        up_weights[0],
        down_weights[0],
    )

    steps = max(1, shard // 16)
    rows = shard // steps

    def by_rows(array):
        return pl.BlockSpec((array.shape[0] // steps, array.shape[1]), lambda step: (step, 0))

    def fixed(array):
        return pl.BlockSpec(array.shape, lambda step: (0, 0))

    output, input_grad, up_sum, down_sum, *small = sums
    small_args = [
        shared_vectors,
        shared_moment,
        shared_second,
        key_value,
        kv_moment,
        kv_second,
        router_weights.T,
        router_moment.T,
        router_second.T,
        attn_weights[0],
        attn_moment[0],
        attn_second[0],
    ]
    large_args = [
        up_weights[0],
        up_moment[0],
        up_second[0],
        down_weights[0],
        down_moment[0],
        down_second[0],
    ]
    attn_low = shape((shard, 2 * HD), BF16)
    large_low = shape((shard, hidden), BF16)
    like = [shape(array.shape, array.dtype) for array in small_args]
    big = [shape(array.shape, array.dtype) for array in large_args]
    outs = [
        shape(output.shape, F32),
        shape(input_grad.shape, F32),
        *like,
        attn_low,
        *big[:3],
        large_low,
        *big[3:],
        large_low,
    ]
    results = pl.pallas_call(
        adam_kernel,
        grid=(steps,),
        out_shape=outs,
        in_specs=[
            by_rows(output),
            by_rows(input_grad),
            by_rows(up_sum),
            by_rows(down_sum),
            *(fixed(array) for array in small),
            *(fixed(array) for array in small_args),
            *(by_rows(array) for array in large_args),
        ],
        out_specs=[
            by_rows(output),
            by_rows(input_grad),
            *(fixed(array) for array in (*like, attn_low)),
            *(by_rows(array) for array in (*big[:3], large_low, *big[3:], large_low)),
        ],
        name="adamw",
    )(*sums, *small_args, *large_args)
    output, input_grad, *rest = results
    shared_kv, router, weights = rest[:6], rest[6:9], rest[9:]
    return (
        output,
        input_grad,
        *shared_kv,
        *(array.T for array in router),
        *(array[None] for array in weights),
    )


def solution(mesh):
    rows = P(("dp", "expert"), None)
    weights = P("expert", "dp", None)
    return jax.shard_map(
        per_device,
        mesh=mesh,
        in_specs=(
            rows,
            rows,
            P("dp", None),
            P("dp"),
            P(None, "dp", None),
            P(None, "dp", None),
            *([P()] * 9),
            *([weights] * 9),
        ),
        out_specs=(rows, rows, *([P()] * 9), *([weights] * 12)),
        check_vma=False,
    )
```

```python
import functools
import math

import jax
import jax.numpy as jnp
from jax import lax
from jax.experimental import pallas as pl
from jax.experimental.pallas import tpu as pltpu
from jax.sharding import PartitionSpec as P

D = 512
HD = 64
FF = 2048
KATT = 4
KFF = 2
LOOPS = 3
STEP = 10
MAXLEN = 512
FILLED = 896

ln_eps = 1e-05
beta_one = 0.9
beta_two = 0.999
adam_eps = 1e-08
decay_rate = 0.01
masked_score = -1e30

F32 = jnp.float32
BF16 = jnp.bfloat16
MESH = pl.DeviceIdType.MESH
LANES = 128
RANK_LANE = 16
RUN_LANE = 17
SEG_LANE = 18
INFO = 32
TILE = 512
EXTRA = 16


def nn(left, right):
    return lax.dot_general(left, right, (((1,), (0,)), ((), ())), preferred_element_type=F32)


def nt(left, right):
    return lax.dot_general(left, right, (((1,), (1,)), ((), ())), preferred_element_type=F32)


def tn(left, right):
    return lax.dot_general(left, right, (((0,), (0,)), ((), ())), preferred_element_type=F32)


def normalise(values):
    centre = values - jnp.mean(values, axis=-1, keepdims=True)
    inverse = lax.rsqrt(jnp.mean(centre * centre, axis=-1, keepdims=True) + ln_eps)
    return centre * inverse, inverse


def norm_back(grad, unit, inverse, gain):
    scaled = grad * gain
    first = jnp.mean(scaled, axis=-1, keepdims=True)
    second = jnp.mean(scaled * unit, axis=-1, keepdims=True)
    return inverse * (scaled - first - unit * second)


def masked_softmax(logits, valid):
    top = jnp.max(jnp.where(valid, logits, masked_score), axis=-1, keepdims=True)
    powers = jnp.where(valid, jnp.exp(jnp.where(valid, logits - top, 0.0)), 0.0)
    return powers / jnp.maximum(jnp.sum(powers, axis=-1, keepdims=True), 0.5)


def adam_update(weight, moment, second, grad, rate, decay):
    moment_new = beta_one * moment + (1.0 - beta_one) * grad
    second_new = beta_two * second + (1.0 - beta_two) * grad * grad
    moment_hat = moment_new * (1.0 / (1.0 - beta_one**STEP))
    second_hat = second_new * (1.0 / (1.0 - beta_two**STEP))
    weight_new = weight - rate * (moment_hat / (jnp.sqrt(second_hat) + adam_eps) + decay * weight)
    return (weight_new, moment_new, second_new)


def block_kernel(
    n_exp,
    n_dp,
    n_act,
    cap,
    x_ref,
    cot_ref,
    len_ref,
    run_ref,
    ar_ref,
    fr_ref,
    vec_ref,
    kvw_ref,
    rw_ref,
    aw_ref,
    uw_hbm,
    dw_hbm,
    out_ref,
    xgrad_ref,
    ugrad_ref,
    dgrad_ref,
    agrad_ref,
    kvgrad_ref,
    rgrad_ref,
    vgrad_ref,
    meta_ref,
    rowm_ref,
    kvb,
    rb,
    w_all,
    up_w,
    down_w,
    up_acc,
    down_acc,
    attn_acc,
    small_acc,
    state,
    middle,
    normed_k,
    second_k,
    kv_k,
    q_k,
    o_k,
    p_k,
    ds_k,
    bias,
    mix,
    dga,
    dkv_t,
    dkv,
    gate_k,
    rows_all,
    rows_two,
    wrow,
    gather_m,
    scatter_m,
    rows_k,
    hid,
    gprime,
    row_grads,
    part_k,
    fgate_k,
    ggrad,
    scaled_k,
    sgrad,
    carry,
    mgrad,
    total,
    total_two,
    pair_send,
    pair_recv,
    far_send,
    far_recv,
    pair_send_two,
    pair_recv_two,
    far_send_two,
    far_recv_two,
    dkv_send,
    dkv_recv,
    u_first,
    u_last,
    d_first,
    d_last,
    a_total,
    a_stage,
    a_recv,
    s_pair_send,
    s_pair_recv,
    s_far_send,
    s_far_recv,
    s_total,
    s_dp,
    s_all,
    in_sems,
    w_send,
    w_recv,
    uw_send,
    uw_recv,
    uw_send_two,
    dw_send,
    dw_recv,
    dw_send_two,
    ag_send,
    ag_recv,
    bg_send,
    bg_recv,
    fg_send,
    fg_recv,
    wg_send,
    wg_recv,
    sg_send,
    sg_recv,
    kg_send,
    kg_recv,
    rs_sems,
    rs_sems_two,
    s_sems,
    a_sems,
    dk_send,
    dk_recv,
    ug_send,
    ug_recv,
    ug_send_two,
    ug_recv_two,
    dg_send,
    dg_recv,
    dg_send_two,
    dg_recv_two,
    t_send,
    t_recv,
):
    me = lax.axis_index("expert")
    dp = lax.axis_index("dp")
    pairs = n_exp // 2
    core = lax.rem(me, 2)
    chip = lax.div(me, 2)
    sibling = 2 * chip + 1 - core
    n_low, n_high = dp_grid(n_dp)
    high = lax.div(dp, n_low)
    low = lax.rem(dp, n_low)
    own = x_ref.shape[0]
    width = x_ref.shape[1]
    slots = run_ref.shape[1]
    shard = aw_ref.shape[0]
    hidden_units = up_w.shape[1]
    tiles = hidden_units // TILE
    valid_rows = n_act * own
    window = min(n_act, MAXLEN // own + 1)
    keys = window * own
    win_at = jnp.clip(me - (window - 1), 0, n_act - window)
    scale = HD ** (-0.5)
    active = me < n_act
    last = LOOPS - 1

    def remote(src, dst, send, recv, **where):
        return pltpu.make_async_remote_copy(
            src_ref=src,
            dst_ref=dst,
            send_sem=send,
            recv_sem=recv,
            device_id=where,
            device_id_type=MESH,
        )

    def shard_rows(index, count=1):
        return pl.ds(pl.multiple_of(index * shard, shard), count * shard)

    def each_peer(body):
        def step(k, none):
            body(lax.rem(dp + k, n_dp))
            return none

        lax.fori_loop(1, n_dp, step, 0)

    def high_peers():
        return [lax.rem(high + k, n_high) for k in range(1, n_high)]

    def low_peers():
        return [lax.rem(low + k, n_low) for k in range(1, n_low)]

    class Gather:
        def __init__(self, buf, send, recv, count):
            self.buf, self.sent, self.got, self.count = buf, send, recv, count

        def copy(self, block, sem, where):
            ref = self.buf.at[block]
            return remote(ref, ref, self.sent.at[sem], self.got.at[block], expert=where)

        def start(self):
            for k in range(1, pairs):
                self.send(k)
            self.send(0)

        def send(self, k):
            zz = lax.rem(chip + k, pairs)

            @pl.when(me < self.count)
            def _():
                self.copy(me, zz, 2 * zz + core if k else sibling).start()

        def finish(self):
            for k in range(pairs - 1, 0, -1):
                zz = lax.rem(chip + k, pairs)
                src = 2 * zz + core

                @pl.when(src < self.count)
                def _():
                    self.copy(src, zz, src).wait_recv()
                    self.copy(src, pairs + zz, sibling).start()

            for k in range(pairs):
                zz = lax.rem(chip + k, pairs)
                src = 2 * zz + 1 - core

                @pl.when(src < self.count)
                def _():
                    self.copy(src, zz, sibling).wait_recv()

            @pl.when(me < self.count)
            def _():
                for k in range(1, pairs):
                    zz = lax.rem(chip + k, pairs)
                    self.copy(me, zz, 2 * zz + core).wait_send()
                self.copy(me, chip, sibling).wait_send()

            for k in range(1, pairs):
                zz = lax.rem(chip + k, pairs)
                src = 2 * zz + core

                @pl.when(src < self.count)
                def _():
                    self.copy(src, pairs + zz, sibling).wait_send()

    class Reduce:
        def __init__(self, count, rows, psend, precv, fsend, frecv, sems, result):
            self.count, self.rows, self.part = count, rows, pl.ds(0, rows)
            self.psend, self.precv, self.fsend, self.frecv = psend, precv, fsend, frecv
            self.sems, self.result = sems, result

        def pair_copy(self, zz):
            return remote(
                self.psend.at[zz, self.part],
                self.precv.at[zz, self.part],
                self.sems.at[0, zz],
                self.sems.at[1, zz],
                expert=sibling,
            )

        def far_copy(self, zz, slot):
            return remote(
                self.fsend.at[zz, self.part],
                self.frecv.at[slot, self.part],
                self.sems.at[2, zz],
                self.sems.at[3, slot],
                expert=2 * zz + core,
            )

        def start(self, make, send=True):
            for k in range(pairs):
                zz = lax.rem(chip + 1 + k, pairs)
                block = 2 * zz + 1 - core

                @pl.when(block < self.count)
                def _():
                    self.psend[zz, self.part] = make(block).astype(BF16)
                    self.pair_copy(zz).start()

            for k in range(1, pairs):
                zz = lax.rem(chip + k, pairs)
                block = 2 * zz + core

                @pl.when(block < self.count)
                def _():
                    mine = make(block)
                    self.pair_copy(zz).wait_recv()
                    self.fsend[zz, self.part] = (
                        mine + self.precv[zz, self.part].astype(F32)
                    ).astype(BF16)
                    if send:
                        self.far_copy(zz, chip).start()

            @pl.when(me < self.count)
            def _():
                mine = make(me)
                self.pair_copy(chip).wait_recv()
                self.result[self.part] = mine + self.precv[chip, self.part].astype(F32)

            @pl.when(me >= self.count)
            def _():
                self.result[self.part] = jnp.zeros((self.rows, self.result.shape[1]), F32)

        def send(self, k):
            zz = lax.rem(chip + k, pairs)

            @pl.when(2 * zz + core < self.count)
            def _():
                self.far_copy(zz, chip).start()

        def finish(self):
            @pl.when(me < self.count)
            def _():
                for k in range(1, pairs):
                    zz = lax.rem(chip + k, pairs)
                    self.far_copy(zz, zz).wait_recv()
                    self.result[self.part] += self.frecv[zz, self.part].astype(F32)

            for k in range(pairs):
                zz = lax.rem(chip + 1 + k, pairs)

                @pl.when(2 * zz + 1 - core < self.count)
                def _():
                    self.pair_copy(zz).wait_send()

            for k in range(1, pairs):
                zz = lax.rem(chip + k, pairs)

                @pl.when(2 * zz + core < self.count)
                def _():
                    self.far_copy(zz, chip).wait_send()

    def attn_weight_copy(peer, slot):
        ref = w_all.at[me, shard_rows(slot)]
        return remote(ref, ref, w_send.at[peer], w_recv.at[slot], dp=peer)

    def up_low(peer, block):
        ref = up_w.at[shard_rows(high * n_low + block)]
        return remote(
            ref,
            ref,
            uw_send.at[peer],
            uw_recv.at[high * n_low + block],
            dp=high * n_low + peer,
        )

    def up_high(peer, row, block):
        ref = up_w.at[shard_rows(row * n_low + block)]
        return remote(
            ref,
            ref,
            uw_send_two.at[peer, block],
            uw_recv.at[row * n_low + block],
            dp=peer * n_low + low,
        )

    def down_high(peer, block):
        ref = down_w.at[shard_rows(block * n_low + low)]
        return remote(
            ref,
            ref,
            dw_send.at[peer],
            dw_recv.at[block * n_low + low],
            dp=peer * n_low + low,
        )

    def down_low(peer, column_at, block):
        ref = down_w.at[shard_rows(block * n_low + column_at)]
        return remote(
            ref,
            ref,
            dw_send_two.at[peer, block],
            dw_recv.at[block * n_low + column_at],
            dp=high * n_low + peer,
        )

    up_in = pltpu.make_async_copy(uw_hbm, ugrad_ref, in_sems.at[0])
    down_in = pltpu.make_async_copy(dw_hbm, dgrad_ref, in_sems.at[1])
    up_in.start()
    down_in.start()
    kv_k[...] = jnp.zeros_like(kv_k)
    barrier = pltpu.get_barrier_semaphore()
    for k in range(1, n_exp):
        pl.semaphore_signal(
            barrier, inc=1, device_id={"expert": lax.rem(me + k, n_exp)}, device_id_type=MESH
        )
    for k in range(1, n_dp):
        pl.semaphore_signal(
            barrier, inc=1, device_id={"dp": lax.rem(dp + k, n_dp)}, device_id_type=MESH
        )
    rows_two[me] = cot_ref[...]
    wrow[...] = jnp.zeros_like(wrow)
    w_all[me, shard_rows(dp)] = aw_ref[...].astype(BF16)
    up_in.wait()
    up_w[shard_rows(dp)] = ugrad_ref[...].astype(BF16)
    down_in.wait()
    down_w[shard_rows(dp)] = dgrad_ref[...].astype(BF16)
    pl.semaphore_wait(barrier, n_exp + n_dp - 2)
    each_peer(lambda peer: attn_weight_copy(peer, dp).start())
    cot_gather = Gather(rows_two, bg_send, bg_recv, n_act)
    cot_gather.send(2)
    for peer in low_peers():
        up_low(peer, low).start()
    for peer in high_peers():
        down_high(peer, high).start()
    for peer in high_peers():
        up_high(peer, high, low).start()
    for peer in low_peers():
        down_low(peer, low, high).start()

    kvb[...] = kvw_ref[...].astype(BF16)
    rb[...] = rw_ref[...].astype(BF16)
    gain_one = vec_ref[0:1, :]
    bias_one = vec_ref[1:2, :]
    gain_two = vec_ref[2:3, :]
    bias_two = vec_ref[3:4, :]
    halt = vec_ref[4:5, :]
    state[0] = x_ref[...].astype(F32)
    own_rows = pl.ds(pl.multiple_of(me * own, own), own)

    lane = lax.broadcasted_iota(jnp.int32, (own, LANES), 1)
    route_lane = lax.broadcasted_iota(jnp.int32, (own, 2 * n_exp), 1)
    lane_two = lax.broadcasted_iota(jnp.int32, (2 * own, LANES), 1)
    lane_cap = lax.broadcasted_iota(jnp.int32, (cap, LANES), 1)
    route_cap = lax.broadcasted_iota(jnp.int32, (cap, 2 * n_exp), 1)

    def column(values, index, lanes):
        return jnp.sum(jnp.where(lanes == index, values, 0.0), axis=1, keepdims=True)

    def cap_rows(loop):
        return pl.ds(pl.multiple_of(loop * cap, cap), cap)

    def window_keys(loop):
        return kv_k[loop, pl.ds(win_at, window)].reshape(keys, 2 * HD)

    def routing():
        position = lax.broadcasted_iota(jnp.int32, (1, slots), 1)
        bound = 0
        segment = jnp.zeros((1, slots), F32)
        for index in range(len_ref.shape[1]):
            bound = bound + len_ref[0, index]
            segment = segment + jnp.where(position >= bound, 1.0, 0.0)
        sub = lax.broadcasted_iota(jnp.int32, (n_exp, slots), 0)
        position_all = lax.broadcasted_iota(jnp.int32, (n_exp, slots), 1)
        valid = segment < len_ref.shape[1] - 0.5
        rowm_ref[LOOPS] = segment
        picks, selected = [], jnp.zeros((n_exp, slots), F32)
        for loop in range(LOOPS):
            running = jnp.where(valid & (run_ref[...] > loop), 1.0, 0.0)
            att = jnp.zeros((n_exp, slots), F32)
            for k in range(ar_ref.shape[1]):
                att = att + jnp.where(ar_ref[loop, k : k + 1, :] == sub, 1.0, 0.0)
            ffn = jnp.zeros((n_exp, slots), F32)
            mine = jnp.zeros((1, slots), F32)
            for k in range(fr_ref.shape[1]):
                ffn = ffn + jnp.where(fr_ref[loop, k : k + 1, :] == sub, 1.0, 0.0)
                mine = mine + jnp.where(fr_ref[loop, k : k + 1, :] == me, running, 0.0)
            picks.append((att, ffn, running))
            selected = selected + jnp.where(sub == loop, mine, 0.0)
        ranks = selected
        shift = 1
        while shift < slots:
            moved = pltpu.roll(ranks, shift, 1)
            ranks = ranks + jnp.where(position_all >= shift, moved, 0.0)
            shift *= 2
        ranks = jnp.where(selected > 0.5, ranks - 1.0, -1.0)
        for loop in range(LOOPS):
            att, ffn, running = picks[loop]
            rank = ranks[loop : loop + 1]
            rowm_ref[loop] = rank
            rest = jnp.where(
                sub == 0,
                rank,
                jnp.where(sub == 1, running, jnp.where(sub == 2, segment, 0.0)),
            )
            spare = jnp.zeros((INFO - 3 * n_exp, slots), F32)
            meta_ref[loop] = jnp.transpose(jnp.concatenate([att, ffn, rest, spare], axis=0))

    def kv_copy(loop, where, sem):
        ref = kv_k.at[loop, me]
        return remote(ref, ref, kg_send.at[sem], kg_recv.at[me], expert=where)

    def prepare(loop):
        unit, _ = normalise(state[loop])
        normed = (unit * gain_one + bias_one).astype(BF16)
        normed_k[loop] = normed
        kv_k[loop, me] = nn(normed, kvb[...]).astype(BF16)
        for k in range(1, window):

            @pl.when(me + k < n_act)
            def _():
                kv_copy(loop, me + k, k - 1).start()

        info = meta_ref[loop, own_rows, 0 : 2 * n_exp]
        gate_k[loop] = masked_softmax(
            nt(normed, rb[...]), (info > 0.5) & (route_lane < n_exp)
        )

    def running_rows(loop):
        return meta_ref[loop, own_rows, RUN_LANE : RUN_LANE + 1]

    each_peer(lambda peer: attn_weight_copy(peer, peer).wait_recv())
    weights_gather = Gather(w_all, wg_send, wg_recv, n_exp)
    weights_gather.start()
    routing()
    prepare(0)
    seg_own = meta_ref[0, own_rows, SEG_LANE : SEG_LANE + 1]
    key_cols = pl.ds(pl.multiple_of(win_at * own, own), keys)
    seg_keys = rowm_ref[LOOPS, :, key_cols]
    row_at = me * own + lax.broadcasted_iota(jnp.int32, (own, keys), 0)
    key_at = win_at * own + lax.broadcasted_iota(jnp.int32, (own, keys), 1)
    allowed = (seg_own == seg_keys) & (key_at <= row_at)
    bias[...] = jnp.where(allowed, 0.0, masked_score)
    down_acc[...] = jnp.zeros_like(down_acc)
    attn_acc[...] = jnp.zeros_like(attn_acc)
    small_acc[...] = jnp.zeros_like(small_acc)
    weights_gather.finish()
    for block in low_peers():
        up_low(block, block).wait_recv()
        for peer in high_peers():
            up_high(peer, high, block).start()
    for block in high_peers():
        down_high(block, block).wait_recv()
        for peer in low_peers():
            down_low(peer, low, block).start()

    def attention(loop):
        normed = normed_k[loop]

        def queries(expert, none):
            query = jnp.where(lane < HD, nn(normed, w_all[expert]), 0.0).astype(BF16)
            q_k[loop, pl.ds(pl.multiple_of(expert * own, own), own)] = query
            return none

        lax.fori_loop(0, n_exp, queries, 0, unroll=True)
        running = running_rows(loop)
        gates = gate_k[loop] * running
        mix[...] = jnp.zeros_like(mix)
        for k in range(1, window):

            @pl.when(active & (me >= k))
            def _():
                ref = kv_k.at[loop, me - k]
                remote(
                    ref, ref, kg_send.at[k - 1], kg_recv.at[me - k], expert=me - k
                ).wait_recv()

        kv_rows = window_keys(loop)

        def attend(pair, none):
            rows = pl.ds(pl.multiple_of(pair * 2 * own, 2 * own), 2 * own)
            scores = nt(q_k[loop, rows], kv_rows) * scale
            scores = (scores.reshape(2, own, keys) + bias[...][None]).reshape(2 * own, keys)
            powers = jnp.exp(scores - jnp.max(scores, axis=1, keepdims=True))
            prob = (powers * (1.0 / jnp.sum(powers, axis=1, keepdims=True))).astype(BF16)
            p_k[loop, rows] = prob
            outs = jnp.where(lane_two < HD, 0.0, nn(prob, kv_rows)).astype(BF16)
            o_k[loop, rows] = outs
            for half in range(2):
                expert = 2 * pair + half
                gate = column(gates, expert, route_lane)
                mix[...] += gate * nt(outs[half * own : (half + 1) * own], w_all[expert])
            return none

        lax.fori_loop(0, n_exp // 2, attend, 0, unroll=True)
        for k in range(1, window):

            @pl.when(me + k < n_act)
            def _():
                kv_copy(loop, me + k, k - 1).wait_send()

        centre = state[loop] + mix[...]
        middle[loop] = centre
        unit, _ = normalise(centre)
        second = (unit * gain_two + bias_two).astype(BF16)
        second_k[loop] = second
        rows_all[me] = second

    rows_gather = Gather(rows_all, ag_send, ag_recv, n_act)
    factor_gather = Gather(wrow, fg_send, fg_recv, n_act)

    def place_matrices(loop):
        ranks = rowm_ref[loop, :, 0:valid_rows]
        slot = lax.broadcasted_iota(jnp.int32, (cap, valid_rows), 0).astype(F32)
        gather_m[...] = jnp.where(slot == ranks, 1.0, 0.0).astype(BF16)
        slot = lax.broadcasted_iota(jnp.int32, (own, cap), 1).astype(F32)

        def block_matrix(block, none):
            rows = pl.ds(pl.multiple_of(block * own, own), own)
            ranks = meta_ref[loop, rows, RANK_LANE : RANK_LANE + 1]
            scatter_m[rows] = jnp.where(slot == ranks, 1.0, 0.0).astype(BF16)
            return none

        lax.fori_loop(0, n_act, block_matrix, 0)

    def scatter_rows(block):
        return scatter_m[pl.ds(pl.multiple_of(block * own, own), own)]

    def take(buf):
        return nn(gather_m[...], buf[0:n_act].reshape(valid_rows, width))

    def expert_rows(loop, chosen):
        rows_in = take(rows_all).astype(BF16)
        rows_k[cap_rows(loop)] = rows_in
        allowed_lanes = (chosen > 0.5) & (route_cap >= n_exp)
        gate = column(masked_softmax(nt(rows_in, rb[...]), allowed_lanes), n_exp + me, route_cap)
        fgate_k[cap_rows(loop)] = gate
        part_k[cap_rows(loop)] = jnp.zeros((cap, width), F32)

    def chosen_rows(loop):
        return nn(gather_m[...], meta_ref[loop, 0:valid_rows, 0 : 2 * n_exp].astype(BF16))

    root = math.sqrt(2.0 / math.pi)

    def tile_cols(tile):
        return pl.ds(pl.multiple_of(tile * TILE, TILE), TILE)

    def hidden_layer(loop, with_slope):
        rows_in = rows_k[cap_rows(loop)]

        def step(tile, none):
            cols = tile_cols(tile)
            inner = nn(rows_in, up_w[:, cols])
            square = inner * inner
            curve = jnp.tanh(root * inner * (1.0 + 0.044715 * square))
            upper = 0.5 * (1.0 + curve)
            hidden = (inner * upper).astype(BF16)
            hid[cap_rows(loop), cols] = hidden
            if with_slope:
                gprime[cap_rows(loop), cols] = slope_of(inner, square, curve).astype(BF16)
            else:
                up_acc[0:cap, cols] = inner
            part_k[cap_rows(loop)] += nt(hidden, down_w[:, cols])
            return none

        lax.fori_loop(0, tiles, step, 0, unroll=True)

    def slope_of(inner, square, curve):
        return 0.5 * (1.0 + curve) + 0.5 * inner * (1.0 - curve * curve) * (
            root + (3.0 * 0.044715 * root) * square
        )

    def slopes(loop):
        def step(tile, none):
            cols = tile_cols(tile)
            inner = up_acc[0:cap, cols]
            square = inner * inner
            curve = jnp.tanh(root * inner * (1.0 + 0.044715 * square))
            gprime[cap_rows(loop), cols] = slope_of(inner, square, curve).astype(BF16)
            return none

        lax.fori_loop(0, tiles, step, 0, unroll=True)

    sums = Reduce(
        n_act, own, pair_send, pair_recv, far_send, far_recv, rs_sems, total
    )
    sums_two = Reduce(
        n_act,
        own,
        pair_send_two,
        pair_recv_two,
        far_send_two,
        far_recv_two,
        rs_sems_two,
        total_two,
    )
    back_sums = Reduce(
        n_act, own + EXTRA, pair_send, pair_recv, far_send, far_recv, rs_sems, total
    )

    def start_terms(loop, where, send=True):
        terms = (part_k[cap_rows(loop)] * fgate_k[cap_rows(loop)]).astype(BF16)
        where.start(lambda block: nn(scatter_rows(block), terms), send)

    def wait_weights():
        for peer in high_peers():
            for block in range(n_low):
                up_high(peer, peer, block).wait_recv()
        for peer in low_peers():
            for block in range(n_high):
                down_low(peer, peer, block).wait_recv()

    def forward(loop, none):
        attention(loop)
        rows_gather.start()
        place_matrices(loop)
        chosen = chosen_rows(loop)

        @pl.when(loop == 0)
        def _():
            wait_weights()

        rows_gather.finish()

        @pl.when(loop == 0)
        def _():
            cot_gather.send(0)
            cot_gather.send(1)

        @pl.when(loop == 1)
        def _():
            cot_gather.send(3)

        expert_rows(loop, chosen)
        hidden_layer(loop, False)
        start_terms(loop, sums)
        slopes(loop)
        sums.finish()
        running = running_rows(loop)
        state[loop + 1] = jnp.where(running > 0.5, middle[loop] + total[0:own], state[loop])
        prepare(loop + 1)
        return none

    lax.fori_loop(0, last, forward, 0)

    cot = cot_ref[...].astype(F32)

    def chances():
        chance_one = jax.nn.sigmoid(jnp.sum(state[1] * halt, axis=1, keepdims=True))
        chance_two = jax.nn.sigmoid(jnp.sum(state[2] * halt, axis=1, keepdims=True))
        return chance_one, chance_two

    chance_one, chance_two = chances()
    weight_last = (1.0 - chance_one) * (1.0 - chance_two)
    sgrad[last] = weight_last * cot
    upper = weight_last.astype(BF16).astype(F32)
    factors = jnp.where(lane == 0, upper, jnp.where(lane == 1, weight_last - upper, 0.0))
    wrow[me] = jnp.transpose(factors)[0:EXTRA].astype(BF16)
    factor_gather.start()
    carry[...] = jnp.zeros_like(carry)

    def state_grads(loop_dot):
        chance_one, chance_two = chances()
        first, next_one = state[1], state[2]
        stay = 1.0 - chance_one
        weight_two = stay * chance_two
        weight_three = stay * (1.0 - chance_two)
        dot_one = jnp.sum(cot * first, axis=1, keepdims=True)
        dot_two = jnp.sum(cot * next_one, axis=1, keepdims=True)
        dot_middle = jnp.sum(cot * middle[last], axis=1, keepdims=True)
        dot_three = jnp.where(
            running_rows(last) > 0.5, weight_three * dot_middle + loop_dot, weight_three * dot_two
        )
        slope_one = chance_one * (stay * dot_one - weight_two * dot_two - dot_three)
        slope_two = chance_two * (weight_three * dot_two - dot_three)
        sgrad[0] = chance_one * cot + slope_one * halt
        sgrad[1] = weight_two * cot + slope_two * halt
        small_acc[vec_at + 4 : vec_at + 5] = jnp.sum(
            slope_one * first + slope_two * next_one, axis=0, keepdims=True
        )

    def finish_output():
        chance_one, chance_two = chances()
        first, next_one = state[1], state[2]
        final = jnp.where(running_rows(last) > 0.5, middle[last] + total_two[0:own], next_one)
        stay = 1.0 - chance_one
        out_ref[...] = (
            chance_one * first + stay * chance_two * next_one + stay * (1.0 - chance_two) * final
        )

    vec_at = 2 * HD + EXTRA

    def expert_back(loop, grad_rows):
        gate = fgate_k[cap_rows(loop)]
        ggrad[...] = jnp.sum(grad_rows * part_k[cap_rows(loop)], axis=1, keepdims=True)
        scaled = (grad_rows * gate).astype(BF16)
        scaled_k[...] = scaled
        row_grads[...] = jnp.zeros_like(row_grads)

        def step(tile, none):
            cols = tile_cols(tile)
            inner_grad = (
                nn(scaled, down_w[:, cols]) * gprime[cap_rows(loop), cols].astype(F32)
            ).astype(BF16)
            gprime[cap_rows(loop), cols] = inner_grad
            row_grads[...] += nt(inner_grad, up_w[:, cols])
            return none

        lax.fori_loop(0, tiles, step, 0, unroll=True)
        terms = row_grads[...].astype(BF16)
        gate_grad = ggrad[...]
        upper = gate_grad.astype(BF16).astype(F32)
        spread = jnp.where(lane_cap == n_exp + me, upper, 0.0) + jnp.where(
            lane_cap == me, gate_grad - upper, 0.0
        )
        spread_t = jnp.transpose(spread)[0:EXTRA].astype(BF16)

        def row_terms(block):
            matrix = scatter_rows(block)
            grads = nt(spread_t, matrix)
            return jnp.concatenate(
                [
                    nn(matrix, terms),
                    jnp.concatenate([grads, jnp.zeros((EXTRA, width - own), F32)], axis=1),
                ],
                axis=0,
            )

        back_sums.start(row_terms)

    def expert_weights(loop):
        rows_in = rows_k[cap_rows(loop)]
        scaled = scaled_k[...]

        def step(tile, none):
            cols = tile_cols(tile)
            down_acc[:, cols] += tn(scaled, hid[cap_rows(loop), cols])
            up_acc[:, cols] += tn(rows_in, gprime[cap_rows(loop), cols])
            return none

        lax.fori_loop(0, tiles, step, 0, unroll=True)

    def order_at(source, receiver, count):
        return lax.rem(source - receiver + count, count) - 1

    spare = width // shard

    def up_grad_first(peer, slot, block, receiver):
        return remote(
            hid.at[shard_rows(block * n_low + peer)],
            u_first.at[order_at(slot, receiver, n_low), shard_rows(block)],
            ug_send.at[peer, block],
            ug_recv.at[slot, block],
            dp=high * n_low + peer,
        )

    def up_grad_second(peer, slot, receiver):
        return remote(
            hid.at[shard_rows(spare + peer)],
            u_last.at[order_at(slot, receiver, n_high)],
            ug_send_two.at[peer],
            ug_recv_two.at[slot],
            dp=peer * n_low + low,
        )

    def down_grad_first(peer, slot, receiver):
        return remote(
            gprime.at[shard_rows(peer * n_low, n_low)],
            d_first.at[order_at(slot, receiver, n_high)],
            dg_send.at[peer],
            dg_recv.at[slot],
            dp=peer * n_low + low,
        )

    def down_grad_second(peer, slot, receiver):
        return remote(
            gprime.at[shard_rows(spare + peer)],
            d_last.at[order_at(slot, receiver, n_low)],
            dg_send_two.at[peer],
            dg_recv_two.at[slot],
            dp=high * n_low + peer,
        )

    def send_expert_weights():
        hid[0:width] = up_acc[...].astype(BF16)
        for peer in low_peers():
            for block in range(n_high):
                up_grad_first(peer, low, block, peer).start()
        gprime[0:width] = down_acc[...].astype(BF16)
        for peer in high_peers():
            down_grad_first(peer, high, peer).start()

    def pass_expert_weights():
        for peer in low_peers():
            for block in range(n_high):
                up_grad_first(peer, peer, block, low).wait_recv()
        for block in range(n_high):
            added = up_acc[shard_rows(block * n_low + low)]
            for peer in low_peers():
                added = added + u_first[
                    order_at(peer, low, n_low), shard_rows(block)
                ].astype(F32)
            hid[shard_rows(spare + block)] = added.astype(BF16)
        for peer in high_peers():
            up_grad_second(peer, high, peer).start()
        for peer in high_peers():
            down_grad_first(peer, peer, high).wait_recv()
        for block in range(n_low):
            added = down_acc[shard_rows(high * n_low + block)]
            for peer in high_peers():
                added = added + d_first[
                    order_at(peer, high, n_high), shard_rows(block)
                ].astype(F32)
            gprime[shard_rows(spare + block)] = added.astype(BF16)
        for peer in low_peers():
            down_grad_second(peer, low, peer).start()

    def finish_expert_weights():
        added = hid[shard_rows(spare + high)].astype(F32)
        for peer in high_peers():
            up_grad_second(peer, peer, high).wait_recv()
            added = added + u_last[order_at(peer, high, n_high)].astype(F32)
        ugrad_ref[...] = added
        added = gprime[shard_rows(spare + low)].astype(F32)
        for peer in low_peers():
            down_grad_second(peer, peer, low).wait_recv()
            added = added + d_last[order_at(peer, low, n_low)].astype(F32)
        dgrad_ref[...] = added

    attn_sums = Reduce(
        n_exp,
        2 * HD,
        pair_send_two,
        pair_recv_two,
        far_send_two,
        far_recv_two,
        a_sems,
        total_two,
    )

    def dkv_copy(distance, owner):
        return remote(
            dkv_send.at[jnp.clip(owner - win_at, 0, window - 1)],
            dkv_recv.at[distance - 1],
            dk_send.at[distance - 1],
            dk_recv.at[distance - 1],
            expert=owner,
        )

    def attention_back(loop, ahead=False):
        info = meta_ref[loop, own_rows, 0 : 2 * n_exp]
        running = running_rows(loop)
        branch = (sgrad[loop] + carry[...]) * running
        second_grad = total[0:own]
        gate_rows = total[own : own + n_exp, 0:own] + total[own + n_exp : own + 2 * n_exp, 0:own]
        gate_rows = jnp.concatenate(
            [jnp.zeros((n_exp, own), F32), gate_rows, jnp.zeros((LANES - 2 * n_exp, own), F32)],
            axis=0,
        )
        gate_grads = jnp.transpose(gate_rows)[:, 0 : 2 * n_exp]
        second = second_k[loop]
        gates = masked_softmax(nt(second, rb[...]), (info > 0.5) & (route_lane >= n_exp))
        loop_dot = jnp.sum(gates * gate_grads, axis=1, keepdims=True)
        logit_grad = (gates * (gate_grads - loop_dot)).astype(BF16)
        second_grad = second_grad + nn(logit_grad, rb[...])
        unit, inverse = normalise(middle[loop])
        middle_grad = norm_back(second_grad, unit, inverse, gain_two) + branch
        mgrad[...] = middle_grad

        gates = gate_k[loop]
        kv_rows = window_keys(loop)
        dkv_t[...] = jnp.zeros_like(dkv_t)

        def scores_back(pair, none):
            rows = pl.ds(pl.multiple_of(pair * 2 * own, 2 * own), 2 * own)
            out_grads = []
            for half in range(2):
                expert = 2 * pair + half
                part_grad = (column(gates, expert, route_lane) * mgrad[...]).astype(BF16)
                out_grads.append(
                    jnp.where(lane < HD, 0.0, nn(part_grad, w_all[expert])).astype(BF16)
                )
            out_grad = jnp.concatenate(out_grads, axis=0)
            prob_low = p_k[loop, rows]
            prob = prob_low.astype(F32)
            prob_grad = nt(out_grad, kv_rows)
            centre = jnp.sum(prob * prob_grad, axis=1, keepdims=True)
            score_grad = (prob * (prob_grad - centre)).astype(BF16)
            ds_k[rows] = score_grad
            dkv_t[...] += tn(q_k[loop, rows], score_grad) * scale + tn(out_grad, prob_low)
            return none

        lax.fori_loop(0, n_exp // 2, scores_back, 0, unroll=True)
        for block in range(window):
            grads = jnp.transpose(dkv_t[:, block * own : (block + 1) * own])
            dkv[block] = grads
            dkv_send[block] = grads.astype(BF16)
        for distance in range(1, window):

            @pl.when(active & (me >= distance))
            def _():
                dkv_copy(distance, me - distance).start()

        if ahead:
            state_grads(loop_dot)
        small_acc[2 * HD : vec_at] += tn(logit_grad, second)
        small_acc[vec_at + 2 : vec_at + 3] += jnp.sum(second_grad * unit, axis=0, keepdims=True)
        small_acc[vec_at + 3 : vec_at + 4] += jnp.sum(second_grad, axis=0, keepdims=True)
        normed = normed_k[loop]
        mix[...] = jnp.zeros_like(mix)
        dga[...] = jnp.zeros_like(dga)

        def queries_back(pair, none):
            rows = pl.ds(pl.multiple_of(pair * 2 * own, 2 * own), 2 * own)
            outs = o_k[loop, rows]
            query_grad = jnp.where(lane_two < HD, nn(ds_k[rows], kv_rows) * scale, 0.0).astype(BF16)
            for half in range(2):
                expert = 2 * pair + half
                cut = slice(half * own, (half + 1) * own)
                middle_grad = mgrad[...]
                dot = jnp.sum(middle_grad * nt(outs[cut], w_all[expert]), axis=1, keepdims=True)
                dga[...] += jnp.where(route_lane == expert, dot, 0.0)
                part_grad = (column(gates, expert, route_lane) * middle_grad).astype(BF16)
                attn_acc[expert] += tn(query_grad[cut], normed) + tn(outs[cut], part_grad)
                mix[...] += nt(query_grad[cut], w_all[expert])
            return none

        lax.fori_loop(0, n_exp // 2, queries_back, 0)

        if not ahead:

            @pl.when(loop == 0)
            def _():
                attn_sums.start(lambda block: attn_acc[block], False)
                attn_sums.send(1)

        gate_grads = dga[...]
        logit_grad = (
            gates * (gate_grads - jnp.sum(gates * gate_grads, axis=1, keepdims=True))
        ).astype(BF16)
        small_acc[2 * HD : vec_at] += tn(logit_grad, normed)
        normed_grad = mix[...] + nn(logit_grad, rb[...])
        unit, inverse = normalise(state[loop])

        own_block = jnp.clip(me - win_at, 0, window - 1)
        dkv[window] = jnp.where(active, dkv[own_block], 0.0)
        for distance in range(1, window):

            @pl.when(me + distance < n_act)
            def _():
                remote(
                    dkv_send.at[0],
                    dkv_recv.at[distance - 1],
                    dk_send.at[distance - 1],
                    dk_recv.at[distance - 1],
                    expert=me + distance,
                ).wait_recv()
                dkv[window] += dkv_recv[distance - 1].astype(F32)

        for distance in range(1, window):

            @pl.when(active & (me >= distance))
            def _():
                dkv_copy(distance, me - distance).wait_send()

        kv_grad = dkv[window].astype(BF16)
        small_acc[0 : 2 * HD] += tn(kv_grad, normed)
        normed_grad = normed_grad + nt(kv_grad, kvb[...])
        small_acc[vec_at : vec_at + 1] += jnp.sum(normed_grad * unit, axis=0, keepdims=True)
        small_acc[vec_at + 1 : vec_at + 2] += jnp.sum(normed_grad, axis=0, keepdims=True)
        carry[...] = (
            (sgrad[loop] + carry[...]) * (1.0 - running)
            + mgrad[...]
            + norm_back(normed_grad, unit, inverse, gain_one)
        )

    attention(last)
    rows_gather.start()
    up_acc[...] = jnp.zeros_like(up_acc)
    place_matrices(last)
    chosen = chosen_rows(last)
    cot_gather.finish()
    factor_gather.finish()
    factors = nt(gather_m[...], jnp.concatenate([wrow[block] for block in range(n_act)], axis=1))
    grad_rows = take(rows_two) * (factors[:, 0:1] + factors[:, 1:2])
    rows_gather.finish()
    expert_rows(last, chosen)
    hidden_layer(last, True)
    expert_back(last, grad_rows)
    start_terms(last, sums_two, False)
    expert_weights(last)
    back_sums.finish()
    sums_two.send(1)
    attention_back(last, True)

    def backward(step, none):
        loop = last - 1 - step

        @pl.when(loop == 0)
        def _():
            sums_two.finish()
            finish_output()

        branch = (sgrad[loop] + carry[...]) * running_rows(loop)
        rows_all[me] = branch.astype(BF16)
        rows_gather.start()
        place_matrices(loop)
        rows_gather.finish()

        @pl.when(loop == 1)
        def _():
            sums_two.send(2)

        expert_back(loop, take(rows_all))
        expert_weights(loop)

        @pl.when(loop == 0)
        def _():
            send_expert_weights()

        back_sums.finish()

        @pl.when(loop == 1)
        def _():
            sums_two.send(3)

        attention_back(loop)
        return none

    lax.fori_loop(0, last, backward, 0)
    xgrad_ref[...] = carry[...]

    chunk = small_acc.shape[0] // n_exp
    small_sums = Reduce(
        n_exp, chunk, s_pair_send, s_pair_recv, s_far_send, s_far_recv, s_sems, s_total
    )
    small_sums.start(lambda block: small_acc[pl.ds(pl.multiple_of(block * chunk, chunk), chunk)])
    attn_sums.send(3)
    attn_sums.send(2)

    def attn_copy(peer, slot):
        return remote(
            a_stage.at[shard_rows(peer)],
            a_recv.at[shard_rows(slot)],
            t_send.at[1, peer],
            t_recv.at[1, slot],
            dp=peer,
        )

    def small_copy(peer, slot):
        return remote(
            s_dp.at[slot], s_dp.at[slot], t_send.at[0, peer], t_recv.at[0, slot], dp=peer
        )

    small_sums.finish()
    s_dp[dp] = s_total[...].astype(BF16)
    each_peer(lambda peer: small_copy(peer, dp).start())
    pass_expert_weights()
    attn_sums.finish()
    a_total[...] = jnp.transpose(total_two[...])
    a_stage[...] = a_total[...].astype(BF16)
    each_peer(lambda peer: attn_copy(peer, dp).start())
    each_peer(lambda peer: small_copy(peer, peer).wait_recv())
    s_total[...] = jnp.zeros_like(s_total)

    def add_small(index, none):
        s_total[...] += s_dp[index].astype(F32)
        return none

    lax.fori_loop(0, n_dp, add_small, 0)
    s_all[me] = s_total[...]
    small_gather = Gather(s_all, sg_send, sg_recv, n_exp)
    small_gather.start()
    agrad_ref[...] = a_total[shard_rows(dp)]

    def add_attn(peer):
        attn_copy(peer, peer).wait_recv()
        agrad_ref[...] += a_recv[shard_rows(peer)].astype(F32)

    each_peer(add_attn)
    finish_expert_weights()
    small_gather.finish()
    small = s_all[...].reshape(n_exp * chunk, width)
    kvgrad_ref[...] = jnp.transpose(small[0 : 2 * HD])
    rgrad_ref[...] = small[2 * HD : vec_at]
    vgrad_ref[...] = small[vec_at : vec_at + 8]

    def sent(peer):
        attn_weight_copy(peer, dp).wait_send()
        small_copy(peer, dp).wait_send()
        attn_copy(peer, dp).wait_send()

    each_peer(sent)
    for peer in low_peers():
        up_low(peer, low).wait_send()
        down_grad_second(peer, low, peer).wait_send()
        for block in range(n_high):
            down_low(peer, low, block).wait_send()
            up_grad_first(peer, low, block, peer).wait_send()
    for peer in high_peers():
        down_high(peer, high).wait_send()
        for block in range(n_low):
            up_high(peer, high, block).wait_send()
        up_grad_second(peer, high, peer).wait_send()
        down_grad_first(peer, high, peer).wait_send()


def adam_kernel(*refs):
    out_in, xgrad_in, ugrad, dgrad, agrad, kvgrad, rgrad, vgrad = refs[:8]
    shared, kv, router, attn, up, down = (refs[8 + 3 * index : 11 + 3 * index] for index in range(6))
    out, xgrad = refs[26:28]
    shared_out, kv_out, router_out, attn_out, up_out, down_out = (
        refs[28:31],
        refs[31:34],
        refs[34:37],
        refs[37:41],
        refs[41:45],
        refs[45:49],
    )

    def update(sources, grad, results, rate, decay):
        values = adam_update(*(source[...] for source in sources), grad, rate, decay)
        for result, value in zip(results, values):
            result[...] = value
        if len(results) > 3:
            results[3][...] = values[0].astype(BF16)

    out[...] = out_in[...]
    xgrad[...] = xgrad_in[...]
    update(up, ugrad[...], up_out, 14.0 / math.sqrt(D), decay_rate)
    update(down, dgrad[...], down_out, 17.0 / math.sqrt(FF), decay_rate)

    @pl.when(pl.program_id(0) == 0)
    def _():
        row = lax.broadcasted_iota(jnp.int32, shared[0].shape, 0)
        rates = jnp.where(row < 4, 6.0, 20.0 / math.sqrt(D))
        update(shared, vgrad[0 : shared[0].shape[0]], shared_out, rates, 0.0)
        update(kv, kvgrad[...], kv_out, 20.0 / math.sqrt(D), decay_rate)
        update(router, rgrad[...], router_out, 50.0 / math.sqrt(3 * D), decay_rate)
        lane = lax.broadcasted_iota(jnp.int32, attn[0].shape, 1)
        rates = jnp.where(lane < HD, 25.0 / math.sqrt(D), 50.0 / math.sqrt(HD))
        update(attn, agrad[...], attn_out, rates, decay_rate)


def dp_grid(n_dp):
    n_low = 1
    while n_low * n_low * 4 <= n_dp:
        n_low *= 2
    return n_low, n_dp // n_low


def per_device(
    block_input,
    cotangent,
    lengths,
    run_loops,
    attn_routes,
    ffn_routes,
    shared_vectors,
    shared_moment,
    shared_second,
    key_value,
    kv_moment,
    kv_second,
    router_weights,
    router_moment,
    router_second,
    attn_weights,
    attn_moment,
    attn_second,
    up_weights,
    up_moment,
    up_second,
    down_weights,
    down_moment,
    down_second,
):
    n_exp = lax.axis_size("expert")
    n_dp = lax.axis_size("dp")
    own, width = block_input.shape
    slots = run_loops.shape[0]
    shard = attn_weights.shape[1]
    hidden = up_weights.shape[2]
    cap = 5 * slots * KFF // (4 * n_exp)
    n_act = FILLED // own
    window = min(n_act, MAXLEN // own + 1)
    pairs = n_exp // 2
    valid_rows = n_act * own
    n_low, n_high = dp_grid(n_dp)

    small_rows = 32 * n_exp
    vmem = pltpu.VMEM
    dma = pltpu.SemaphoreType.DMA
    block = (pairs, own + EXTRA, width)
    small_block = (pairs, 32, width)
    scratch = [
        vmem((LOOPS, slots, INFO), F32),
        vmem((LOOPS + 1, 1, slots), F32),
        vmem((width, 2 * HD), BF16),
        vmem((2 * n_exp, width), BF16),
        vmem((n_exp, width, 2 * HD), BF16),
        vmem((width, hidden), BF16),
        vmem((width, hidden), BF16),
        vmem((width, hidden), F32),
        vmem((width, hidden), F32),
        vmem((n_exp, 2 * HD, width), F32),
        vmem((small_rows, width), F32),
        vmem((LOOPS, own, width), F32),
        vmem((LOOPS, own, width), F32),
        vmem((LOOPS, own, width), BF16),
        vmem((LOOPS, own, width), BF16),
        vmem((LOOPS, n_exp, own, 2 * HD), BF16),
        vmem((LOOPS, n_exp * own, 2 * HD), BF16),
        vmem((LOOPS, n_exp * own, 2 * HD), BF16),
        vmem((LOOPS, n_exp * own, window * own), BF16),
        vmem((n_exp * own, window * own), BF16),
        vmem((own, window * own), F32),
        vmem((own, width), F32),
        vmem((own, 2 * n_exp), F32),
        vmem((2 * HD, window * own), F32),
        vmem((window + 1, own, 2 * HD), F32),
        vmem((LOOPS, own, 2 * n_exp), F32),
        vmem((n_exp, own, width), BF16),
        vmem((n_exp, own, width), BF16),
        vmem((n_exp, EXTRA, own), BF16),
        vmem((cap, valid_rows), BF16),
        vmem((valid_rows, cap), BF16),
        vmem((LOOPS * cap, width), BF16),
        vmem((LOOPS * cap, hidden), BF16),
        vmem((LOOPS * cap, hidden), BF16),
        vmem((cap, width), F32),
        vmem((LOOPS * cap, width), F32),
        vmem((LOOPS * cap, 1), F32),
        vmem((cap, 1), F32),
        vmem((cap, width), BF16),
        vmem((LOOPS, own, width), F32),
        vmem((own, width), F32),
        vmem((own, width), F32),
        vmem((own + EXTRA, width), F32),
        vmem((own, width), F32),
        vmem(block, BF16),
        vmem(block, BF16),
        vmem(block, BF16),
        vmem(block, BF16),
        vmem((pairs, own, width), BF16),
        vmem((pairs, own, width), BF16),
        vmem((pairs, own, width), BF16),
        vmem((pairs, own, width), BF16),
        vmem((window, own, 2 * HD), BF16),
        vmem((window, own, 2 * HD), BF16),
        vmem((n_low - 1, n_high * shard, hidden), BF16),
        vmem((n_high - 1, shard, hidden), BF16),
        vmem((n_high - 1, n_low * shard, hidden), BF16),
        vmem((n_low - 1, shard, hidden), BF16),
        vmem((width, 2 * HD), F32),
        vmem((width, 2 * HD), BF16),
        vmem((width, 2 * HD), BF16),
        vmem(small_block, BF16),
        vmem(small_block, BF16),
        vmem(small_block, BF16),
        vmem(small_block, BF16),
        vmem((32, width), F32),
        vmem((n_dp, 32, width), BF16),
        vmem((n_exp, 32, width), F32),
        dma((2,)),
        dma((n_dp,)),
        dma((n_dp,)),
        dma((n_low,)),
        dma((n_dp,)),
        dma((n_high, n_low)),
        dma((n_high,)),
        dma((n_dp,)),
        dma((n_low, n_high)),
        dma((2 * pairs,)),
        dma((n_exp,)),
        dma((2 * pairs,)),
        dma((n_exp,)),
        dma((2 * pairs,)),
        dma((n_exp,)),
        dma((2 * pairs,)),
        dma((n_exp,)),
        dma((2 * pairs,)),
        dma((n_exp,)),
        dma((window,)),
        dma((n_exp,)),
        dma((4, pairs)),
        dma((4, pairs)),
        dma((4, pairs)),
        dma((4, pairs)),
        dma((window,)),
        dma((window,)),
        dma((n_low, n_high)),
        dma((n_low, n_high)),
        dma((n_high,)),
        dma((n_high,)),
        dma((n_high,)),
        dma((n_high,)),
        dma((n_low,)),
        dma((n_low,)),
        dma((2, n_dp)),
        dma((2, n_dp)),
    ]
    whole = pl.BlockSpec(memory_space=pltpu.VMEM)
    scalars = pl.BlockSpec(memory_space=pltpu.SMEM)
    outside = pl.BlockSpec(memory_space=pl.ANY)
    shape = jax.ShapeDtypeStruct
    sums = pl.pallas_call(
        functools.partial(block_kernel, n_exp, n_dp, n_act, cap),
        out_shape=(
            shape((own, width), F32),
            shape((own, width), F32),
            shape((shard, hidden), F32),
            shape((shard, hidden), F32),
            shape((shard, 2 * HD), F32),
            shape((width, 2 * HD), F32),
            shape((2 * n_exp, width), F32),
            shape((8, width), F32),
        ),
        in_specs=[whole, whole, scalars, *([whole] * 7), outside, outside],
        out_specs=[whole] * 8,
        scratch_shapes=scratch,
        compiler_params=pltpu.CompilerParams(
            collective_id=0, has_side_effects=True, vmem_limit_bytes=63 * 1024 * 1024
        ),
        name="block",
    )(
        block_input,
        cotangent,
        lengths,
        run_loops[None],
        attn_routes.transpose(0, 2, 1),
        ffn_routes.transpose(0, 2, 1),
        shared_vectors,
        key_value,
        router_weights.T,
        attn_weights[0],
        up_weights[0],
        down_weights[0],
    )

    steps = max(1, shard // 64)
    rows = shard // steps

    def by_rows(array):
        return pl.BlockSpec((array.shape[0] // steps, array.shape[1]), lambda step: (step, 0))

    def fixed(array):
        return pl.BlockSpec(array.shape, lambda step: (0, 0))

    output, input_grad, up_sum, down_sum, *small = sums
    small_args = [
        shared_vectors,
        shared_moment,
        shared_second,
        key_value,
        kv_moment,
        kv_second,
        router_weights.T,
        router_moment.T,
        router_second.T,
        attn_weights[0],
        attn_moment[0],
        attn_second[0],
    ]
    large_args = [
        up_weights[0],
        up_moment[0],
        up_second[0],
        down_weights[0],
        down_moment[0],
        down_second[0],
    ]
    attn_low = shape((shard, 2 * HD), BF16)
    large_low = shape((shard, hidden), BF16)
    like = [shape(array.shape, array.dtype) for array in small_args]
    big = [shape(array.shape, array.dtype) for array in large_args]
    outs = [
        shape(output.shape, F32),
        shape(input_grad.shape, F32),
        *like,
        attn_low,
        *big[:3],
        large_low,
        *big[3:],
        large_low,
    ]
    results = pl.pallas_call(
        adam_kernel,
        grid=(steps,),
        out_shape=outs,
        in_specs=[
            by_rows(output),
            by_rows(input_grad),
            by_rows(up_sum),
            by_rows(down_sum),
            *(fixed(array) for array in small),
            *(fixed(array) for array in small_args),
            *(by_rows(array) for array in large_args),
        ],
        out_specs=[
            by_rows(output),
            by_rows(input_grad),
            *(fixed(array) for array in (*like, attn_low)),
            *(by_rows(array) for array in (*big[:3], large_low, *big[3:], large_low)),
        ],
        compiler_params=pltpu.CompilerParams(vmem_limit_bytes=63 * 1024 * 1024),
        name="adamw",
    )(*sums, *small_args, *large_args)
    output, input_grad, *rest = results
    shared_kv, router, weights = rest[:6], rest[6:9], rest[9:]
    return (
        output,
        input_grad,
        *shared_kv,
        *(array.T for array in router),
        *(array[None] for array in weights),
    )


def solution(mesh):
    rows = P(("dp", "expert"), None)
    weights = P("expert", "dp", None)
    return jax.shard_map(
        per_device,
        mesh=mesh,
        in_specs=(
            rows,
            rows,
            P("dp", None),
            P("dp"),
            P(None, "dp", None),
            P(None, "dp", None),
            *([P()] * 9),
            *([weights] * 9),
        ),
        out_specs=(rows, rows, *([P()] * 9), *([weights] * 12)),
        check_vma=False,
    )
```

```python
import functools
import math

import jax
import jax.numpy as jnp
from jax import lax
from jax.experimental import pallas as pl
from jax.experimental.pallas import tpu as pltpu
from jax.sharding import PartitionSpec as P

D = 512
HD = 64
FF = 2048
KATT = 4
KFF = 2
LOOPS = 3
STEP = 10
MAXLEN = 512
FILLED = 896

ln_eps = 1e-05
beta_one = 0.9
beta_two = 0.999
adam_eps = 1e-08
decay_rate = 0.01
masked_score = -1e30

F32 = jnp.float32
BF16 = jnp.bfloat16
MESH = pl.DeviceIdType.MESH
LANES = 128
RANK_LANE = 16
RUN_LANE = 17
SEG_LANE = 18
INFO = 32
TILE = 512
EXTRA = 16


def nn(left, right):
    return lax.dot_general(left, right, (((1,), (0,)), ((), ())), preferred_element_type=F32)


def nt(left, right):
    return lax.dot_general(left, right, (((1,), (1,)), ((), ())), preferred_element_type=F32)


def tn(left, right):
    return lax.dot_general(left, right, (((0,), (0,)), ((), ())), preferred_element_type=F32)


def normalise(values):
    centre = values - jnp.mean(values, axis=-1, keepdims=True)
    inverse = lax.rsqrt(jnp.mean(centre * centre, axis=-1, keepdims=True) + ln_eps)
    return centre * inverse, inverse


def norm_back(grad, unit, inverse, gain):
    scaled = grad * gain
    first = jnp.mean(scaled, axis=-1, keepdims=True)
    second = jnp.mean(scaled * unit, axis=-1, keepdims=True)
    return inverse * (scaled - first - unit * second)


def masked_softmax(logits, valid):
    top = jnp.max(jnp.where(valid, logits, masked_score), axis=-1, keepdims=True)
    powers = jnp.where(valid, jnp.exp(jnp.where(valid, logits - top, 0.0)), 0.0)
    return powers / jnp.maximum(jnp.sum(powers, axis=-1, keepdims=True), 0.5)


def adam_update(weight, moment, second, grad, rate, decay):
    moment_new = beta_one * moment + (1.0 - beta_one) * grad
    second_new = beta_two * second + (1.0 - beta_two) * grad * grad
    moment_hat = moment_new * (1.0 / (1.0 - beta_one**STEP))
    second_hat = second_new * (1.0 / (1.0 - beta_two**STEP))
    weight_new = weight - rate * (moment_hat / (jnp.sqrt(second_hat) + adam_eps) + decay * weight)
    return (weight_new, moment_new, second_new)


def block_kernel(
    n_exp,
    n_dp,
    n_act,
    cap,
    x_ref,
    cot_ref,
    len_ref,
    run_ref,
    ar_ref,
    fr_ref,
    vec_ref,
    kvw_ref,
    rw_ref,
    aw_ref,
    uw_hbm,
    dw_hbm,
    out_ref,
    xgrad_ref,
    ugrad_ref,
    dgrad_ref,
    agrad_ref,
    kvgrad_ref,
    rgrad_ref,
    vgrad_ref,
    meta_ref,
    rowm_ref,
    kvb,
    rb,
    w_all,
    up_w,
    down_w,
    up_acc,
    down_acc,
    attn_acc,
    small_acc,
    state,
    middle,
    normed_k,
    second_k,
    kv_k,
    q_k,
    o_k,
    p_k,
    ds_k,
    bias,
    mix,
    dga,
    dkv_t,
    dkv,
    gate_k,
    rows_all,
    wrow,
    gather_m,
    scatter_m,
    rows_k,
    hid,
    gprime,
    row_grads,
    part_k,
    fgate_k,
    chosen_k,
    ggrad,
    scaled_k,
    sgrad,
    carry,
    mgrad,
    total,
    total_two,
    pair_send,
    pair_recv,
    far_send,
    far_recv,
    pair_send_two,
    pair_recv_two,
    far_send_two,
    far_recv_two,
    dkv_send,
    dkv_recv,
    u_first,
    u_last,
    d_first,
    d_last,
    a_total,
    a_stage,
    a_recv,
    s_pair_send,
    s_pair_recv,
    s_far_send,
    s_far_recv,
    s_total,
    s_dp,
    s_all,
    in_sems,
    w_send,
    w_recv,
    uw_send,
    uw_recv,
    uw_send_two,
    dw_send,
    dw_recv,
    dw_send_two,
    ag_send,
    ag_recv,
    bg_send,
    bg_recv,
    fg_send,
    fg_recv,
    wg_send,
    wg_recv,
    sg_send,
    sg_recv,
    kg_send,
    kg_recv,
    rs_sems,
    rs_sems_two,
    s_sems,
    a_sems,
    dk_send,
    dk_recv,
    ug_send,
    ug_recv,
    ug_send_two,
    ug_recv_two,
    dg_send,
    dg_recv,
    dg_send_two,
    dg_recv_two,
    t_send,
    t_recv,
):
    me = lax.axis_index("expert")
    dp = lax.axis_index("dp")
    pairs = n_exp // 2
    core = lax.rem(me, 2)
    chip = lax.div(me, 2)
    sibling = 2 * chip + 1 - core
    n_low, n_high = dp_grid(n_dp)
    high = lax.div(dp, n_low)
    low = lax.rem(dp, n_low)
    own = x_ref.shape[0]
    width = x_ref.shape[1]
    slots = run_ref.shape[1]
    shard = aw_ref.shape[0]
    hidden_units = up_w.shape[1]
    tiles = hidden_units // TILE
    valid_rows = n_act * own
    window = min(n_act, MAXLEN // own + 1)
    keys = window * own
    win_at = jnp.clip(me - (window - 1), 0, n_act - window)
    scale = HD ** (-0.5)
    active = me < n_act
    last = LOOPS - 1

    def remote(src, dst, send, recv, **where):
        return pltpu.make_async_remote_copy(
            src_ref=src,
            dst_ref=dst,
            send_sem=send,
            recv_sem=recv,
            device_id=where,
            device_id_type=MESH,
        )

    def shard_rows(index, count=1):
        return pl.ds(pl.multiple_of(index * shard, shard), count * shard)

    def each_peer(body):
        def step(k, none):
            body(lax.rem(dp + k, n_dp))
            return none

        lax.fori_loop(1, n_dp, step, 0)

    def high_peers():
        return [lax.rem(high + k, n_high) for k in range(1, n_high)]

    def low_peers():
        return [lax.rem(low + k, n_low) for k in range(1, n_low)]

    class Gather:
        def __init__(self, buf, send, recv, count):
            self.buf, self.sent, self.got, self.count = buf, send, recv, count

        def copy(self, block, sem, where):
            ref = self.buf.at[block]
            return remote(ref, ref, self.sent.at[sem], self.got.at[block], expert=where)

        def start(self):
            for k in (*range(1, pairs, 2), *range(2, pairs, 2)):
                self.send(k)
            self.send(0)

        def send(self, k):
            zz = lax.rem(chip + k, pairs)

            @pl.when(me < self.count)
            def _():
                self.copy(me, zz, 2 * zz + core if k else sibling).start()

        def finish(self):
            for k in range(pairs - 1, 0, -1):
                zz = lax.rem(chip + k, pairs)
                src = 2 * zz + core

                @pl.when(src < self.count)
                def _():
                    self.copy(src, zz, src).wait_recv()
                    self.copy(src, pairs + zz, sibling).start()

            for k in range(pairs):
                zz = lax.rem(chip + k, pairs)
                src = 2 * zz + 1 - core

                @pl.when(src < self.count)
                def _():
                    self.copy(src, zz, sibling).wait_recv()

            @pl.when(me < self.count)
            def _():
                for k in range(1, pairs):
                    zz = lax.rem(chip + k, pairs)
                    self.copy(me, zz, 2 * zz + core).wait_send()
                self.copy(me, chip, sibling).wait_send()

            for k in range(1, pairs):
                zz = lax.rem(chip + k, pairs)
                src = 2 * zz + core

                @pl.when(src < self.count)
                def _():
                    self.copy(src, pairs + zz, sibling).wait_send()

    class Reduce:
        def __init__(self, count, rows, psend, precv, fsend, frecv, sems, result, halves=False):
            self.halves = halves
            self.count, self.rows, self.part = count, rows, pl.ds(0, rows)
            self.psend, self.precv, self.fsend, self.frecv = psend, precv, fsend, frecv
            self.sems, self.result = sems, result

        def pair_copy(self, zz):
            return remote(
                self.psend.at[zz, self.part],
                self.precv.at[zz, self.part],
                self.sems.at[0, zz],
                self.sems.at[1, zz],
                expert=sibling,
            )

        def far_copy(self, zz, slot, half=None):
            part = self.part if half is None else pl.ds(half * (self.rows // 2), self.rows // 2)
            at = 2 if half is None else 2 + 2 * half
            return remote(
                self.fsend.at[zz, part],
                self.frecv.at[slot, part],
                self.sems.at[at, zz],
                self.sems.at[at + 1, slot],
                expert=2 * zz + core,
            )

        def far_parts(self):
            return (0, 1) if self.halves else (None,)

        def far_copies(self, zz, slot):
            return [self.far_copy(zz, slot, half) for half in self.far_parts()]

        def start(self, make, send):
            for k in range(pairs):
                zz = lax.rem(chip + 1 + k, pairs)
                block = 2 * zz + 1 - core

                @pl.when(block < self.count)
                def _():
                    self.psend[zz, self.part] = make(block).astype(BF16)
                    self.pair_copy(zz).start()

            for k in range(1, pairs):
                zz = lax.rem(chip + k, pairs)
                block = 2 * zz + core

                @pl.when(block < self.count)
                def _():
                    mine = make(block)
                    self.pair_copy(zz).wait_recv()
                    self.fsend[zz, self.part] = (
                        mine + self.precv[zz, self.part].astype(F32)
                    ).astype(BF16)

                    def go():
                        for copy in self.far_copies(zz, chip):
                            copy.start()

                    if isinstance(send, bool):
                        if send:
                            go()
                    else:
                        pl.when(send)(go)

            @pl.when(me < self.count)
            def _():
                mine = make(me)
                self.pair_copy(chip).wait_recv()
                self.result[self.part] = mine + self.precv[chip, self.part].astype(F32)

            @pl.when(me >= self.count)
            def _():
                self.result[self.part] = jnp.zeros((self.rows, self.result.shape[1]), F32)

        def send(self, *parts):
            for k, half in parts:
                zz = lax.rem(chip + k, pairs)

                @pl.when(2 * zz + core < self.count)
                def _():
                    self.far_copy(zz, chip, self.far_parts()[half]).start()

        def finish(self):
            @pl.when(me < self.count)
            def _():
                for k in range(1, pairs):
                    zz = lax.rem(chip + k, pairs)
                    for copy in self.far_copies(zz, zz):
                        copy.wait_recv()
                    self.result[self.part] += self.frecv[zz, self.part].astype(F32)

            for k in range(pairs):
                zz = lax.rem(chip + 1 + k, pairs)

                @pl.when(2 * zz + 1 - core < self.count)
                def _():
                    self.pair_copy(zz).wait_send()

            for k in range(1, pairs):
                zz = lax.rem(chip + k, pairs)

                @pl.when(2 * zz + core < self.count)
                def _():
                    for copy in self.far_copies(zz, chip):
                        copy.wait_send()

    def attn_weight_copy(peer, slot):
        ref = w_all.at[me, shard_rows(slot)]
        return remote(ref, ref, w_send.at[peer], w_recv.at[slot], dp=peer)

    def up_low(peer, block):
        ref = up_w.at[shard_rows(high * n_low + block)]
        return remote(
            ref,
            ref,
            uw_send.at[peer],
            uw_recv.at[high * n_low + block],
            dp=high * n_low + peer,
        )

    def up_high(peer, row, block):
        ref = up_w.at[shard_rows(row * n_low + block)]
        return remote(
            ref,
            ref,
            uw_send_two.at[peer, block],
            uw_recv.at[row * n_low + block],
            dp=peer * n_low + low,
        )

    def down_high(peer, block):
        ref = down_w.at[shard_rows(block * n_low + low)]
        return remote(
            ref,
            ref,
            dw_send.at[peer],
            dw_recv.at[block * n_low + low],
            dp=peer * n_low + low,
        )

    def down_low(peer, column_at, block):
        ref = down_w.at[shard_rows(block * n_low + column_at)]
        return remote(
            ref,
            ref,
            dw_send_two.at[peer, block],
            dw_recv.at[block * n_low + column_at],
            dp=high * n_low + peer,
        )

    up_in = pltpu.make_async_copy(uw_hbm, ugrad_ref, in_sems.at[0])
    down_in = pltpu.make_async_copy(dw_hbm, dgrad_ref, in_sems.at[1])
    up_in.start()
    down_in.start()
    kv_k[...] = jnp.zeros_like(kv_k)
    barrier = pltpu.get_barrier_semaphore()
    for k in range(1, n_exp):
        pl.semaphore_signal(
            barrier, inc=1, device_id={"expert": lax.rem(me + k, n_exp)}, device_id_type=MESH
        )
    for k in range(1, n_dp):
        pl.semaphore_signal(
            barrier, inc=1, device_id={"dp": lax.rem(dp + k, n_dp)}, device_id_type=MESH
        )
    rows_all[1, me] = cot_ref[...]
    wrow[...] = jnp.zeros_like(wrow)
    w_all[me, shard_rows(dp)] = aw_ref[...].astype(BF16)
    up_in.wait()
    up_w[shard_rows(dp)] = ugrad_ref[...].astype(BF16)
    down_in.wait()
    down_w[shard_rows(dp)] = dgrad_ref[...].astype(BF16)
    pl.semaphore_wait(barrier, n_exp + n_dp - 2)
    each_peer(lambda peer: attn_weight_copy(peer, dp).start())
    cot_gather = Gather(rows_all.at[1], bg_send, bg_recv, n_act)
    cot_gather.send(2)
    for peer in low_peers():
        up_low(peer, low).start()
    for peer in high_peers():
        down_high(peer, high).start()
    for peer in high_peers():
        up_high(peer, high, low).start()
    for peer in low_peers():
        down_low(peer, low, high).start()

    kvb[...] = kvw_ref[...].astype(BF16)
    rb[...] = rw_ref[...].astype(BF16)
    gain_one = vec_ref[0:1, :]
    bias_one = vec_ref[1:2, :]
    gain_two = vec_ref[2:3, :]
    bias_two = vec_ref[3:4, :]
    halt = vec_ref[4:5, :]
    state[0] = x_ref[...].astype(F32)
    own_rows = pl.ds(pl.multiple_of(me * own, own), own)

    lane = lax.broadcasted_iota(jnp.int32, (own, LANES), 1)
    route_lane = lax.broadcasted_iota(jnp.int32, (own, 2 * n_exp), 1)
    lane_two = lax.broadcasted_iota(jnp.int32, (2 * own, LANES), 1)
    lane_cap = lax.broadcasted_iota(jnp.int32, (cap, LANES), 1)
    route_cap = lax.broadcasted_iota(jnp.int32, (cap, 2 * n_exp), 1)

    def column(values, index, lanes):
        return jnp.sum(jnp.where(lanes == index, values, 0.0), axis=1, keepdims=True)

    def cap_rows(loop):
        return pl.ds(pl.multiple_of(loop * cap, cap), cap)

    def window_keys(loop):
        return kv_k[loop, pl.ds(win_at, window)].reshape(keys, 2 * HD)

    def routing():
        position = lax.broadcasted_iota(jnp.int32, (1, slots), 1)
        bound = 0
        segment = jnp.zeros((1, slots), F32)
        for index in range(len_ref.shape[1]):
            bound = bound + len_ref[0, index]
            segment = segment + jnp.where(position >= bound, 1.0, 0.0)
        sub = lax.broadcasted_iota(jnp.int32, (n_exp, slots), 0)
        position_all = lax.broadcasted_iota(jnp.int32, (n_exp, slots), 1)
        valid = segment < len_ref.shape[1] - 0.5
        rowm_ref[LOOPS] = segment
        picks, selected = [], jnp.zeros((n_exp, slots), F32)
        for loop in range(LOOPS):
            running = jnp.where(valid & (run_ref[...] > loop), 1.0, 0.0)
            att = jnp.zeros((n_exp, slots), F32)
            for k in range(ar_ref.shape[1]):
                att = att + jnp.where(ar_ref[loop, k : k + 1, :] == sub, 1.0, 0.0)
            ffn = jnp.zeros((n_exp, slots), F32)
            mine = jnp.zeros((1, slots), F32)
            for k in range(fr_ref.shape[1]):
                ffn = ffn + jnp.where(fr_ref[loop, k : k + 1, :] == sub, 1.0, 0.0)
                mine = mine + jnp.where(fr_ref[loop, k : k + 1, :] == me, running, 0.0)
            picks.append((att, ffn, running))
            selected = selected + jnp.where(sub == loop, mine, 0.0)
        ranks = selected
        shift = 1
        while shift < slots:
            moved = pltpu.roll(ranks, shift, 1)
            ranks = ranks + jnp.where(position_all >= shift, moved, 0.0)
            shift *= 2
        ranks = jnp.where(selected > 0.5, ranks - 1.0, -1.0)
        for loop in range(LOOPS):
            att, ffn, running = picks[loop]
            rank = ranks[loop : loop + 1]
            rowm_ref[loop] = rank
            rest = jnp.where(
                sub == 0,
                rank,
                jnp.where(sub == 1, running, jnp.where(sub == 2, segment, 0.0)),
            )
            spare = jnp.zeros((INFO - 3 * n_exp, slots), F32)
            meta_ref[loop] = jnp.transpose(jnp.concatenate([att, ffn, rest, spare], axis=0))

    def kv_copy(loop, where, sem):
        ref = kv_k.at[loop, me]
        return remote(ref, ref, kg_send.at[sem], kg_recv.at[me], expert=where)

    def prepare(loop):
        unit, _ = normalise(state[loop])
        normed = (unit * gain_one + bias_one).astype(BF16)
        normed_k[loop] = normed
        kv_k[loop, me] = nn(normed, kvb[...]).astype(BF16)
        for k in range(1, window):

            @pl.when(me + k < n_act)
            def _():
                kv_copy(loop, me + k, k - 1).start()

        info = meta_ref[loop, own_rows, 0 : 2 * n_exp]
        gate_k[loop] = masked_softmax(
            nt(normed, rb[...]), (info > 0.5) & (route_lane < n_exp)
        )

    def running_rows(loop):
        return meta_ref[loop, own_rows, RUN_LANE : RUN_LANE + 1]

    each_peer(lambda peer: attn_weight_copy(peer, peer).wait_recv())
    weights_gather = Gather(w_all, wg_send, wg_recv, n_exp)
    weights_gather.start()
    routing()
    prepare(0)
    seg_own = meta_ref[0, own_rows, SEG_LANE : SEG_LANE + 1]
    key_cols = pl.ds(pl.multiple_of(win_at * own, own), keys)
    seg_keys = rowm_ref[LOOPS, :, key_cols]
    row_at = me * own + lax.broadcasted_iota(jnp.int32, (own, keys), 0)
    key_at = win_at * own + lax.broadcasted_iota(jnp.int32, (own, keys), 1)
    allowed = (seg_own == seg_keys) & (key_at <= row_at)
    bias[...] = jnp.where(allowed, 0.0, masked_score)
    up_acc[...] = jnp.zeros_like(up_acc)
    down_acc[...] = jnp.zeros_like(down_acc)
    attn_acc[...] = jnp.zeros_like(attn_acc)
    small_acc[...] = jnp.zeros_like(small_acc)
    weights_gather.finish()
    for block in low_peers():
        up_low(block, block).wait_recv()
        for peer in high_peers():
            up_high(peer, high, block).start()
    for block in high_peers():
        down_high(block, block).wait_recv()
        for peer in low_peers():
            down_low(peer, low, block).start()

    def attention(loop):
        normed = normed_k[loop]

        def queries(expert, none):
            query = jnp.where(lane < HD, nn(normed, w_all[expert]), 0.0).astype(BF16)
            q_k[loop, pl.ds(pl.multiple_of(expert * own, own), own)] = query
            return none

        lax.fori_loop(0, n_exp, queries, 0, unroll=True)
        running = running_rows(loop)
        gates = gate_k[loop] * running
        mix[...] = jnp.zeros_like(mix)
        for k in range(1, window):

            @pl.when(active & (me >= k))
            def _():
                ref = kv_k.at[loop, me - k]
                remote(
                    ref, ref, kg_send.at[k - 1], kg_recv.at[me - k], expert=me - k
                ).wait_recv()

        kv_rows = window_keys(loop)

        def attend(pair, none):
            rows = pl.ds(pl.multiple_of(pair * 2 * own, 2 * own), 2 * own)
            scores = nt(q_k[loop, rows], kv_rows) * scale
            scores = (scores.reshape(2, own, keys) + bias[...][None]).reshape(2 * own, keys)
            powers = jnp.exp(scores - jnp.max(scores, axis=1, keepdims=True))
            prob = (powers * (1.0 / jnp.sum(powers, axis=1, keepdims=True))).astype(BF16)
            p_k[loop, rows] = prob
            outs = jnp.where(lane_two < HD, 0.0, nn(prob, kv_rows)).astype(BF16)
            o_k[loop, rows] = outs
            for half in range(2):
                expert = 2 * pair + half
                gate = column(gates, expert, route_lane)
                mix[...] += gate * nt(outs[half * own : (half + 1) * own], w_all[expert])
            return none

        lax.fori_loop(0, n_exp // 2, attend, 0, unroll=True)
        for k in range(1, window):

            @pl.when(me + k < n_act)
            def _():
                kv_copy(loop, me + k, k - 1).wait_send()

        centre = state[loop] + mix[...]
        middle[loop] = centre
        unit, _ = normalise(centre)
        second = (unit * gain_two + bias_two).astype(BF16)
        second_k[loop] = second
        rows_all[0, me] = second

    rows_gather = Gather(rows_all.at[0], ag_send, ag_recv, n_act)
    factor_gather = Gather(wrow, fg_send, fg_recv, n_act)

    def place_matrices(loop):
        ranks = rowm_ref[loop, :, 0:valid_rows]
        slot = lax.broadcasted_iota(jnp.int32, (cap, valid_rows), 0).astype(F32)
        gather_m[...] = jnp.where(slot == ranks, 1.0, 0.0).astype(BF16)
        slot = lax.broadcasted_iota(jnp.int32, (own, cap), 1).astype(F32)

        def block_matrix(block, none):
            rows = pl.ds(pl.multiple_of(block * own, own), own)
            ranks = meta_ref[loop, rows, RANK_LANE : RANK_LANE + 1]
            scatter_m[rows] = jnp.where(slot == ranks, 1.0, 0.0).astype(BF16)
            return none

        lax.fori_loop(0, n_act, block_matrix, 0)

    def scatter_rows(block):
        return scatter_m[pl.ds(pl.multiple_of(block * own, own), own)]

    def take(buf):
        return nn(gather_m[...], rows_all[buf, 0:n_act].reshape(valid_rows, width))

    def expert_rows(loop):
        rows_in = take(0).astype(BF16)
        rows_k[cap_rows(loop)] = rows_in
        allowed_lanes = (chosen_k[...] > 0.5) & (route_cap >= n_exp)
        gate = column(masked_softmax(nt(rows_in, rb[...]), allowed_lanes), n_exp + me, route_cap)
        fgate_k[cap_rows(loop)] = gate
        part_k[cap_rows(loop)] = jnp.zeros((cap, width), F32)

    root = math.sqrt(2.0 / math.pi)

    def tile_cols(tile):
        return pl.ds(pl.multiple_of(tile * TILE, TILE), TILE)

    def hidden_layer(loop):
        rows_in = rows_k[cap_rows(loop)]

        def step(tile, none):
            cols = tile_cols(tile)
            inner = nn(rows_in, up_w[:, cols])
            square = inner * inner
            curve = jnp.tanh(root * inner * (1.0 + 0.044715 * square))
            upper = 0.5 * (1.0 + curve)
            hidden = (inner * upper).astype(BF16)
            hid[cap_rows(loop), cols] = hidden
            slope = upper + 0.5 * inner * (1.0 - curve * curve) * (
                root + (3.0 * 0.044715 * root) * square
            )
            gprime[cap_rows(loop), cols] = slope.astype(BF16)
            part_k[cap_rows(loop)] += nt(hidden, down_w[:, cols])
            return none

        lax.fori_loop(0, tiles, step, 0, unroll=True)

    sums = Reduce(
        n_act,
        own,
        pair_send_two,
        pair_recv_two,
        far_send_two,
        far_recv_two,
        rs_sems_two,
        total_two,
        True,
    )
    back_sums = Reduce(
        n_act, own + EXTRA, pair_send, pair_recv, far_send, far_recv, rs_sems, total
    )

    def start_terms(loop, send):
        terms = (part_k[cap_rows(loop)] * fgate_k[cap_rows(loop)]).astype(BF16)
        sums.start(lambda block: nn(scatter_rows(block), terms), send)

    def wait_weights():
        for peer in high_peers():
            for block in range(n_low):
                up_high(peer, peer, block).wait_recv()
        for peer in low_peers():
            for block in range(n_high):
                down_low(peer, peer, block).wait_recv()

    def chances():
        chance_one = jax.nn.sigmoid(jnp.sum(state[1] * halt, axis=1, keepdims=True))
        chance_two = jax.nn.sigmoid(jnp.sum(state[2] * halt, axis=1, keepdims=True))
        return chance_one, chance_two

    def last_factor():
        chance_one, chance_two = chances()
        weight_last = (1.0 - chance_one) * (1.0 - chance_two)
        sgrad[last] = weight_last * cot_ref[...].astype(F32)
        upper = weight_last.astype(BF16).astype(F32)
        factors = jnp.where(lane == 0, upper, jnp.where(lane == 1, weight_last - upper, 0.0))
        wrow[me] = jnp.transpose(factors)[0:EXTRA].astype(BF16)
        factor_gather.start()

    carry[...] = jnp.zeros_like(carry)

    def state_grads(loop_dot):
        chance_one, chance_two = chances()
        cot = cot_ref[...].astype(F32)
        first, next_one = state[1], state[2]
        stay = 1.0 - chance_one
        weight_two = stay * chance_two
        weight_three = stay * (1.0 - chance_two)
        dot_one = jnp.sum(cot * first, axis=1, keepdims=True)
        dot_two = jnp.sum(cot * next_one, axis=1, keepdims=True)
        dot_middle = jnp.sum(cot * middle[last], axis=1, keepdims=True)
        dot_three = jnp.where(
            running_rows(last) > 0.5, weight_three * dot_middle + loop_dot, weight_three * dot_two
        )
        slope_one = chance_one * (stay * dot_one - weight_two * dot_two - dot_three)
        slope_two = chance_two * (weight_three * dot_two - dot_three)
        sgrad[0] = chance_one * cot + slope_one * halt
        sgrad[1] = weight_two * cot + slope_two * halt
        small_acc[vec_at + 4 : vec_at + 5] = jnp.sum(
            slope_one * first + slope_two * next_one, axis=0, keepdims=True
        )

    def finish_output():
        chance_one, chance_two = chances()
        first, next_one = state[1], state[2]
        final = jnp.where(running_rows(last) > 0.5, middle[last] + total_two[0:own], next_one)
        stay = 1.0 - chance_one
        out_ref[...] = (
            chance_one * first + stay * chance_two * next_one + stay * (1.0 - chance_two) * final
        )

    vec_at = 2 * HD + EXTRA

    def expert_back(loop):
        grad_rows = row_grads[...]
        gate = fgate_k[cap_rows(loop)]
        ggrad[...] = jnp.sum(grad_rows * part_k[cap_rows(loop)], axis=1, keepdims=True)
        scaled = (grad_rows * gate).astype(BF16)
        scaled_k[...] = scaled
        row_grads[...] = jnp.zeros_like(row_grads)

        def step(tile, none):
            cols = tile_cols(tile)
            inner_grad = (
                nn(scaled, down_w[:, cols]) * gprime[cap_rows(loop), cols].astype(F32)
            ).astype(BF16)
            gprime[cap_rows(loop), cols] = inner_grad
            row_grads[...] += nt(inner_grad, up_w[:, cols])
            return none

        lax.fori_loop(0, tiles, step, 0, unroll=True)
        terms = row_grads[...].astype(BF16)
        gate_grad = ggrad[...]
        upper = gate_grad.astype(BF16).astype(F32)
        spread = jnp.where(lane_cap == n_exp + me, upper, 0.0) + jnp.where(
            lane_cap == me, gate_grad - upper, 0.0
        )
        spread_t = jnp.transpose(spread)[0:EXTRA].astype(BF16)

        def row_terms(block):
            matrix = scatter_rows(block)
            grads = nt(spread_t, matrix)
            return jnp.concatenate(
                [
                    nn(matrix, terms),
                    jnp.concatenate([grads, jnp.zeros((EXTRA, width - own), F32)], axis=1),
                ],
                axis=0,
            )

        back_sums.start(row_terms, True)

    def expert_weights(loop):
        rows_in = rows_k[cap_rows(loop)]
        scaled = scaled_k[...]

        def step(tile, none):
            cols = tile_cols(tile)
            down_acc[:, cols] += tn(scaled, hid[cap_rows(loop), cols])
            up_acc[:, cols] += tn(rows_in, gprime[cap_rows(loop), cols])
            return none

        lax.fori_loop(0, tiles, step, 0, unroll=True)

    def order_at(source, receiver, count):
        return lax.rem(source - receiver + count, count) - 1

    spare = width // shard

    def up_grad_first(peer, slot, block, receiver):
        return remote(
            hid.at[shard_rows(block * n_low + peer)],
            u_first.at[order_at(slot, receiver, n_low), shard_rows(block)],
            ug_send.at[peer, block],
            ug_recv.at[slot, block],
            dp=high * n_low + peer,
        )

    def up_grad_second(peer, slot, receiver):
        return remote(
            hid.at[shard_rows(spare + peer)],
            u_last.at[order_at(slot, receiver, n_high)],
            ug_send_two.at[peer],
            ug_recv_two.at[slot],
            dp=peer * n_low + low,
        )

    def down_grad_first(peer, slot, block, receiver):
        return remote(
            gprime.at[shard_rows(peer * n_low + block)],
            d_first.at[order_at(slot, receiver, n_high), shard_rows(block)],
            dg_send.at[peer, block],
            dg_recv.at[slot, block],
            dp=peer * n_low + low,
        )

    def down_grad_second(peer, slot, receiver):
        return remote(
            gprime.at[shard_rows(spare + peer)],
            d_last.at[order_at(slot, receiver, n_low)],
            dg_send_two.at[peer],
            dg_recv_two.at[slot],
            dp=high * n_low + peer,
        )

    def send_expert_weights():
        hid[0:width] = up_acc[...].astype(BF16)
        for peer in low_peers():
            for block in high_peers():
                up_grad_first(peer, low, block, peer).start()
        gprime[0:width] = down_acc[...].astype(BF16)
        for peer in high_peers():
            for block in low_peers():
                down_grad_first(peer, high, block, peer).start()
        for peer in low_peers():
            up_grad_first(peer, low, high, peer).start()
        for peer in high_peers():
            down_grad_first(peer, high, low, peer).start()

    def pass_expert_weights():
        for block in high_peers():
            added = up_acc[shard_rows(block * n_low + low)]
            for peer in low_peers():
                up_grad_first(peer, peer, block, low).wait_recv()
                added = added + u_first[
                    order_at(peer, low, n_low), shard_rows(block)
                ].astype(F32)
            hid[shard_rows(spare + block)] = added.astype(BF16)
            up_grad_second(block, high, block).start()
        for block in low_peers():
            added = down_acc[shard_rows(high * n_low + block)]
            for peer in high_peers():
                down_grad_first(peer, peer, block, high).wait_recv()
                added = added + d_first[
                    order_at(peer, high, n_high), shard_rows(block)
                ].astype(F32)
            gprime[shard_rows(spare + block)] = added.astype(BF16)
            down_grad_second(block, low, block).start()

    def finish_expert_weights():
        added = up_acc[shard_rows(dp)]
        for peer in low_peers():
            up_grad_first(peer, peer, high, low).wait_recv()
            added = added + u_first[order_at(peer, low, n_low), shard_rows(high)].astype(F32)
        for peer in high_peers():
            up_grad_second(peer, peer, high).wait_recv()
            added = added + u_last[order_at(peer, high, n_high)].astype(F32)
        ugrad_ref[...] = added
        added = down_acc[shard_rows(dp)]
        for peer in high_peers():
            down_grad_first(peer, peer, low, high).wait_recv()
            added = added + d_first[order_at(peer, high, n_high), shard_rows(low)].astype(F32)
        for peer in low_peers():
            down_grad_second(peer, peer, low).wait_recv()
            added = added + d_last[order_at(peer, low, n_low)].astype(F32)
        dgrad_ref[...] = added

    attn_sums = Reduce(
        n_exp,
        2 * HD,
        pair_send_two,
        pair_recv_two,
        far_send_two,
        far_recv_two,
        a_sems,
        total_two,
    )

    def dkv_copy(distance, owner):
        return remote(
            dkv_send.at[jnp.clip(owner - win_at, 0, window - 1)],
            dkv_recv.at[distance - 1],
            dk_send.at[distance - 1],
            dk_recv.at[distance - 1],
            expert=owner,
        )

    def attention_back(loop, step):
        info = meta_ref[loop, own_rows, 0 : 2 * n_exp]
        running = running_rows(loop)
        branch = (sgrad[loop] + carry[...]) * running
        second_grad = total[0:own]
        gate_rows = total[own : own + n_exp, 0:own] + total[own + n_exp : own + 2 * n_exp, 0:own]
        gate_rows = jnp.concatenate(
            [jnp.zeros((n_exp, own), F32), gate_rows, jnp.zeros((LANES - 2 * n_exp, own), F32)],
            axis=0,
        )
        gate_grads = jnp.transpose(gate_rows)[:, 0 : 2 * n_exp]
        second = second_k[loop]
        gates = masked_softmax(nt(second, rb[...]), (info > 0.5) & (route_lane >= n_exp))
        loop_dot = jnp.sum(gates * gate_grads, axis=1, keepdims=True)
        logit_grad = (gates * (gate_grads - loop_dot)).astype(BF16)
        second_grad = second_grad + nn(logit_grad, rb[...])
        unit, inverse = normalise(middle[loop])
        middle_grad = norm_back(second_grad, unit, inverse, gain_two) + branch
        mgrad[...] = middle_grad

        gates = gate_k[loop]
        kv_rows = window_keys(loop)
        dkv_t[...] = jnp.zeros_like(dkv_t)

        def scores_back(pair, none):
            rows = pl.ds(pl.multiple_of(pair * 2 * own, 2 * own), 2 * own)
            out_grads = []
            for half in range(2):
                expert = 2 * pair + half
                part_grad = (column(gates, expert, route_lane) * mgrad[...]).astype(BF16)
                out_grads.append(
                    jnp.where(lane < HD, 0.0, nn(part_grad, w_all[expert])).astype(BF16)
                )
            out_grad = jnp.concatenate(out_grads, axis=0)
            prob_low = p_k[loop, rows]
            prob = prob_low.astype(F32)
            prob_grad = nt(out_grad, kv_rows)
            centre = jnp.sum(prob * prob_grad, axis=1, keepdims=True)
            score_grad = (prob * (prob_grad - centre)).astype(BF16)
            ds_k[rows] = score_grad
            dkv_t[...] += tn(q_k[loop, rows], score_grad) * scale + tn(out_grad, prob_low)
            return none

        lax.fori_loop(0, n_exp // 2, scores_back, 0, unroll=True)
        for block in range(window):
            grads = jnp.transpose(dkv_t[:, block * own : (block + 1) * own])
            dkv[block] = grads
            dkv_send[block] = grads.astype(BF16)
        for distance in range(1, window):

            @pl.when(active & (me >= distance))
            def _():
                dkv_copy(distance, me - distance).start()

        @pl.when(step == last)
        def _():
            state_grads(loop_dot)
            sums.send((1, 0))

        @pl.when(step == last + 1)
        def _():
            sums.send((3, 1))

        small_acc[2 * HD : vec_at] += tn(logit_grad, second)
        small_acc[vec_at + 2 : vec_at + 3] += jnp.sum(second_grad * unit, axis=0, keepdims=True)
        small_acc[vec_at + 3 : vec_at + 4] += jnp.sum(second_grad, axis=0, keepdims=True)
        normed = normed_k[loop]
        mix[...] = jnp.zeros_like(mix)
        dga[...] = jnp.zeros_like(dga)

        def queries_back(pair, none):
            rows = pl.ds(pl.multiple_of(pair * 2 * own, 2 * own), 2 * own)
            outs = o_k[loop, rows]
            query_grad = jnp.where(lane_two < HD, nn(ds_k[rows], kv_rows) * scale, 0.0).astype(BF16)
            for half in range(2):
                expert = 2 * pair + half
                cut = slice(half * own, (half + 1) * own)
                middle_grad = mgrad[...]
                dot = jnp.sum(middle_grad * nt(outs[cut], w_all[expert]), axis=1, keepdims=True)
                dga[...] += jnp.where(route_lane == expert, dot, 0.0)
                part_grad = (column(gates, expert, route_lane) * middle_grad).astype(BF16)
                attn_acc[expert] += tn(query_grad[cut], normed) + tn(outs[cut], part_grad)
                mix[...] += nt(query_grad[cut], w_all[expert])
            return none

        lax.fori_loop(0, n_exp // 2, queries_back, 0)

        @pl.when(loop == 0)
        def _():
            attn_sums.start(lambda block: attn_acc[block], False)

        gate_grads = dga[...]
        logit_grad = (
            gates * (gate_grads - jnp.sum(gates * gate_grads, axis=1, keepdims=True))
        ).astype(BF16)
        small_acc[2 * HD : vec_at] += tn(logit_grad, normed)
        normed_grad = mix[...] + nn(logit_grad, rb[...])
        unit, inverse = normalise(state[loop])

        own_block = jnp.clip(me - win_at, 0, window - 1)
        dkv[window] = jnp.where(active, dkv[own_block], 0.0)
        for distance in range(1, window):

            @pl.when(me + distance < n_act)
            def _():
                remote(
                    dkv_send.at[0],
                    dkv_recv.at[distance - 1],
                    dk_send.at[distance - 1],
                    dk_recv.at[distance - 1],
                    expert=me + distance,
                ).wait_recv()
                dkv[window] += dkv_recv[distance - 1].astype(F32)

        for distance in range(1, window):

            @pl.when(active & (me >= distance))
            def _():
                dkv_copy(distance, me - distance).wait_send()

        kv_grad = dkv[window].astype(BF16)
        small_acc[0 : 2 * HD] += tn(kv_grad, normed)
        normed_grad = normed_grad + nt(kv_grad, kvb[...])
        small_acc[vec_at : vec_at + 1] += jnp.sum(normed_grad * unit, axis=0, keepdims=True)
        small_acc[vec_at + 1 : vec_at + 2] += jnp.sum(normed_grad, axis=0, keepdims=True)
        carry[...] = (
            (sgrad[loop] + carry[...]) * (1.0 - running)
            + mgrad[...]
            + norm_back(normed_grad, unit, inverse, gain_one)
        )

    def phase(step, none):
        loop = jnp.where(step <= last, step, 2 * last - step)

        @pl.when(step <= last)
        def _():
            attention(loop)

        @pl.when(step == 2 * last)
        def _():
            sums.finish()
            finish_output()

        @pl.when(step > last)
        def _():
            rows_all[0, me] = ((sgrad[loop] + carry[...]) * running_rows(loop)).astype(BF16)

        rows_gather.start()
        place_matrices(loop)

        @pl.when(step <= last)
        def _():
            chosen_k[...] = nn(
                gather_m[...], meta_ref[loop, 0:valid_rows, 0 : 2 * n_exp].astype(BF16)
            )

        @pl.when(step == 0)
        def _():
            wait_weights()

        @pl.when(step == last)
        def _():
            cot_gather.finish()
            factor_gather.finish()

        rows_gather.finish()

        @pl.when(step == 0)
        def _():
            cot_gather.send(0)
            cot_gather.send(1)

        @pl.when(step == 1)
        def _():
            cot_gather.send(3)

        @pl.when(step <= last)
        def _():
            expert_rows(loop)
            hidden_layer(loop)

        @pl.when(step == last + 1)
        def _():
            sums.send((2, 1))

        @pl.when(step >= last)
        def _():
            factors = nt(
                gather_m[...], jnp.concatenate([wrow[block] for block in range(n_act)], axis=1)
            )
            factor = jnp.where(step == last, factors[:, 0:1] + factors[:, 1:2], 1.0)
            row_grads[...] = take(jnp.where(step == last, 1, 0)) * factor
            expert_back(loop)

        @pl.when(step <= last)
        def _():
            start_terms(loop, step < last)

        @pl.when(step < last)
        def _():
            sums.finish()
            state[loop + 1] = jnp.where(
                running_rows(loop) > 0.5, middle[loop] + total_two[0:own], state[loop]
            )
            prepare(loop + 1)

        @pl.when(step == last - 1)
        def _():
            last_factor()

        @pl.when(step >= last)
        def _():
            expert_weights(loop)

            @pl.when(step == 2 * last)
            def _():
                send_expert_weights()

            back_sums.finish()

            @pl.when(step == last)
            def _():
                sums.send((2, 0))

            @pl.when(step == last + 1)
            def _():
                sums.send((3, 0), (1, 1))

            attention_back(loop, step)

        return none

    lax.fori_loop(0, 2 * last + 1, phase, 0)
    xgrad_ref[...] = carry[...]

    chunk = small_acc.shape[0] // n_exp
    small_sums = Reduce(
        n_exp, chunk, s_pair_send, s_pair_recv, s_far_send, s_far_recv, s_sems, s_total
    )
    small_sums.start(
        lambda block: small_acc[pl.ds(pl.multiple_of(block * chunk, chunk), chunk)], True
    )
    attn_sums.send((1, 0), (3, 0), (2, 0))

    def attn_copy(peer, slot):
        return remote(
            a_stage.at[shard_rows(peer)],
            a_recv.at[shard_rows(slot)],
            t_send.at[1, peer],
            t_recv.at[1, slot],
            dp=peer,
        )

    def small_copy(peer, slot):
        return remote(
            s_dp.at[slot], s_dp.at[slot], t_send.at[0, peer], t_recv.at[0, slot], dp=peer
        )

    small_sums.finish()
    s_dp[dp] = s_total[...].astype(BF16)
    each_peer(lambda peer: small_copy(peer, dp).start())
    pass_expert_weights()
    attn_sums.finish()
    a_total[...] = jnp.transpose(total_two[...])
    a_stage[...] = a_total[...].astype(BF16)
    each_peer(lambda peer: attn_copy(peer, dp).start())
    each_peer(lambda peer: small_copy(peer, peer).wait_recv())
    s_total[...] = jnp.zeros_like(s_total)

    def add_small(index, none):
        s_total[...] += s_dp[index].astype(F32)
        return none

    lax.fori_loop(0, n_dp, add_small, 0)
    s_all[me] = s_total[...]
    small_gather = Gather(s_all, sg_send, sg_recv, n_exp)
    small_gather.start()
    agrad_ref[...] = a_total[shard_rows(dp)]

    def add_attn(peer):
        attn_copy(peer, peer).wait_recv()
        agrad_ref[...] += a_recv[shard_rows(peer)].astype(F32)

    each_peer(add_attn)
    finish_expert_weights()
    small_gather.finish()
    small = s_all[...].reshape(n_exp * chunk, width)
    kvgrad_ref[...] = jnp.transpose(small[0 : 2 * HD])
    rgrad_ref[...] = small[2 * HD : vec_at]
    vgrad_ref[...] = small[vec_at : vec_at + 8]

    def sent(peer):
        attn_weight_copy(peer, dp).wait_send()
        small_copy(peer, dp).wait_send()
        attn_copy(peer, dp).wait_send()

    each_peer(sent)
    for peer in low_peers():
        up_low(peer, low).wait_send()
        down_grad_second(peer, low, peer).wait_send()
        for block in range(n_high):
            down_low(peer, low, block).wait_send()
            up_grad_first(peer, low, block, peer).wait_send()
    for peer in high_peers():
        down_high(peer, high).wait_send()
        for block in range(n_low):
            up_high(peer, high, block).wait_send()
            down_grad_first(peer, high, block, peer).wait_send()
        up_grad_second(peer, high, peer).wait_send()


def adam_kernel(*refs):
    out_in, xgrad_in, ugrad, dgrad, agrad, kvgrad, rgrad, vgrad = refs[:8]
    shared, kv, router, attn, up, down = (refs[8 + 3 * index : 11 + 3 * index] for index in range(6))
    out, xgrad = refs[26:28]
    shared_out, kv_out, router_out, attn_out, up_out, down_out = (
        refs[28:31],
        refs[31:34],
        refs[34:37],
        refs[37:41],
        refs[41:45],
        refs[45:49],
    )

    def update(sources, grad, results, rate, decay):
        values = adam_update(*(source[...] for source in sources), grad, rate, decay)
        for result, value in zip(results, values):
            result[...] = value
        if len(results) > 3:
            results[3][...] = values[0].astype(BF16)

    out[...] = out_in[...]
    xgrad[...] = xgrad_in[...]
    update(up, ugrad[...], up_out, 14.0 / math.sqrt(D), decay_rate)
    update(down, dgrad[...], down_out, 17.0 / math.sqrt(FF), decay_rate)

    @pl.when(pl.program_id(0) == 0)
    def _():
        row = lax.broadcasted_iota(jnp.int32, shared[0].shape, 0)
        rates = jnp.where(row < 4, 6.0, 20.0 / math.sqrt(D))
        update(shared, vgrad[0 : shared[0].shape[0]], shared_out, rates, 0.0)
        update(kv, kvgrad[...], kv_out, 20.0 / math.sqrt(D), decay_rate)
        update(router, rgrad[...], router_out, 50.0 / math.sqrt(3 * D), decay_rate)
        lane = lax.broadcasted_iota(jnp.int32, attn[0].shape, 1)
        rates = jnp.where(lane < HD, 25.0 / math.sqrt(D), 50.0 / math.sqrt(HD))
        update(attn, agrad[...], attn_out, rates, decay_rate)


def dp_grid(n_dp):
    n_low = 1
    while n_low * n_low * 4 <= n_dp:
        n_low *= 2
    return n_low, n_dp // n_low


def per_device(
    block_input,
    cotangent,
    lengths,
    run_loops,
    attn_routes,
    ffn_routes,
    shared_vectors,
    shared_moment,
    shared_second,
    key_value,
    kv_moment,
    kv_second,
    router_weights,
    router_moment,
    router_second,
    attn_weights,
    attn_moment,
    attn_second,
    up_weights,
    up_moment,
    up_second,
    down_weights,
    down_moment,
    down_second,
):
    n_exp = lax.axis_size("expert")
    n_dp = lax.axis_size("dp")
    own, width = block_input.shape
    slots = run_loops.shape[0]
    shard = attn_weights.shape[1]
    hidden = up_weights.shape[2]
    cap = 5 * slots * KFF // (4 * n_exp)
    n_act = FILLED // own
    window = min(n_act, MAXLEN // own + 1)
    pairs = n_exp // 2
    valid_rows = n_act * own
    n_low, n_high = dp_grid(n_dp)

    small_rows = 32 * n_exp
    vmem = pltpu.VMEM
    dma = pltpu.SemaphoreType.DMA
    block = (pairs, own + EXTRA, width)
    small_block = (pairs, 32, width)
    scratch = [
        vmem((LOOPS, slots, INFO), F32),
        vmem((LOOPS + 1, 1, slots), F32),
        vmem((width, 2 * HD), BF16),
        vmem((2 * n_exp, width), BF16),
        vmem((n_exp, width, 2 * HD), BF16),
        vmem((width, hidden), BF16),
        vmem((width, hidden), BF16),
        vmem((width, hidden), F32),
        vmem((width, hidden), F32),
        vmem((n_exp, 2 * HD, width), F32),
        vmem((small_rows, width), F32),
        vmem((LOOPS, own, width), F32),
        vmem((LOOPS, own, width), F32),
        vmem((LOOPS, own, width), BF16),
        vmem((LOOPS, own, width), BF16),
        vmem((LOOPS, n_exp, own, 2 * HD), BF16),
        vmem((LOOPS, n_exp * own, 2 * HD), BF16),
        vmem((LOOPS, n_exp * own, 2 * HD), BF16),
        vmem((LOOPS, n_exp * own, window * own), BF16),
        vmem((n_exp * own, window * own), BF16),
        vmem((own, window * own), F32),
        vmem((own, width), F32),
        vmem((own, 2 * n_exp), F32),
        vmem((2 * HD, window * own), F32),
        vmem((window + 1, own, 2 * HD), F32),
        vmem((LOOPS, own, 2 * n_exp), F32),
        vmem((2, n_exp, own, width), BF16),
        vmem((n_exp, EXTRA, own), BF16),
        vmem((cap, valid_rows), BF16),
        vmem((valid_rows, cap), BF16),
        vmem((LOOPS * cap, width), BF16),
        vmem((LOOPS * cap, hidden), BF16),
        vmem((LOOPS * cap, hidden), BF16),
        vmem((cap, width), F32),
        vmem((LOOPS * cap, width), F32),
        vmem((LOOPS * cap, 1), F32),
        vmem((cap, 2 * n_exp), F32),
        vmem((cap, 1), F32),
        vmem((cap, width), BF16),
        vmem((LOOPS, own, width), F32),
        vmem((own, width), F32),
        vmem((own, width), F32),
        vmem((own + EXTRA, width), F32),
        vmem((own, width), F32),
        vmem(block, BF16),
        vmem(block, BF16),
        vmem(block, BF16),
        vmem(block, BF16),
        vmem((pairs, own, width), BF16),
        vmem((pairs, own, width), BF16),
        vmem((pairs, own, width), BF16),
        vmem((pairs, own, width), BF16),
        vmem((window, own, 2 * HD), BF16),
        vmem((window, own, 2 * HD), BF16),
        vmem((n_low - 1, n_high * shard, hidden), BF16),
        vmem((n_high - 1, shard, hidden), BF16),
        vmem((n_high - 1, n_low * shard, hidden), BF16),
        vmem((n_low - 1, shard, hidden), BF16),
        vmem((width, 2 * HD), F32),
        vmem((width, 2 * HD), BF16),
        vmem((width, 2 * HD), BF16),
        vmem(small_block, BF16),
        vmem(small_block, BF16),
        vmem(small_block, BF16),
        vmem(small_block, BF16),
        vmem((32, width), F32),
        vmem((n_dp, 32, width), BF16),
        vmem((n_exp, 32, width), F32),
        dma((2,)),
        dma((n_dp,)),
        dma((n_dp,)),
        dma((n_low,)),
        dma((n_dp,)),
        dma((n_high, n_low)),
        dma((n_high,)),
        dma((n_dp,)),
        dma((n_low, n_high)),
        dma((2 * pairs,)),
        dma((n_exp,)),
        dma((2 * pairs,)),
        dma((n_exp,)),
        dma((2 * pairs,)),
        dma((n_exp,)),
        dma((2 * pairs,)),
        dma((n_exp,)),
        dma((2 * pairs,)),
        dma((n_exp,)),
        dma((window,)),
        dma((n_exp,)),
        dma((4, pairs)),
        dma((6, pairs)),
        dma((4, pairs)),
        dma((4, pairs)),
        dma((window,)),
        dma((window,)),
        dma((n_low, n_high)),
        dma((n_low, n_high)),
        dma((n_high,)),
        dma((n_high,)),
        dma((n_high, n_low)),
        dma((n_high, n_low)),
        dma((n_low,)),
        dma((n_low,)),
        dma((2, n_dp)),
        dma((2, n_dp)),
    ]
    whole = pl.BlockSpec(memory_space=pltpu.VMEM)
    scalars = pl.BlockSpec(memory_space=pltpu.SMEM)
    outside = pl.BlockSpec(memory_space=pl.ANY)
    shape = jax.ShapeDtypeStruct
    sums = pl.pallas_call(
        functools.partial(block_kernel, n_exp, n_dp, n_act, cap),
        out_shape=(
            shape((own, width), F32),
            shape((own, width), F32),
            shape((shard, hidden), F32),
            shape((shard, hidden), F32),
            shape((shard, 2 * HD), F32),
            shape((width, 2 * HD), F32),
            shape((2 * n_exp, width), F32),
            shape((8, width), F32),
        ),
        in_specs=[whole, whole, scalars, *([whole] * 7), outside, outside],
        out_specs=[whole] * 8,
        scratch_shapes=scratch,
        compiler_params=pltpu.CompilerParams(
            collective_id=0, has_side_effects=True, vmem_limit_bytes=63 * 1024 * 1024
        ),
        name="block",
    )(
        block_input,
        cotangent,
        lengths,
        run_loops[None],
        attn_routes.transpose(0, 2, 1),
        ffn_routes.transpose(0, 2, 1),
        shared_vectors,
        key_value,
        router_weights.T,
        attn_weights[0],
        up_weights[0],
        down_weights[0],
    )

    steps = max(1, shard // 64)
    rows = shard // steps

    def by_rows(array):
        return pl.BlockSpec((array.shape[0] // steps, array.shape[1]), lambda step: (step, 0))

    def fixed(array):
        return pl.BlockSpec(array.shape, lambda step: (0, 0))

    output, input_grad, up_sum, down_sum, *small = sums
    small_args = [
        shared_vectors,
        shared_moment,
        shared_second,
        key_value,
        kv_moment,
        kv_second,
        router_weights.T,
        router_moment.T,
        router_second.T,
        attn_weights[0],
        attn_moment[0],
        attn_second[0],
    ]
    large_args = [
        up_weights[0],
        up_moment[0],
        up_second[0],
        down_weights[0],
        down_moment[0],
        down_second[0],
    ]
    attn_low = shape((shard, 2 * HD), BF16)
    large_low = shape((shard, hidden), BF16)
    like = [shape(array.shape, array.dtype) for array in small_args]
    big = [shape(array.shape, array.dtype) for array in large_args]
    outs = [
        shape(output.shape, F32),
        shape(input_grad.shape, F32),
        *like,
        attn_low,
        *big[:3],
        large_low,
        *big[3:],
        large_low,
    ]
    results = pl.pallas_call(
        adam_kernel,
        grid=(steps,),
        out_shape=outs,
        in_specs=[
            by_rows(output),
            by_rows(input_grad),
            by_rows(up_sum),
            by_rows(down_sum),
            *(fixed(array) for array in small),
            *(fixed(array) for array in small_args),
            *(by_rows(array) for array in large_args),
        ],
        out_specs=[
            by_rows(output),
            by_rows(input_grad),
            *(fixed(array) for array in (*like, attn_low)),
            *(by_rows(array) for array in (*big[:3], large_low, *big[3:], large_low)),
        ],
        compiler_params=pltpu.CompilerParams(vmem_limit_bytes=63 * 1024 * 1024),
        name="adamw",
    )(*sums, *small_args, *large_args)
    output, input_grad, *rest = results
    shared_kv, router, weights = rest[:6], rest[6:9], rest[9:]
    return (
        output,
        input_grad,
        *shared_kv,
        *(array.T for array in router),
        *(array[None] for array in weights),
    )


def solution(mesh):
    rows = P(("dp", "expert"), None)
    weights = P("expert", "dp", None)
    return jax.shard_map(
        per_device,
        mesh=mesh,
        in_specs=(
            rows,
            rows,
            P("dp", None),
            P("dp"),
            P(None, "dp", None),
            P(None, "dp", None),
            *([P()] * 9),
            *([weights] * 9),
        ),
        out_specs=(rows, rows, *([P()] * 9), *([weights] * 12)),
        check_vma=False,
    )
```

```python
import functools
import math

import jax
import jax.numpy as jnp
from jax import lax
from jax.experimental import pallas as pl
from jax.experimental.pallas import tpu as pltpu
from jax.sharding import PartitionSpec as P

D = 512
HD = 64
FF = 2048
KATT = 4
KFF = 2
LOOPS = 3
STEP = 10
MAXLEN = 512
FILLED = 896

ln_eps = 1e-05
beta_one = 0.9
beta_two = 0.999
adam_eps = 1e-08
decay_rate = 0.01
masked_score = -1e30

F32 = jnp.float32
BF16 = jnp.bfloat16
MESH = pl.DeviceIdType.MESH
LANES = 128
RANK_LANE = 16
RUN_LANE = 17
SEG_LANE = 18
INFO = 32
TILE = 512
EXTRA = 16


def nn(left, right):
    return lax.dot_general(left, right, (((1,), (0,)), ((), ())), preferred_element_type=F32)


def nt(left, right):
    return lax.dot_general(left, right, (((1,), (1,)), ((), ())), preferred_element_type=F32)


def tn(left, right):
    return lax.dot_general(left, right, (((0,), (0,)), ((), ())), preferred_element_type=F32)


def normalise(values):
    centre = values - jnp.mean(values, axis=-1, keepdims=True)
    inverse = lax.rsqrt(jnp.mean(centre * centre, axis=-1, keepdims=True) + ln_eps)
    return centre * inverse, inverse


def norm_back(grad, unit, inverse, gain):
    scaled = grad * gain
    first = jnp.mean(scaled, axis=-1, keepdims=True)
    second = jnp.mean(scaled * unit, axis=-1, keepdims=True)
    return inverse * (scaled - first - unit * second)


def masked_softmax(logits, valid):
    top = jnp.max(jnp.where(valid, logits, masked_score), axis=-1, keepdims=True)
    powers = jnp.where(valid, jnp.exp(jnp.where(valid, logits - top, 0.0)), 0.0)
    return powers / jnp.maximum(jnp.sum(powers, axis=-1, keepdims=True), 0.5)


def adam_update(weight, moment, second, grad, rate, decay):
    moment_new = beta_one * moment + (1.0 - beta_one) * grad
    second_new = beta_two * second + (1.0 - beta_two) * grad * grad
    moment_hat = moment_new * (1.0 / (1.0 - beta_one**STEP))
    second_hat = second_new * (1.0 / (1.0 - beta_two**STEP))
    weight_new = weight - rate * (moment_hat / (jnp.sqrt(second_hat) + adam_eps) + decay * weight)
    return (weight_new, moment_new, second_new)


def block_kernel(
    n_exp,
    n_dp,
    n_act,
    cap,
    x_ref,
    cot_ref,
    len_ref,
    run_ref,
    ar_ref,
    fr_ref,
    vec_ref,
    kvw_ref,
    rw_ref,
    aw_ref,
    uw_hbm,
    dw_hbm,
    out_ref,
    xgrad_ref,
    ugrad_ref,
    dgrad_ref,
    agrad_ref,
    kvgrad_ref,
    rgrad_ref,
    vgrad_ref,
    meta_ref,
    rowm_ref,
    kvb,
    rb,
    w_all,
    up_w,
    down_w,
    up_acc,
    down_acc,
    attn_acc,
    small_acc,
    state,
    middle,
    normed_k,
    second_k,
    kv_k,
    q_k,
    o_k,
    p_k,
    ds_k,
    bias,
    mix,
    dga,
    dkv_t,
    dkv,
    gate_k,
    rows_all,
    wrow,
    gather_m,
    scatter_m,
    rows_k,
    hid,
    gprime,
    row_grads,
    part_k,
    fgate_k,
    chosen_k,
    ggrad,
    scaled_k,
    sgrad,
    carry,
    mgrad,
    total,
    total_two,
    g_blocks,
    g_pair_recv,
    g_far_recv,
    g_total,
    blocks_one,
    pair_recv,
    far_recv,
    blocks_two,
    pair_recv_two,
    far_recv_two,
    dkv_send,
    dkv_recv,
    u_first,
    u_last,
    d_first,
    d_last,
    a_total,
    a_stage,
    a_recv,
    s_blocks,
    s_pair_recv,
    s_far_recv,
    s_total,
    s_dp,
    s_all,
    in_sems,
    w_send,
    w_recv,
    uw_send,
    uw_recv,
    uw_send_two,
    dw_send,
    dw_recv,
    dw_send_two,
    ag_send,
    ag_recv,
    bg_send,
    bg_recv,
    fg_send,
    fg_recv,
    wg_send,
    wg_recv,
    sg_send,
    sg_recv,
    kg_send,
    kg_recv,
    rs_sems,
    g_sems,
    rs_sems_two,
    s_sems,
    a_sems,
    dk_send,
    dk_recv,
    ug_send,
    ug_recv,
    ug_send_two,
    ug_recv_two,
    dg_send,
    dg_recv,
    dg_send_two,
    dg_recv_two,
    t_send,
    t_recv,
):
    me = lax.axis_index("expert")
    dp = lax.axis_index("dp")
    pairs = n_exp // 2
    core = lax.rem(me, 2)
    chip = lax.div(me, 2)
    sibling = 2 * chip + 1 - core
    n_low, n_high = dp_grid(n_dp)
    high = lax.div(dp, n_low)
    low = lax.rem(dp, n_low)
    own = x_ref.shape[0]
    width = x_ref.shape[1]
    slots = run_ref.shape[1]
    shard = aw_ref.shape[0]
    hidden_units = up_w.shape[1]
    tiles = hidden_units // TILE
    valid_rows = n_act * own
    window = min(n_act, MAXLEN // own + 1)
    keys = window * own
    win_at = jnp.clip(me - (window - 1), 0, n_act - window)
    scale = HD ** (-0.5)
    active = me < n_act
    last = LOOPS - 1

    def remote(src, dst, send, recv, **where):
        return pltpu.make_async_remote_copy(
            src_ref=src,
            dst_ref=dst,
            send_sem=send,
            recv_sem=recv,
            device_id=where,
            device_id_type=MESH,
        )

    def shard_rows(index, count=1):
        return pl.ds(pl.multiple_of(index * shard, shard), count * shard)

    def each_peer(body):
        def step(k, none):
            body(lax.rem(dp + k, n_dp))
            return none

        lax.fori_loop(1, n_dp, step, 0)

    def high_peers():
        return [lax.rem(high + k, n_high) for k in range(1, n_high)]

    def low_peers():
        return [lax.rem(low + k, n_low) for k in range(1, n_low)]

    class Gather:
        def __init__(self, buf, send, recv, count, parts=1):
            self.buf, self.sent, self.got, self.count = buf, send, recv, count
            self.parts, self.rows = parts, buf.shape[1] // parts

        def copy(self, block, sem, where, part):
            ref = self.buf.at[block]
            if self.parts > 1:
                ref = self.buf.at[block, pl.ds(part * self.rows, self.rows)]
            return remote(
                ref, ref, self.sent.at[part, sem], self.got.at[part, block], expert=where
            )

        def start(self):
            for part in range(self.parts):
                self.start_part(part)

        def start_part(self, part):
            for k in (*range(pairs - 1, 0, -2), *range(pairs - 2, 0, -2)):
                self.send(k, part)
            self.send(0, part)

        def send(self, k, part=0):
            zz = lax.rem(chip + k, pairs)

            @pl.when(me < self.count)
            def _():
                self.copy(me, zz, 2 * zz + core if k else sibling, part).start()

        def finish(self):
            for part in range(self.parts):
                for k in (*range(1, pairs, 2), *range(2, pairs, 2)):
                    zz = lax.rem(chip + k, pairs)
                    src = 2 * zz + core

                    @pl.when(src < self.count)
                    def _():
                        self.copy(src, zz, src, part).wait_recv()
                        self.copy(src, pairs + zz, sibling, part).start()

            for part in range(self.parts):
                for k in range(pairs):
                    zz = lax.rem(chip + k, pairs)
                    src = 2 * zz + 1 - core

                    @pl.when(src < self.count)
                    def _():
                        self.copy(src, zz, sibling, part).wait_recv()

            for part in range(self.parts):

                @pl.when(me < self.count)
                def _():
                    for k in range(1, pairs):
                        zz = lax.rem(chip + k, pairs)
                        self.copy(me, zz, 2 * zz + core, part).wait_send()
                    self.copy(me, chip, sibling, part).wait_send()

                for k in range(1, pairs):
                    zz = lax.rem(chip + k, pairs)
                    src = 2 * zz + core

                    @pl.when(src < self.count)
                    def _():
                        self.copy(src, pairs + zz, sibling, part).wait_send()

    class Reduce:
        def __init__(self, count, cuts, blocks, precv, frecv, sems, result):
            rows = sum(cuts)
            self.count, self.rows, self.part = count, rows, pl.ds(0, rows)
            self.cuts = [pl.ds(sum(cuts[:at]), size) for at, size in enumerate(cuts)]
            self.blocks, self.precv, self.frecv = blocks, precv, frecv
            self.sems, self.result = sems, result

        def pair_copy(self, zz):
            return remote(
                self.blocks.at[2 * zz + 1 - core, self.part],
                self.precv.at[zz, self.part],
                self.sems.at[0, zz],
                self.sems.at[1, zz],
                expert=sibling,
            )

        def far_copy(self, zz, slot, part):
            return remote(
                self.blocks.at[2 * zz + core, self.cuts[part]],
                self.frecv.at[slot, self.cuts[part]],
                self.sems.at[2 + 2 * part, zz],
                self.sems.at[3 + 2 * part, slot],
                expert=2 * zz + core,
            )

        def start(self, send):
            self.start_pairs()
            self.start_far(send)

        def start_pairs(self):
            for k in (*range(pairs - 1, 0, -1), 0):
                zz = lax.rem(chip + k, pairs)

                @pl.when(2 * zz + 1 - core < self.count)
                def _():
                    self.pair_copy(zz).start()

        def start_far(self, send):
            for k in range(pairs - 1, 0, -1):
                zz = lax.rem(chip + k, pairs)
                block = 2 * zz + core

                @pl.when(block < self.count)
                def _():
                    self.pair_copy(zz).wait_recv()
                    for part, cut in enumerate(self.cuts):
                        self.blocks[block, cut] = (
                            self.blocks[block, cut].astype(F32) + self.precv[zz, cut].astype(F32)
                        ).astype(BF16)
                        if isinstance(send, bool):
                            if send:
                                self.far_copy(zz, chip, part).start()
                        else:
                            pl.when(send)(self.far_copy(zz, chip, part).start)

            @pl.when(me < self.count)
            def _():
                self.pair_copy(chip).wait_recv()
                self.result[self.part] = self.blocks[me, self.part].astype(F32) + self.precv[
                    chip, self.part
                ].astype(F32)

            @pl.when(me >= self.count)
            def _():
                self.result[self.part] = jnp.zeros((self.rows, self.result.shape[1]), F32)

        def send(self, *parts):
            for k, part in parts:
                zz = lax.rem(chip + k, pairs)

                @pl.when(2 * zz + core < self.count)
                def _():
                    self.far_copy(zz, chip, part).start()

        def finish(self):
            for part in range(len(self.cuts)):
                self.finish_part(part)
            self.finish_sends()

        def finish_part(self, part):
            @pl.when(me < self.count)
            def _():
                for k in range(1, pairs):
                    zz = lax.rem(chip + k, pairs)
                    self.far_copy(zz, zz, part).wait_recv()
                    self.result[self.cuts[part]] += self.frecv[zz, self.cuts[part]].astype(F32)

        def finish_sends(self):
            for k in range(pairs):
                zz = lax.rem(chip + 1 + k, pairs)

                @pl.when(2 * zz + 1 - core < self.count)
                def _():
                    self.pair_copy(zz).wait_send()

            for k in range(1, pairs):
                zz = lax.rem(chip + k, pairs)

                @pl.when(2 * zz + core < self.count)
                def _():
                    for part in range(len(self.cuts)):
                        self.far_copy(zz, chip, part).wait_send()

    def attn_weight_copy(peer, slot):
        ref = w_all.at[me, shard_rows(slot)]
        return remote(ref, ref, w_send.at[peer], w_recv.at[slot], dp=peer)

    def up_low(peer, block):
        ref = up_w.at[shard_rows(high * n_low + block)]
        return remote(
            ref,
            ref,
            uw_send.at[peer],
            uw_recv.at[high * n_low + block],
            dp=high * n_low + peer,
        )

    def up_high(peer, row, block):
        ref = up_w.at[shard_rows(row * n_low + block)]
        return remote(
            ref,
            ref,
            uw_send_two.at[peer, block],
            uw_recv.at[row * n_low + block],
            dp=peer * n_low + low,
        )

    def down_high(peer, block):
        ref = down_w.at[shard_rows(block * n_low + low)]
        return remote(
            ref,
            ref,
            dw_send.at[peer],
            dw_recv.at[block * n_low + low],
            dp=peer * n_low + low,
        )

    def down_low(peer, column_at, block):
        ref = down_w.at[shard_rows(block * n_low + column_at)]
        return remote(
            ref,
            ref,
            dw_send_two.at[peer, block],
            dw_recv.at[block * n_low + column_at],
            dp=high * n_low + peer,
        )

    up_in = pltpu.make_async_copy(uw_hbm, ugrad_ref, in_sems.at[0])
    down_in = pltpu.make_async_copy(dw_hbm, dgrad_ref, in_sems.at[1])
    up_in.start()
    down_in.start()
    kv_k[...] = jnp.zeros_like(kv_k)
    barrier = pltpu.get_barrier_semaphore()
    for k in range(1, n_exp):
        pl.semaphore_signal(
            barrier, inc=1, device_id={"expert": lax.rem(me + k, n_exp)}, device_id_type=MESH
        )
    for k in range(1, n_dp):
        pl.semaphore_signal(
            barrier, inc=1, device_id={"dp": lax.rem(dp + k, n_dp)}, device_id_type=MESH
        )
    rows_all[1, me] = cot_ref[...]
    wrow[...] = jnp.zeros_like(wrow)
    w_all[me, shard_rows(dp)] = aw_ref[...].astype(BF16)
    up_in.wait()
    up_w[shard_rows(dp)] = ugrad_ref[...].astype(BF16)
    down_in.wait()
    down_w[shard_rows(dp)] = dgrad_ref[...].astype(BF16)
    pl.semaphore_wait(barrier, n_exp + n_dp - 2)
    each_peer(lambda peer: attn_weight_copy(peer, dp).start())
    cot_gather = Gather(rows_all.at[1], bg_send, bg_recv, n_act)
    cot_gather.send(2)
    for peer in low_peers():
        up_low(peer, low).start()
    for peer in high_peers():
        down_high(peer, high).start()
    for peer in high_peers():
        up_high(peer, high, low).start()
    for peer in low_peers():
        down_low(peer, low, high).start()

    kvb[...] = kvw_ref[...].astype(BF16)
    rb[...] = rw_ref[...].astype(BF16)
    gain_one = vec_ref[0:1, :]
    bias_one = vec_ref[1:2, :]
    gain_two = vec_ref[2:3, :]
    bias_two = vec_ref[3:4, :]
    halt = vec_ref[4:5, :]
    state[0] = x_ref[...].astype(F32)
    own_rows = pl.ds(pl.multiple_of(me * own, own), own)

    lane = lax.broadcasted_iota(jnp.int32, (own, LANES), 1)
    route_lane = lax.broadcasted_iota(jnp.int32, (own, 2 * n_exp), 1)
    lane_two = lax.broadcasted_iota(jnp.int32, (2 * own, LANES), 1)
    lane_cap = lax.broadcasted_iota(jnp.int32, (cap, LANES), 1)
    route_cap = lax.broadcasted_iota(jnp.int32, (cap, 2 * n_exp), 1)

    def column(values, index, lanes):
        return jnp.sum(jnp.where(lanes == index, values, 0.0), axis=1, keepdims=True)

    def cap_rows(loop):
        return pl.ds(pl.multiple_of(loop * cap, cap), cap)

    def window_keys(loop):
        return kv_k[loop, pl.ds(win_at, window)].reshape(keys, 2 * HD)

    def routing():
        position = lax.broadcasted_iota(jnp.int32, (1, slots), 1)
        bound = 0
        segment = jnp.zeros((1, slots), F32)
        for index in range(len_ref.shape[1]):
            bound = bound + len_ref[0, index]
            segment = segment + jnp.where(position >= bound, 1.0, 0.0)
        sub = lax.broadcasted_iota(jnp.int32, (n_exp, slots), 0)
        position_all = lax.broadcasted_iota(jnp.int32, (n_exp, slots), 1)
        valid = segment < len_ref.shape[1] - 0.5
        rowm_ref[LOOPS] = segment
        picks, selected = [], jnp.zeros((n_exp, slots), F32)
        for loop in range(LOOPS):
            running = jnp.where(valid & (run_ref[...] > loop), 1.0, 0.0)
            att = jnp.zeros((n_exp, slots), F32)
            for k in range(ar_ref.shape[1]):
                att = att + jnp.where(ar_ref[loop, k : k + 1, :] == sub, 1.0, 0.0)
            ffn = jnp.zeros((n_exp, slots), F32)
            mine = jnp.zeros((1, slots), F32)
            for k in range(fr_ref.shape[1]):
                ffn = ffn + jnp.where(fr_ref[loop, k : k + 1, :] == sub, 1.0, 0.0)
                mine = mine + jnp.where(fr_ref[loop, k : k + 1, :] == me, running, 0.0)
            picks.append((att, ffn, running))
            selected = selected + jnp.where(sub == loop, mine, 0.0)
        ranks = selected
        shift = 1
        while shift < slots:
            moved = pltpu.roll(ranks, shift, 1)
            ranks = ranks + jnp.where(position_all >= shift, moved, 0.0)
            shift *= 2
        ranks = jnp.where(selected > 0.5, ranks - 1.0, -1.0)
        for loop in range(LOOPS):
            att, ffn, running = picks[loop]
            rank = ranks[loop : loop + 1]
            rowm_ref[loop] = rank
            rest = jnp.where(
                sub == 0,
                rank,
                jnp.where(sub == 1, running, jnp.where(sub == 2, segment, 0.0)),
            )
            spare = jnp.zeros((INFO - 3 * n_exp, slots), F32)
            meta_ref[loop] = jnp.transpose(jnp.concatenate([att, ffn, rest, spare], axis=0))

    def kv_copy(loop, where, sem):
        ref = kv_k.at[loop, me]
        return remote(ref, ref, kg_send.at[sem], kg_recv.at[me], expert=where)

    def prepare(loop):
        unit, _ = normalise(state[loop])
        normed = (unit * gain_one + bias_one).astype(BF16)
        normed_k[loop] = normed
        kv_k[loop, me] = nn(normed, kvb[...]).astype(BF16)
        for k in range(1, window):

            @pl.when(me + k < n_act)
            def _():
                kv_copy(loop, me + k, k - 1).start()

        info = meta_ref[loop, own_rows, 0 : 2 * n_exp]
        gate_k[loop] = masked_softmax(
            nt(normed, rb[...]), (info > 0.5) & (route_lane < n_exp)
        )

    def running_rows(loop):
        return meta_ref[loop, own_rows, RUN_LANE : RUN_LANE + 1]

    each_peer(lambda peer: attn_weight_copy(peer, peer).wait_recv())
    weights_gather = Gather(w_all, wg_send, wg_recv, n_exp)
    weights_gather.start()
    routing()
    prepare(0)
    seg_own = meta_ref[0, own_rows, SEG_LANE : SEG_LANE + 1]
    key_cols = pl.ds(pl.multiple_of(win_at * own, own), keys)
    seg_keys = rowm_ref[LOOPS, :, key_cols]
    row_at = me * own + lax.broadcasted_iota(jnp.int32, (own, keys), 0)
    key_at = win_at * own + lax.broadcasted_iota(jnp.int32, (own, keys), 1)
    allowed = (seg_own == seg_keys) & (key_at <= row_at)
    bias[...] = jnp.where(allowed, 0.0, masked_score)
    up_acc[...] = jnp.zeros_like(up_acc)
    down_acc[...] = jnp.zeros_like(down_acc)
    attn_acc[...] = jnp.zeros_like(attn_acc)
    small_acc[...] = jnp.zeros_like(small_acc)
    weights_gather.finish()
    for block in low_peers():
        up_low(block, block).wait_recv()
        for peer in high_peers():
            up_high(peer, high, block).start()
    for block in high_peers():
        down_high(block, block).wait_recv()
        for peer in low_peers():
            down_low(peer, low, block).start()

    rows_gather = Gather(rows_all.at[0], ag_send, ag_recv, n_act)

    def attention(loop):
        normed = normed_k[loop]

        def queries(expert, none):
            query = jnp.where(lane < HD, nn(normed, w_all[expert]), 0.0).astype(BF16)
            q_k[loop, pl.ds(pl.multiple_of(expert * own, own), own)] = query
            return none

        lax.fori_loop(0, n_exp, queries, 0, unroll=True)
        running = running_rows(loop)
        gates = gate_k[loop] * running
        mix[...] = jnp.zeros_like(mix)
        for k in range(1, window):

            @pl.when(active & (me >= k))
            def _():
                ref = kv_k.at[loop, me - k]
                remote(
                    ref, ref, kg_send.at[k - 1], kg_recv.at[me - k], expert=me - k
                ).wait_recv()

        kv_rows = window_keys(loop)

        def attend(pair, none):
            rows = pl.ds(pl.multiple_of(pair * 2 * own, 2 * own), 2 * own)
            scores = nt(q_k[loop, rows], kv_rows) * scale
            scores = (scores.reshape(2, own, keys) + bias[...][None]).reshape(2 * own, keys)
            powers = jnp.exp(scores - jnp.max(scores, axis=1, keepdims=True))
            prob = (powers * (1.0 / jnp.sum(powers, axis=1, keepdims=True))).astype(BF16)
            p_k[loop, rows] = prob
            outs = jnp.where(lane_two < HD, 0.0, nn(prob, kv_rows)).astype(BF16)
            o_k[loop, rows] = outs
            for half in range(2):
                expert = 2 * pair + half
                gate = column(gates, expert, route_lane)
                mix[...] += gate * nt(outs[half * own : (half + 1) * own], w_all[expert])
            return none

        lax.fori_loop(0, n_exp // 2, attend, 0, unroll=True)
        for k in range(1, window):

            @pl.when(me + k < n_act)
            def _():
                kv_copy(loop, me + k, k - 1).wait_send()

        centre = state[loop] + mix[...]
        middle[loop] = centre
        unit, _ = normalise(centre)
        second = (unit * gain_two + bias_two).astype(BF16)
        second_k[loop] = second
        rows_all[0, me] = second

    factor_gather = Gather(wrow, fg_send, fg_recv, n_act)

    def place_matrices(loop):
        ranks = rowm_ref[loop, :, 0:valid_rows]
        slot = lax.broadcasted_iota(jnp.int32, (cap, valid_rows), 0).astype(F32)
        gather_m[...] = jnp.where(slot == ranks, 1.0, 0.0).astype(BF16)
        slot = lax.broadcasted_iota(jnp.int32, (own, cap), 1).astype(F32)

        def block_matrix(block, none):
            rows = pl.ds(pl.multiple_of(block * own, own), own)
            ranks = meta_ref[loop, rows, RANK_LANE : RANK_LANE + 1]
            scatter_m[rows] = jnp.where(slot == ranks, 1.0, 0.0).astype(BF16)
            return none

        lax.fori_loop(0, n_act, block_matrix, 0)

    def spread_rows(blocks, terms):
        rows = nn(scatter_m[...], terms).astype(BF16)
        blocks[0:n_act] = rows.reshape(n_act, own, width)

    def take(buf):
        return nn(gather_m[...], rows_all[buf, 0:n_act].reshape(valid_rows, width))

    def expert_rows(loop):
        rows_in = take(0).astype(BF16)
        rows_k[cap_rows(loop)] = rows_in
        allowed_lanes = (chosen_k[...] > 0.5) & (route_cap >= n_exp)
        gate = column(masked_softmax(nt(rows_in, rb[...]), allowed_lanes), n_exp + me, route_cap)
        fgate_k[cap_rows(loop)] = gate
        part_k[cap_rows(loop)] = jnp.zeros((cap, width), F32)

    root = math.sqrt(2.0 / math.pi)

    def tile_cols(tile):
        return pl.ds(pl.multiple_of(tile * TILE, TILE), TILE)

    def hidden_layer(loop):
        rows_in = rows_k[cap_rows(loop)]

        def step(tile, none):
            cols = tile_cols(tile)
            inner = nn(rows_in, up_w[:, cols])
            square = inner * inner
            curve = jnp.tanh(root * inner * (1.0 + 0.044715 * square))
            upper = 0.5 * (1.0 + curve)
            hidden = (inner * upper).astype(BF16)
            hid[cap_rows(loop), cols] = hidden
            slope = upper + 0.5 * inner * (1.0 - curve * curve) * (
                root + (3.0 * 0.044715 * root) * square
            )
            gprime[cap_rows(loop), cols] = slope.astype(BF16)
            part_k[cap_rows(loop)] += nt(hidden, down_w[:, cols])
            return none

        lax.fori_loop(0, tiles, step, 0, unroll=True)

    sums = Reduce(
        n_act,
        [own // 2, own // 2],
        blocks_two,
        pair_recv_two,
        far_recv_two,
        rs_sems_two,
        total_two,
    )
    back_sums = Reduce(
        n_act, [own // 2, own // 2], blocks_one, pair_recv, far_recv, rs_sems, total
    )
    gate_sums = Reduce(n_act, [EXTRA], g_blocks, g_pair_recv, g_far_recv, g_sems, g_total)

    def start_terms(loop, send):
        terms = (part_k[cap_rows(loop)] * fgate_k[cap_rows(loop)]).astype(BF16)
        spread_rows(blocks_two, terms)
        sums.start(send)

    def wait_weights():
        for peer in high_peers():
            for block in range(n_low):
                up_high(peer, peer, block).wait_recv()
        for peer in low_peers():
            for block in range(n_high):
                down_low(peer, peer, block).wait_recv()

    def chances():
        chance_one = jax.nn.sigmoid(jnp.sum(state[1] * halt, axis=1, keepdims=True))
        chance_two = jax.nn.sigmoid(jnp.sum(state[2] * halt, axis=1, keepdims=True))
        return chance_one, chance_two

    def last_factor():
        chance_one, chance_two = chances()
        weight_last = (1.0 - chance_one) * (1.0 - chance_two)
        sgrad[last] = weight_last * cot_ref[...].astype(F32)
        upper = weight_last.astype(BF16).astype(F32)
        factors = jnp.where(lane == 0, upper, jnp.where(lane == 1, weight_last - upper, 0.0))
        wrow[me] = jnp.transpose(factors)[0:EXTRA].astype(BF16)
        factor_gather.start()

    carry[...] = jnp.zeros_like(carry)

    def state_grads(loop_dot):
        chance_one, chance_two = chances()
        cot = cot_ref[...].astype(F32)
        first, next_one = state[1], state[2]
        stay = 1.0 - chance_one
        weight_two = stay * chance_two
        weight_three = stay * (1.0 - chance_two)
        dot_one = jnp.sum(cot * first, axis=1, keepdims=True)
        dot_two = jnp.sum(cot * next_one, axis=1, keepdims=True)
        dot_middle = jnp.sum(cot * middle[last], axis=1, keepdims=True)
        dot_three = jnp.where(
            running_rows(last) > 0.5, weight_three * dot_middle + loop_dot, weight_three * dot_two
        )
        slope_one = chance_one * (stay * dot_one - weight_two * dot_two - dot_three)
        slope_two = chance_two * (weight_three * dot_two - dot_three)
        sgrad[0] = chance_one * cot + slope_one * halt
        sgrad[1] = weight_two * cot + slope_two * halt
        small_acc[vec_at + 4 : vec_at + 5] = jnp.sum(
            slope_one * first + slope_two * next_one, axis=0, keepdims=True
        )

    def finish_output():
        chance_one, chance_two = chances()
        first, next_one = state[1], state[2]
        final = jnp.where(running_rows(last) > 0.5, middle[last] + total_two[0:own], next_one)
        stay = 1.0 - chance_one
        out_ref[...] = (
            chance_one * first + stay * chance_two * next_one + stay * (1.0 - chance_two) * final
        )

    vec_at = 2 * HD + EXTRA

    def expert_back(loop):
        grad_rows = row_grads[...]
        gate = fgate_k[cap_rows(loop)]
        ggrad[...] = jnp.sum(grad_rows * part_k[cap_rows(loop)], axis=1, keepdims=True)
        scaled = (grad_rows * gate).astype(BF16)
        scaled_k[...] = scaled
        row_grads[...] = jnp.zeros_like(row_grads)

        def step(tile, none):
            cols = tile_cols(tile)
            inner_grad = (
                nn(scaled, down_w[:, cols]) * gprime[cap_rows(loop), cols].astype(F32)
            ).astype(BF16)
            gprime[cap_rows(loop), cols] = inner_grad
            row_grads[...] += nt(inner_grad, up_w[:, cols])
            return none

        lax.fori_loop(0, tiles, step, 0, unroll=True)
        terms = row_grads[...].astype(BF16)
        gate_grad = ggrad[...]
        upper = gate_grad.astype(BF16).astype(F32)
        spread = jnp.where(lane_cap == n_exp + me, upper, 0.0) + jnp.where(
            lane_cap == me, gate_grad - upper, 0.0
        )
        spread_t = jnp.transpose(spread)[0:EXTRA].astype(BF16)

        grads = nt(spread_t, scatter_m[...]).astype(BF16)
        for block in range(n_act):
            g_blocks[block] = grads[:, block * own : (block + 1) * own]
        gate_sums.start_pairs()
        spread_rows(blocks_one, terms)
        back_sums.start_pairs()
        gate_sums.start_far(True)
        back_sums.start_far(True)

    def expert_weights(loop):
        rows_in = rows_k[cap_rows(loop)]
        scaled = scaled_k[...]

        def step(tile, none):
            cols = tile_cols(tile)
            down_acc[:, cols] += tn(scaled, hid[cap_rows(loop), cols])
            up_acc[:, cols] += tn(rows_in, gprime[cap_rows(loop), cols])
            return none

        lax.fori_loop(0, tiles, step, 0, unroll=True)

    def order_at(source, receiver, count):
        return lax.rem(source - receiver + count, count) - 1

    spare = width // shard

    def up_grad_first(peer, slot, block, receiver):
        return remote(
            hid.at[shard_rows(block * n_low + peer)],
            u_first.at[order_at(slot, receiver, n_low), shard_rows(block)],
            ug_send.at[peer, block],
            ug_recv.at[slot, block],
            dp=high * n_low + peer,
        )

    def up_grad_second(peer, slot, receiver):
        return remote(
            hid.at[shard_rows(spare + peer)],
            u_last.at[order_at(slot, receiver, n_high)],
            ug_send_two.at[peer],
            ug_recv_two.at[slot],
            dp=peer * n_low + low,
        )

    def down_grad_first(peer, slot, block, receiver):
        return remote(
            gprime.at[shard_rows(peer * n_low + block)],
            d_first.at[order_at(slot, receiver, n_high), shard_rows(block)],
            dg_send.at[peer, block],
            dg_recv.at[slot, block],
            dp=peer * n_low + low,
        )

    def down_grad_second(peer, slot, receiver):
        return remote(
            gprime.at[shard_rows(spare + peer)],
            d_last.at[order_at(slot, receiver, n_low)],
            dg_send_two.at[peer],
            dg_recv_two.at[slot],
            dp=high * n_low + peer,
        )

    def send_expert_weights():
        hid[0:width] = up_acc[...].astype(BF16)
        for peer in low_peers():
            for block in high_peers():
                up_grad_first(peer, low, block, peer).start()
        gprime[0:width] = down_acc[...].astype(BF16)
        for peer in high_peers():
            for block in low_peers():
                down_grad_first(peer, high, block, peer).start()
        for peer in low_peers():
            up_grad_first(peer, low, high, peer).start()
        for peer in high_peers():
            down_grad_first(peer, high, low, peer).start()

    def pass_expert_weights():
        for block in high_peers():
            added = up_acc[shard_rows(block * n_low + low)]
            for peer in low_peers():
                up_grad_first(peer, peer, block, low).wait_recv()
                added = added + u_first[
                    order_at(peer, low, n_low), shard_rows(block)
                ].astype(F32)
            hid[shard_rows(spare + block)] = added.astype(BF16)
            up_grad_second(block, high, block).start()
        for block in low_peers():
            added = down_acc[shard_rows(high * n_low + block)]
            for peer in high_peers():
                down_grad_first(peer, peer, block, high).wait_recv()
                added = added + d_first[
                    order_at(peer, high, n_high), shard_rows(block)
                ].astype(F32)
            gprime[shard_rows(spare + block)] = added.astype(BF16)
            down_grad_second(block, low, block).start()

    def finish_expert_weights():
        added = up_acc[shard_rows(dp)]
        for peer in low_peers():
            up_grad_first(peer, peer, high, low).wait_recv()
            added = added + u_first[order_at(peer, low, n_low), shard_rows(high)].astype(F32)
        for peer in high_peers():
            up_grad_second(peer, peer, high).wait_recv()
            added = added + u_last[order_at(peer, high, n_high)].astype(F32)
        ugrad_ref[...] = added
        added = down_acc[shard_rows(dp)]
        for peer in high_peers():
            down_grad_first(peer, peer, low, high).wait_recv()
            added = added + d_first[order_at(peer, high, n_high), shard_rows(low)].astype(F32)
        for peer in low_peers():
            down_grad_second(peer, peer, low).wait_recv()
            added = added + d_last[order_at(peer, low, n_low)].astype(F32)
        dgrad_ref[...] = added

    attn_sums = Reduce(
        n_exp,
        [2 * HD],
        blocks_two,
        pair_recv_two,
        far_recv_two,
        a_sems,
        total_two,
    )

    def dkv_copy(distance, owner):
        return remote(
            dkv_send.at[jnp.clip(owner - win_at, 0, window - 1)],
            dkv_recv.at[distance - 1],
            dk_send.at[distance - 1],
            dk_recv.at[distance - 1],
            expert=owner,
        )

    def attention_back(loop, step):
        info = meta_ref[loop, own_rows, 0 : 2 * n_exp]
        running = running_rows(loop)
        branch = (sgrad[loop] + carry[...]) * running
        gate_sums.finish_part(0)
        gate_rows = g_total[0:n_exp] + g_total[n_exp : 2 * n_exp]
        gate_rows = jnp.concatenate(
            [jnp.zeros((n_exp, own), F32), gate_rows, jnp.zeros((LANES - 2 * n_exp, own), F32)],
            axis=0,
        )
        gate_grads = jnp.transpose(gate_rows)[:, 0 : 2 * n_exp]
        second = second_k[loop]
        gates = masked_softmax(nt(second, rb[...]), (info > 0.5) & (route_lane >= n_exp))
        loop_dot = jnp.sum(gates * gate_grads, axis=1, keepdims=True)
        logit_grad = (gates * (gate_grads - loop_dot)).astype(BF16)
        router_part = nn(logit_grad, rb[...])
        gates = gate_k[loop]
        kv_rows = window_keys(loop)
        half = own // 2

        for part in range(2):
            at = part * half
            back_sums.finish_part(part)
            second_grad = total[at : at + half] + router_part[at : at + half]
            total[at : at + half] = second_grad
            unit, inverse = normalise(middle[loop, at : at + half])
            middle_grad = norm_back(second_grad, unit, inverse, gain_two) + branch[at : at + half]
            mgrad[at : at + half] = middle_grad
            for quad in range(n_exp // 4):
                experts = range(4 * quad, 4 * quad + 4)
                out_grads = []
                for expert in experts:
                    part_grad = (gates[at : at + half, expert : expert + 1] * middle_grad).astype(
                        BF16
                    )
                    out_grads.append(nn(part_grad, w_all[expert]))
                out_grad = jnp.concatenate(out_grads, axis=0)
                out_grad = jnp.where(lane_two < HD, 0.0, out_grad).astype(BF16)
                rows = [slice(e * own + at, e * own + at + half) for e in experts]
                prob_low = jnp.concatenate([p_k[loop, cut] for cut in rows], axis=0)
                query = jnp.concatenate([q_k[loop, cut] for cut in rows], axis=0)
                prob = prob_low.astype(F32)
                prob_grad = nt(out_grad, kv_rows)
                centre = jnp.sum(prob * prob_grad, axis=1, keepdims=True)
                score_grad = (prob * (prob_grad - centre)).astype(BF16)
                for index, cut in enumerate(rows):
                    ds_k[cut] = score_grad[index * half : (index + 1) * half]
                grads = tn(query, score_grad) * scale + tn(out_grad, prob_low)
                if part or quad:
                    dkv_t[...] += grads
                else:
                    dkv_t[...] = grads
        for block in range(window):
            grads = jnp.transpose(dkv_t[:, block * own : (block + 1) * own])
            dkv[block] = grads
            dkv_send[block] = grads.astype(BF16)
        for distance in range(1, window):

            @pl.when(active & (me >= distance))
            def _():
                dkv_copy(distance, me - distance).start()

        back_sums.finish_sends()
        gate_sums.finish_sends()
        @pl.when(step == last)
        def _():
            state_grads(loop_dot)
            sums.send((1, 0))

        @pl.when(step == last + 1)
        def _():
            sums.send((3, 1))

        small_acc[2 * HD : vec_at] += tn(logit_grad, second)
        second_grad = total[...]
        unit, _ = normalise(middle[loop])
        small_acc[vec_at + 2 : vec_at + 3] += jnp.sum(second_grad * unit, axis=0, keepdims=True)
        small_acc[vec_at + 3 : vec_at + 4] += jnp.sum(second_grad, axis=0, keepdims=True)
        normed = normed_k[loop]
        mix[...] = jnp.zeros_like(mix)
        dga[...] = jnp.zeros_like(dga)

        def queries_back(pair, none):
            rows = pl.ds(pl.multiple_of(pair * 2 * own, 2 * own), 2 * own)
            outs = o_k[loop, rows]
            query_grad = jnp.where(lane_two < HD, nn(ds_k[rows], kv_rows) * scale, 0.0).astype(BF16)
            for half in range(2):
                expert = 2 * pair + half
                cut = slice(half * own, (half + 1) * own)
                middle_grad = mgrad[...]
                dot = jnp.sum(middle_grad * nt(outs[cut], w_all[expert]), axis=1, keepdims=True)
                dga[...] += jnp.where(route_lane == expert, dot, 0.0)
                part_grad = (column(gates, expert, route_lane) * middle_grad).astype(BF16)
                attn_acc[expert] += tn(query_grad[cut], normed) + tn(outs[cut], part_grad)
                mix[...] += nt(query_grad[cut], w_all[expert])
            return none

        lax.fori_loop(0, n_exp // 2, queries_back, 0)

        @pl.when(loop == 0)
        def _():
            blocks_two[...] = attn_acc[...].astype(BF16)
            attn_sums.start(False)

        gate_grads = dga[...]
        logit_grad = (
            gates * (gate_grads - jnp.sum(gates * gate_grads, axis=1, keepdims=True))
        ).astype(BF16)
        small_acc[2 * HD : vec_at] += tn(logit_grad, normed)
        normed_grad = mix[...] + nn(logit_grad, rb[...])
        unit, inverse = normalise(state[loop])

        own_block = jnp.clip(me - win_at, 0, window - 1)
        dkv[window] = jnp.where(active, dkv[own_block], 0.0)
        for distance in range(1, window):

            @pl.when(me + distance < n_act)
            def _():
                remote(
                    dkv_send.at[0],
                    dkv_recv.at[distance - 1],
                    dk_send.at[distance - 1],
                    dk_recv.at[distance - 1],
                    expert=me + distance,
                ).wait_recv()
                dkv[window] += dkv_recv[distance - 1].astype(F32)

        for distance in range(1, window):

            @pl.when(active & (me >= distance))
            def _():
                dkv_copy(distance, me - distance).wait_send()

        kv_grad = dkv[window].astype(BF16)
        small_acc[0 : 2 * HD] += tn(kv_grad, normed)
        normed_grad = normed_grad + nt(kv_grad, kvb[...])
        small_acc[vec_at : vec_at + 1] += jnp.sum(normed_grad * unit, axis=0, keepdims=True)
        small_acc[vec_at + 1 : vec_at + 2] += jnp.sum(normed_grad, axis=0, keepdims=True)
        carry[...] = (
            (sgrad[loop] + carry[...]) * (1.0 - running)
            + mgrad[...]
            + norm_back(normed_grad, unit, inverse, gain_one)
        )

    def phase(step, none):
        loop = jnp.where(step <= last, step, 2 * last - step)

        @pl.when(step <= last)
        def _():
            attention(loop)

        @pl.when(step == 2 * last)
        def _():
            sums.finish()
            finish_output()

        @pl.when(step > last)
        def _():
            rows_all[0, me] = ((sgrad[loop] + carry[...]) * running_rows(loop)).astype(BF16)

        rows_gather.start()
        place_matrices(loop)

        @pl.when(step <= last)
        def _():
            chosen_k[...] = nn(
                gather_m[...], meta_ref[loop, 0:valid_rows, 0 : 2 * n_exp].astype(BF16)
            )

        @pl.when(step == 0)
        def _():
            wait_weights()

        @pl.when(step == last)
        def _():
            cot_gather.finish()
            factor_gather.finish()

        rows_gather.finish()

        @pl.when(step == 0)
        def _():
            cot_gather.send(0)
            cot_gather.send(1)

        @pl.when(step == 1)
        def _():
            cot_gather.send(3)

        @pl.when(step <= last)
        def _():
            expert_rows(loop)
            hidden_layer(loop)

        @pl.when(step == last + 1)
        def _():
            sums.send((2, 1))

        @pl.when(step >= last)
        def _():
            factors = nt(
                gather_m[...], jnp.concatenate([wrow[block] for block in range(n_act)], axis=1)
            )
            factor = jnp.where(step == last, factors[:, 0:1] + factors[:, 1:2], 1.0)
            row_grads[...] = take(jnp.where(step == last, 1, 0)) * factor
            expert_back(loop)

        @pl.when(step <= last)
        def _():
            start_terms(loop, step < last)

        @pl.when(step < last)
        def _():
            sums.finish()
            state[loop + 1] = jnp.where(
                running_rows(loop) > 0.5, middle[loop] + total_two[0:own], state[loop]
            )
            prepare(loop + 1)

        @pl.when(step == last - 1)
        def _():
            last_factor()

        @pl.when(step >= last)
        def _():
            expert_weights(loop)

            @pl.when(step == 2 * last)
            def _():
                send_expert_weights()


            @pl.when(step == last)
            def _():
                sums.send((2, 0))

            @pl.when(step == last + 1)
            def _():
                sums.send((3, 0), (1, 1))

            attention_back(loop, step)

        return none

    lax.fori_loop(0, 2 * last + 1, phase, 0)
    xgrad_ref[...] = carry[...]

    chunk = small_acc.shape[0] // n_exp
    small_sums = Reduce(
        n_exp, [chunk], s_blocks, s_pair_recv, s_far_recv, s_sems, s_total
    )
    s_blocks[...] = small_acc[...].astype(BF16).reshape(n_exp, chunk, width)
    small_sums.start(True)
    attn_sums.send((1, 0), (3, 0), (2, 0))

    def attn_copy(peer, slot):
        return remote(
            a_stage.at[shard_rows(peer)],
            a_recv.at[shard_rows(slot)],
            t_send.at[1, peer],
            t_recv.at[1, slot],
            dp=peer,
        )

    def small_copy(peer, slot):
        return remote(
            s_dp.at[slot], s_dp.at[slot], t_send.at[0, peer], t_recv.at[0, slot], dp=peer
        )

    small_sums.finish()
    s_dp[dp] = s_total[...].astype(BF16)
    each_peer(lambda peer: small_copy(peer, dp).start())
    pass_expert_weights()
    attn_sums.finish()
    a_total[...] = jnp.transpose(total_two[...])
    a_stage[...] = a_total[...].astype(BF16)
    each_peer(lambda peer: attn_copy(peer, dp).start())
    each_peer(lambda peer: small_copy(peer, peer).wait_recv())
    s_total[...] = jnp.zeros_like(s_total)

    def add_small(index, none):
        s_total[...] += s_dp[index].astype(F32)
        return none

    lax.fori_loop(0, n_dp, add_small, 0)
    s_all[me] = s_total[...]
    small_gather = Gather(s_all, sg_send, sg_recv, n_exp)
    small_gather.start()
    agrad_ref[...] = a_total[shard_rows(dp)]

    def add_attn(peer):
        attn_copy(peer, peer).wait_recv()
        agrad_ref[...] += a_recv[shard_rows(peer)].astype(F32)

    each_peer(add_attn)
    finish_expert_weights()
    small_gather.finish()
    small = s_all[...].reshape(n_exp * chunk, width)
    kvgrad_ref[...] = jnp.transpose(small[0 : 2 * HD])
    rgrad_ref[...] = small[2 * HD : vec_at]
    vgrad_ref[...] = small[vec_at : vec_at + 8]

    def sent(peer):
        attn_weight_copy(peer, dp).wait_send()
        small_copy(peer, dp).wait_send()
        attn_copy(peer, dp).wait_send()

    each_peer(sent)
    for peer in low_peers():
        up_low(peer, low).wait_send()
        down_grad_second(peer, low, peer).wait_send()
        for block in range(n_high):
            down_low(peer, low, block).wait_send()
            up_grad_first(peer, low, block, peer).wait_send()
    for peer in high_peers():
        down_high(peer, high).wait_send()
        for block in range(n_low):
            up_high(peer, high, block).wait_send()
            down_grad_first(peer, high, block, peer).wait_send()
        up_grad_second(peer, high, peer).wait_send()


def adam_kernel(*refs):
    out_in, xgrad_in, ugrad, dgrad, agrad, kvgrad, rgrad, vgrad = refs[:8]
    shared, kv, router, attn, up, down = (refs[8 + 3 * index : 11 + 3 * index] for index in range(6))
    out, xgrad = refs[26:28]
    shared_out, kv_out, router_out, attn_out, up_out, down_out = (
        refs[28:31],
        refs[31:34],
        refs[34:37],
        refs[37:41],
        refs[41:45],
        refs[45:49],
    )

    def update(sources, grad, results, rate, decay):
        values = adam_update(*(source[...] for source in sources), grad, rate, decay)
        for result, value in zip(results, values):
            result[...] = value
        if len(results) > 3:
            results[3][...] = values[0].astype(BF16)

    out[...] = out_in[...]
    xgrad[...] = xgrad_in[...]
    update(up, ugrad[...], up_out, 14.0 / math.sqrt(D), decay_rate)
    update(down, dgrad[...], down_out, 17.0 / math.sqrt(FF), decay_rate)

    @pl.when(pl.program_id(0) == 0)
    def _():
        row = lax.broadcasted_iota(jnp.int32, shared[0].shape, 0)
        rates = jnp.where(row < 4, 6.0, 20.0 / math.sqrt(D))
        update(shared, vgrad[0 : shared[0].shape[0]], shared_out, rates, 0.0)
        update(kv, kvgrad[...], kv_out, 20.0 / math.sqrt(D), decay_rate)
        update(router, rgrad[...], router_out, 50.0 / math.sqrt(3 * D), decay_rate)
        lane = lax.broadcasted_iota(jnp.int32, attn[0].shape, 1)
        rates = jnp.where(lane < HD, 25.0 / math.sqrt(D), 50.0 / math.sqrt(HD))
        update(attn, agrad[...], attn_out, rates, decay_rate)


def dp_grid(n_dp):
    n_low = 1
    while n_low * n_low * 4 <= n_dp:
        n_low *= 2
    return n_low, n_dp // n_low


def per_device(
    block_input,
    cotangent,
    lengths,
    run_loops,
    attn_routes,
    ffn_routes,
    shared_vectors,
    shared_moment,
    shared_second,
    key_value,
    kv_moment,
    kv_second,
    router_weights,
    router_moment,
    router_second,
    attn_weights,
    attn_moment,
    attn_second,
    up_weights,
    up_moment,
    up_second,
    down_weights,
    down_moment,
    down_second,
):
    n_exp = lax.axis_size("expert")
    n_dp = lax.axis_size("dp")
    own, width = block_input.shape
    slots = run_loops.shape[0]
    shard = attn_weights.shape[1]
    hidden = up_weights.shape[2]
    cap = 5 * slots * KFF // (4 * n_exp)
    n_act = FILLED // own
    window = min(n_act, MAXLEN // own + 1)
    pairs = n_exp // 2
    valid_rows = n_act * own
    n_low, n_high = dp_grid(n_dp)

    small_rows = 32 * n_exp
    vmem = pltpu.VMEM
    dma = pltpu.SemaphoreType.DMA
    block = (pairs, own, width)
    small_block = (pairs, 32, width)
    scratch = [
        vmem((LOOPS, slots, INFO), F32),
        vmem((LOOPS + 1, 1, slots), F32),
        vmem((width, 2 * HD), BF16),
        vmem((2 * n_exp, width), BF16),
        vmem((n_exp, width, 2 * HD), BF16),
        vmem((width, hidden), BF16),
        vmem((width, hidden), BF16),
        vmem((width, hidden), F32),
        vmem((width, hidden), F32),
        vmem((n_exp, 2 * HD, width), F32),
        vmem((small_rows, width), F32),
        vmem((LOOPS, own, width), F32),
        vmem((LOOPS, own, width), F32),
        vmem((LOOPS, own, width), BF16),
        vmem((LOOPS, own, width), BF16),
        vmem((LOOPS, n_exp, own, 2 * HD), BF16),
        vmem((LOOPS, n_exp * own, 2 * HD), BF16),
        vmem((LOOPS, n_exp * own, 2 * HD), BF16),
        vmem((LOOPS, n_exp * own, window * own), BF16),
        vmem((n_exp * own, window * own), BF16),
        vmem((own, window * own), F32),
        vmem((own, width), F32),
        vmem((own, 2 * n_exp), F32),
        vmem((2 * HD, window * own), F32),
        vmem((window + 1, own, 2 * HD), F32),
        vmem((LOOPS, own, 2 * n_exp), F32),
        vmem((2, n_exp, own, width), BF16),
        vmem((n_exp, EXTRA, own), BF16),
        vmem((cap, valid_rows), BF16),
        vmem((valid_rows, cap), BF16),
        vmem((LOOPS * cap, width), BF16),
        vmem((LOOPS * cap, hidden), BF16),
        vmem((LOOPS * cap, hidden), BF16),
        vmem((cap, width), F32),
        vmem((LOOPS * cap, width), F32),
        vmem((LOOPS * cap, 1), F32),
        vmem((cap, 2 * n_exp), F32),
        vmem((cap, 1), F32),
        vmem((cap, width), BF16),
        vmem((LOOPS, own, width), F32),
        vmem((own, width), F32),
        vmem((own, width), F32),
        vmem((own, width), F32),
        vmem((own, width), F32),
        vmem((n_exp, EXTRA, own), BF16),
        vmem((pairs, EXTRA, own), BF16),
        vmem((pairs, EXTRA, own), BF16),
        vmem((EXTRA, own), F32),
        vmem((n_exp, own, width), BF16),
        vmem(block, BF16),
        vmem(block, BF16),
        vmem((n_exp, own, width), BF16),
        vmem((pairs, own, width), BF16),
        vmem((pairs, own, width), BF16),
        vmem((window, own, 2 * HD), BF16),
        vmem((window, own, 2 * HD), BF16),
        vmem((n_low - 1, n_high * shard, hidden), BF16),
        vmem((n_high - 1, shard, hidden), BF16),
        vmem((n_high - 1, n_low * shard, hidden), BF16),
        vmem((n_low - 1, shard, hidden), BF16),
        vmem((width, 2 * HD), F32),
        vmem((width, 2 * HD), BF16),
        vmem((width, 2 * HD), BF16),
        vmem((n_exp, 32, width), BF16),
        vmem(small_block, BF16),
        vmem(small_block, BF16),
        vmem((32, width), F32),
        vmem((n_dp, 32, width), BF16),
        vmem((n_exp, 32, width), F32),
        dma((2,)),
        dma((n_dp,)),
        dma((n_dp,)),
        dma((n_low,)),
        dma((n_dp,)),
        dma((n_high, n_low)),
        dma((n_high,)),
        dma((n_dp,)),
        dma((n_low, n_high)),
        dma((1, 2 * pairs)),
        dma((1, n_exp)),
        dma((1, 2 * pairs)),
        dma((1, n_exp)),
        dma((1, 2 * pairs)),
        dma((1, n_exp)),
        dma((1, 2 * pairs)),
        dma((1, n_exp)),
        dma((1, 2 * pairs)),
        dma((1, n_exp)),
        dma((window,)),
        dma((n_exp,)),
        dma((6, pairs)),
        dma((4, pairs)),
        dma((6, pairs)),
        dma((4, pairs)),
        dma((4, pairs)),
        dma((window,)),
        dma((window,)),
        dma((n_low, n_high)),
        dma((n_low, n_high)),
        dma((n_high,)),
        dma((n_high,)),
        dma((n_high, n_low)),
        dma((n_high, n_low)),
        dma((n_low,)),
        dma((n_low,)),
        dma((2, n_dp)),
        dma((2, n_dp)),
    ]
    whole = pl.BlockSpec(memory_space=pltpu.VMEM)
    scalars = pl.BlockSpec(memory_space=pltpu.SMEM)
    outside = pl.BlockSpec(memory_space=pl.ANY)
    shape = jax.ShapeDtypeStruct
    sums = pl.pallas_call(
        functools.partial(block_kernel, n_exp, n_dp, n_act, cap),
        out_shape=(
            shape((own, width), F32),
            shape((own, width), F32),
            shape((shard, hidden), F32),
            shape((shard, hidden), F32),
            shape((shard, 2 * HD), F32),
            shape((width, 2 * HD), F32),
            shape((2 * n_exp, width), F32),
            shape((8, width), F32),
        ),
        in_specs=[whole, whole, scalars, *([whole] * 7), outside, outside],
        out_specs=[whole] * 8,
        scratch_shapes=scratch,
        compiler_params=pltpu.CompilerParams(
            collective_id=0, has_side_effects=True, vmem_limit_bytes=63 * 1024 * 1024
        ),
        name="block",
    )(
        block_input,
        cotangent,
        lengths,
        run_loops[None],
        attn_routes.transpose(0, 2, 1),
        ffn_routes.transpose(0, 2, 1),
        shared_vectors,
        key_value,
        router_weights.T,
        attn_weights[0],
        up_weights[0],
        down_weights[0],
    )

    steps = max(1, shard // 64)
    rows = shard // steps

    def by_rows(array):
        return pl.BlockSpec((array.shape[0] // steps, array.shape[1]), lambda step: (step, 0))

    def fixed(array):
        return pl.BlockSpec(array.shape, lambda step: (0, 0))

    output, input_grad, up_sum, down_sum, *small = sums
    small_args = [
        shared_vectors,
        shared_moment,
        shared_second,
        key_value,
        kv_moment,
        kv_second,
        router_weights.T,
        router_moment.T,
        router_second.T,
        attn_weights[0],
        attn_moment[0],
        attn_second[0],
    ]
    large_args = [
        up_weights[0],
        up_moment[0],
        up_second[0],
        down_weights[0],
        down_moment[0],
        down_second[0],
    ]
    attn_low = shape((shard, 2 * HD), BF16)
    large_low = shape((shard, hidden), BF16)
    like = [shape(array.shape, array.dtype) for array in small_args]
    big = [shape(array.shape, array.dtype) for array in large_args]
    outs = [
        shape(output.shape, F32),
        shape(input_grad.shape, F32),
        *like,
        attn_low,
        *big[:3],
        large_low,
        *big[3:],
        large_low,
    ]
    results = pl.pallas_call(
        adam_kernel,
        grid=(steps,),
        out_shape=outs,
        in_specs=[
            by_rows(output),
            by_rows(input_grad),
            by_rows(up_sum),
            by_rows(down_sum),
            *(fixed(array) for array in small),
            *(fixed(array) for array in small_args),
            *(by_rows(array) for array in large_args),
        ],
        out_specs=[
            by_rows(output),
            by_rows(input_grad),
            *(fixed(array) for array in (*like, attn_low)),
            *(by_rows(array) for array in (*big[:3], large_low, *big[3:], large_low)),
        ],
        compiler_params=pltpu.CompilerParams(vmem_limit_bytes=63 * 1024 * 1024),
        name="adamw",
    )(*sums, *small_args, *large_args)
    output, input_grad, *rest = results
    shared_kv, router, weights = rest[:6], rest[6:9], rest[9:]
    return (
        output,
        input_grad,
        *shared_kv,
        *(array.T for array in router),
        *(array[None] for array in weights),
    )


def solution(mesh):
    rows = P(("dp", "expert"), None)
    weights = P("expert", "dp", None)
    return jax.shard_map(
        per_device,
        mesh=mesh,
        in_specs=(
            rows,
            rows,
            P("dp", None),
            P("dp"),
            P(None, "dp", None),
            P(None, "dp", None),
            *([P()] * 9),
            *([weights] * 9),
        ),
        out_specs=(rows, rows, *([P()] * 9), *([weights] * 12)),
        check_vma=False,
    )
```
